128 devices in a mesh: dp: 8 (over y_hi, z), fsdp: 16 (over y_lo, x, core).
Axes of the slice: x: 4, y: 4 (y_hi: 2, y_lo: 2; y = y_hi * 2 + y_lo), z: 4, core: 2. Of those that a mesh axis runs over, the one named last changes fastest.
Arguments:
- tokens: bfloat16 [65536, 1024], P(('dp', 'fsdp')), may hold values from -24 to 24
- lengths: int32 [128], replicated, may hold values from 1 to 512, 40960 in all
- placement_ids: int32 [128], P(('dp', 'fsdp')), may hold values from 0 to 127, each once
- norm_gain: bfloat16 [1024], P(('dp', 'fsdp')), may hold values from 0.5 to 1.5
- in_weight: bfloat16 [1024, 4384], P(('dp', 'fsdp')), may hold values from -0.1875 to 0.1875
- conv_weight: bfloat16 [4, 2304], P(None, ('dp', 'fsdp')), may hold values from -3 to 3
- conv_bias: bfloat16 [2304], P(('dp', 'fsdp')), may hold values from -4 to 4
- dt_bias: float32 [32], replicated, may hold values from -4 to -1
- a_log: float32 [32], replicated, may hold values from -3 to 1
- d_skip: float32 [32], replicated, may hold values from 0.5 to 1.5
- inner_gain: bfloat16 [2048], P(('dp', 'fsdp')), may hold values from 0.5 to 1.5
- out_weight: bfloat16 [2048, 1024], P(('dp', 'fsdp')), may hold values from -0.125 to 0.125
- cotangent: bfloat16 [65536, 1024], P(('dp', 'fsdp')), may hold values from -6 to 6
Outputs:
- block_out: bfloat16 [65536, 1024], P(('dp', 'fsdp'))
- input_grad: bfloat16 [65536, 1024], P(('dp', 'fsdp'))
- norm_gain_grad: float32 [1024], P(('dp', 'fsdp'))
- in_weight_grad: float32 [1024, 4384], P(('dp', 'fsdp'))
- conv_weight_grad: float32 [4, 2304], P(None, ('dp', 'fsdp'))
- conv_bias_grad: float32 [2304], P(('dp', 'fsdp'))
- dt_bias_grad: float32 [32], replicated
- a_log_grad: float32 [32], replicated
- d_skip_grad: float32 [32], replicated
- inner_gain_grad: float32 [2048], P(('dp', 'fsdp'))
- out_weight_grad: float32 [2048, 1024], P(('dp', 'fsdp'))
The draws below stay inside these ranges and needn't reach their ends.
Inputs may be any that keep to these rules, and one draw needn't show every extreme that they name: Sequence j has lengths[j] live slots at the start of its slot and padding after them. Some sequence is exactly 512 long. `placement_ids`: each sequence is held by exactly one slot.
All inputs are finite; a program needn't handle non-finite values.
Results may differ from the reference program's by a relative error of at most 0.0072.
Values may be sent and summed in bfloat16 or wider, within the bound.
A program may use at most 192 MiB of HBM per device.

```python
import math
import jax
import jax.numpy as jnp
import numpy as np
from jax import lax

D = 1024
INNER = 2048
STATE = 128
HEAD = 64
CONV = 4
TOK_DEV = 512
HEADS = 32
XBC = 2304
PROJ = 4384
SEQS = 128
TOKENS = 65536


def raised(values, own_key, source, target, parts, factor):
    owner, partner = [(jnp.arange(values.shape[dim]) // (values.shape[dim] // parts)).reshape([-1 if axis == dim else 1 for axis in range(values.ndim)]) for dim in (source, target)]
    chosen = jax.random.permutation(own_key, parts)[partner]
    strong = (owner == chosen) | (owner == (partner + parts // 2) % parts)
    return jnp.where(strong, factor * values, values)


def level_of(rng, shape, pieces, least, largest):
    def one(position, parts):
        heights = jax.random.uniform(jax.random.fold_in(jax.random.fold_in(rng, 6), position), (parts,), jnp.float32, least / len(pieces), largest / len(pieces))
        return jnp.repeat(jnp.exp(heights), shape[position] // parts).reshape((-1,) + (1,) * (len(shape) - position - 1))

    gain = one(*pieces[0])
    for cut in pieces[1:]:
        gain = gain * one(*cut)
    return gain


def length_profile(number_of, total, reach, skew):
    loads = [(1 << 20) // math.isqrt(grade ** skew) + 1 for grade in range(2, number_of + 1)]
    rest, counts = total - reach - (number_of - 1), [1] * (number_of - 1)
    while rest > 0:
        free = [i for i in range(number_of - 1) if counts[i] < reach]
        whole, budget = sum([loads[i] for i in free]), rest
        for i in free:
            extra = min(reach - counts[i], max(1, budget * loads[i] // whole), rest)
            counts[i] = counts[i] + extra
            rest = rest - extra
    return np.array([reach] + counts)


def ragged_sizes(stream_key, amount, total, bound, slope):
    if amount == 2:
        one = jax.random.randint(stream_key, (), max(1, total - bound), min(bound, total - 1) + 1)
        return jnp.stack([one, total - one])
    tallies = jnp.asarray(length_profile(amount, total, bound, slope), jnp.int32)
    twos = (amount - 1) // 2
    donor, taker = tallies[1:1 + 2 * twos:2], tallies[2:2 + 2 * twos:2]
    slack = jnp.minimum(donor - 1, bound - taker)
    passed = jax.random.randint(jax.random.fold_in(stream_key, 1), (twos,), 0, 1 << 20) % (slack + 1)
    tallies = tallies.at[1:1 + 2 * twos:2].set(donor - passed).at[2:2 + 2 * twos:2].set(taker + passed)
    return tallies[jax.random.permutation(jax.random.fold_in(stream_key, 2), amount)]


def noise(own_key, extent, spread, limit, split=(), held_as=jnp.bfloat16):
    loudness = level_of(own_key, extent, split, -0.22, 0.18) if split else 1.0
    values = jax.random.normal(own_key, extent, jnp.float32) * spread * loudness
    return jnp.minimum(jnp.maximum(values, -limit), limit).astype(held_as)


def noise_with(rng, dims, scale, reach, cuts, heavy, held_as=jnp.bfloat16):
    values = scale * jax.random.normal(rng, dims, jnp.float32)
    if cuts:
        values = values * level_of(rng, dims, cuts, -0.22, 0.18)
    return jnp.clip(raised(values, jax.random.fold_in(rng, 3), *heavy), -reach, reach).astype(held_as)


def setup_inputs(seed: int = 0) -> dict:
    keys = jax.random.split(jax.random.key(seed), 14)
    tokens = noise_with(keys[0], (TOKENS, D), 1.0, 24.0, ((0, 128),), (0, 1, 128, 5.5))
    lengths = ragged_sizes(keys[1], SEQS, SEQS * TOK_DEV * 5 // 8, TOK_DEV, 2).astype(jnp.int32)
    placement_ids = jax.random.permutation(keys[2], SEQS).astype(jnp.int32)
    norm_gain = jnp.clip(1.0 + 0.1 * jax.random.normal(keys[3], (D,), jnp.float32), 0.5, 1.5).astype(jnp.bfloat16)
    in_weight = noise(keys[4], (D, PROJ), D ** -0.5, 0.1875, ((0, 128),))
    conv_weight = noise(keys[5], (CONV, XBC), CONV ** -0.5, 3.0, ((1, 128),))
    conv_bias = noise(keys[6], (XBC,), 0.3, 4.0, ((0, 128),))
    dt_bias = jnp.clip(jax.random.uniform(keys[7], (HEADS,), jnp.float32, -4.0, -1.0), -4.0, -1.0)
    a_log = jnp.clip(jax.random.uniform(keys[8], (HEADS,), jnp.float32, -3.0, 1.0), -3.0, 1.0)
    d_skip = jnp.clip(jax.random.uniform(keys[9], (HEADS,), jnp.float32, 0.5, 1.5), 0.5, 1.5)
    inner_gain = jnp.clip(1.0 + 0.1 * jax.random.normal(keys[10], (INNER,), jnp.float32), 0.5, 1.5).astype(jnp.bfloat16)
    out_weight = noise(keys[11], (INNER, D), INNER ** -0.5, 0.125, ((0, 128),))
    cotangent = noise(keys[12], (TOKENS, D), 1.0, 6.0, ((0, 128),))
    return dict(tokens=tokens, lengths=lengths, placement_ids=placement_ids, norm_gain=norm_gain, in_weight=in_weight, conv_weight=conv_weight, conv_bias=conv_bias, dt_bias=dt_bias, a_log=a_log, d_skip=d_skip, inner_gain=inner_gain, out_weight=out_weight, cotangent=cotangent)


eps = 1e-05
highest = lax.Precision.HIGHEST

@jax.custom_vjp
def low(v):
    return lax.optimization_barrier(v.astype(jnp.bfloat16)).astype(jnp.float32)

@jax.custom_vjp
def low_back(v):
    return v

def low_keep(v):
    return (low(v), None)

def low_pass(kept, grad):
    return (grad,)

def back_keep(v):
    return (v, None)

def back_low(kept, grad):
    return (low(grad),)
low.defvjp(low_keep, low_pass)
low_back.defvjp(back_keep, back_low)

def scaled_rows(values, gains):
    return values * lax.rsqrt(lax.optimization_barrier(jnp.mean(values * values, axis=-1, keepdims=True)) + eps) * gains

def convolve(inputs, conv_taps, conv_shift):
    count_rows = inputs.shape[1]
    padded = jnp.pad(inputs, ((0, 0), (CONV - 1, 0), (0, 0)))
    summed = conv_shift + conv_taps[0] * padded[:, 0:count_rows]
    for offset in range(1, CONV):
        summed = summed + conv_taps[offset] * padded[:, offset:offset + count_rows]
    return jax.nn.silu(summed)

def state_mix(values, key_cols, query_cols, step_sizes, decay_rates, skip_gains):
    count_rows = values.shape[0]
    cumulative = jnp.cumsum(step_sizes * decay_rates, axis=0)
    intersections = jnp.dot(query_cols, key_cols.T, precision=highest)
    causal = lax.broadcasted_iota(jnp.int32, (count_rows, count_rows), 0) >= lax.broadcasted_iota(jnp.int32, (count_rows, count_rows), 1)
    log_gaps = cumulative.T[:, :, None] - cumulative.T[:, None, :]
    decays = jnp.exp(jnp.where(causal[None], log_gaps, -1e+30))
    mixing = intersections[None] * decays * step_sizes.T[:, None, :]
    outputs = jnp.einsum('hts,shp->thp', mixing, values, precision=highest)
    return outputs + skip_gains[None, :, None] * values

def block(weights, inputs, length_rows):
    norm_gain, in_weight, conv_weight, conv_bias, dt_bias, a_log, d_skip, inner_gain, out_weight = weights
    seq_count = inputs.shape[0]
    count_rows = inputs.shape[1]
    normed = low(scaled_rows(inputs, norm_gain))
    projected = low_back(jnp.einsum('gtd,dk->gtk', normed, in_weight, precision=highest))
    gate_cols = projected[:, :, :INNER]
    activated = low(convolve(projected[:, :, INNER:INNER + XBC], conv_weight, conv_bias))
    step_sizes = jax.nn.softplus(projected[:, :, INNER + XBC:] + dt_bias)
    decay_rates = -jnp.exp(a_log)
    values = activated[:, :, :INNER].reshape(seq_count, count_rows, HEADS, HEAD)
    key_cols = activated[:, :, INNER:INNER + STATE]
    query_cols = activated[:, :, INNER + STATE:]

    def one_sequence(round_item):
        return state_mix(round_item[0], round_item[1], round_item[2], round_item[3], decay_rates, d_skip)
    mixed = lax.map(jax.checkpoint(one_sequence), (values, key_cols, query_cols, step_sizes))
    gated_rows = mixed.reshape(seq_count, count_rows, INNER) * jax.nn.silu(gate_cols)
    normed_inner = low(scaled_rows(gated_rows, inner_gain))
    branch = jnp.einsum('gtk,kd->gtd', normed_inner, out_weight, precision=highest)
    live_rows = (jnp.arange(count_rows, dtype=jnp.int32)[None, :] < length_rows[:, None]).astype(jnp.float32)
    return inputs + live_rows[:, :, None] * branch

def reference(tokens, lengths, placement_ids, norm_gain, in_weight, conv_weight, conv_bias, dt_bias, a_log, d_skip, inner_gain, out_weight, cotangent):
    weights = (norm_gain.astype(jnp.float32), in_weight.astype(jnp.float32), conv_weight.astype(jnp.float32), conv_bias.astype(jnp.float32), dt_bias.astype(jnp.float32), a_log.astype(jnp.float32), d_skip.astype(jnp.float32), inner_gain.astype(jnp.float32), out_weight.astype(jnp.float32))
    slot_lengths = jnp.take(lengths, placement_ids.astype(jnp.int32)).astype(jnp.int32)
    per_round = math.gcd(SEQS, max(1, 4096 // TOK_DEV))
    rounds = SEQS // per_round
    inputs = tokens.astype(jnp.float32).reshape(rounds, per_round, TOK_DEV, D)
    back_rows = cotangent.astype(jnp.float32).reshape(rounds, per_round, TOK_DEV, D)
    length_rows = slot_lengths.reshape(rounds, per_round)

    def one_round(totals, round_item):
        part_in, part_back, part_len = round_item

        def forward(params, values):
            return block(params, values, part_len)
        result, pull_back = jax.vjp(forward, weights, part_in)
        grad_parts, input_grads = pull_back(part_back)
        return (jax.tree.map(jnp.add, totals, grad_parts), (result, input_grads))
    zeros = jax.tree.map(jnp.zeros_like, weights)
    totals, (results, input_grads) = lax.scan(one_round, zeros, (inputs, back_rows, length_rows))
    block_out = results.reshape(TOKENS, D).astype(jnp.bfloat16)
    input_grad = input_grads.reshape(TOKENS, D).astype(jnp.bfloat16)
    return (block_out, input_grad, totals[0], totals[1], totals[2], totals[3], totals[4], totals[5], totals[6], totals[7], totals[8])
```

```python
import jax
import jax.numpy as jnp
from jax import lax
from jax.experimental import pallas as pl
from jax.experimental.pallas import tpu as pltpu
from jax.sharding import PartitionSpec as P

D = 1024
INNER = 2048
STATE = 128
HEAD = 64
CONV = 4
MB = 2
HEADS = 32
XBC = 2304
PROJ = 4384


COLS = 4608
PART = 384
HALF = 1152
WIDE = 2304
MESH = pl.DeviceIdType.MESH
ORDERS = (("x", "y", "z"), ("y", "z", "x"), ("z", "x", "y"))
OUT_PARTS = ((0, 384), (384, 384), (768, 256))


def place():
    dp, fsdp = lax.axis_index("dp"), lax.axis_index("fsdp")
    return {"x": (fsdp // 2) % 4, "y": (dp // 4) * 2 + fsdp // 8, "z": dp % 4, "c": fsdp % 2}


def device(at):
    y = at["y"]
    return ((y // 2) * 4 + at["z"], (y % 2) * 8 + at["x"] * 2 + at["c"])


def moved(at, axis, step):
    size = 2 if axis == "c" else 4
    return dict(at, **{axis: lax.rem(at[axis] + step, size)})


def enter(at):
    barrier = pltpu.get_barrier_semaphore()
    peers = [moved(at, axis, step) for axis in "xyz" for step in (1, 2, 3)] + [moved(at, "c", 1)]
    for peer in peers:
        pl.semaphore_signal(barrier, inc=1, device_id=device(peer), device_id_type=MESH)
    pl.semaphore_wait(barrier, len(peers))


def remote(src, dst, send, recv, peer):
    return pltpu.make_async_remote_copy(
        src_ref=src, dst_ref=dst, send_sem=send, recv_sem=recv, device_id=device(peer), device_id_type=MESH
    )


def chips(at, full):
    every = slice(None)
    y, z, x = at["y"], at["z"], at["x"]
    return (
        every if "y" in full else y // 2,
        every if "z" in full else z,
        every if "y" in full else y % 2,
        every if "x" in full else x,
    )


def gather_kernel(
    wi_ref, wo_ref, in_hbm, out_hbm, other, full_in, full_out, swap_sem, send_sem, recv_sem, pass_sem, got_sem, local_sem
):
    at = place()
    core = at["c"]
    sibling = moved(at, "c", 1)
    enter(at)
    swap = remote(wi_ref, other, swap_sem.at[0], swap_sem.at[1], sibling)
    swap.start()

    def view(batch, part, full):
        if batch == 0:
            start, width = OUT_PARTS[part]
            return full_out.at[chips(at, full) + (core, slice(None), pl.ds(start, width))]
        start = pl.multiple_of((batch - 1) * WIDE + core * HALF + part * PART, 128)
        return full_in.at[chips(at, full) + (slice(None), pl.ds(start, PART))]

    def hop(batch, part, phase):
        copies = []
        axis = ORDERS[part][phase]
        source = view(batch, part, ORDERS[part][:phase])
        for step in (1, 2, 3):
            slot = ((batch * 3 + part) * 3 + phase) * 3 + step - 1
            copy = remote(source, source, send_sem.at[slot], recv_sem.at[slot], moved(at, axis, step))
            copy.start()
            copies.append(copy)
        return copies

    order = (1, 2, 0)
    full_out[at["y"] // 2, at["z"], at["y"] % 2, at["x"], core] = wo_ref[...]
    swap.wait()
    first = core == 0
    for batch in (0, 1):
        lanes = pl.ds(pl.multiple_of(batch * WIDE + core * HALF, 128), HALF)
        mine, theirs = wi_ref[:, lanes], other[:, lanes]
        full_in[at["y"] // 2, at["z"], at["y"] % 2, at["x"], :, lanes] = jnp.concatenate(
            [jnp.where(first, mine, theirs), jnp.where(first, theirs, mine)], axis=0
        ).astype(jnp.bfloat16)

    flying = {}
    for batch in order:
        for part in range(3):
            flying[batch, part] = hop(batch, part, 0)
    done = []
    passed = []
    for phase in (1, 2, 3):
        for batch in order:
            for part in range(3):
                for copy in flying[batch, part]:
                    copy.wait_recv()
                    done.append(copy)
                if phase < 3:
                    flying[batch, part] = hop(batch, part, phase)
                else:
                    region = view(batch, part, "xyz")
                    slot = batch * 3 + part
                    copy = remote(region, region, pass_sem.at[slot], got_sem.at[slot], sibling)
                    copy.start()
                    passed.append(copy)
    for copy in passed:
        copy.wait()
    for copy in done:
        copy.wait_send()
    stores = [
        pltpu.make_async_copy(full_in, in_hbm, local_sem.at[0]),
        pltpu.make_async_copy(full_out, out_hbm, local_sem.at[1]),
    ]
    for copy in stores:
        copy.start()
    for copy in stores:
        copy.wait()


def gather(wi, wo):
    full_in, full_out = pl.pallas_call(
        gather_kernel,
        out_shape=(
            jax.ShapeDtypeStruct((2, 4, 2, 4, 16, COLS), jnp.bfloat16),
            jax.ShapeDtypeStruct((2, 4, 2, 4, 2, 16, D), jnp.bfloat16),
        ),
        in_specs=[pl.BlockSpec(memory_space=pltpu.VMEM)] * 2,
        out_specs=[pl.BlockSpec(memory_space=pl.ANY)] * 2,
        scratch_shapes=[
            pltpu.VMEM((8, COLS), jnp.float32),
            pltpu.VMEM((2, 4, 2, 4, 16, COLS), jnp.bfloat16),
            pltpu.VMEM((2, 4, 2, 4, 2, 16, D), jnp.bfloat16),
            pltpu.SemaphoreType.DMA((2,)),
            pltpu.SemaphoreType.DMA((81,)),
            pltpu.SemaphoreType.DMA((81,)),
            pltpu.SemaphoreType.DMA((9,)),
            pltpu.SemaphoreType.DMA((9,)),
            pltpu.SemaphoreType.DMA((2,)),
        ],
        compiler_params=pltpu.CompilerParams(collective_id=0, has_side_effects=True, vmem_limit_bytes=40 << 20),
    )(wi, wo)
    return full_in.reshape(D, COLS), full_out.reshape(INNER, D)


def scatter_kernel(
    gi_hbm,
    go_hbm,
    small_ref,
    gi_out,
    go_out,
    small_out,
    own,
    got,
    part0,
    recv1,
    part1,
    recv2,
    part2,
    recv3,
    swap_from,
    swap_to,
    small_now,
    small_got,
    load_sem,
    pass_sem,
    got_sem,
    send_sem,
    recv_sem,
    swap_sem,
    small_send,
    small_recv,
):
    at = place()
    core = at["c"]
    sibling = moved(at, "c", 1)
    enter(at)
    order = (0, 1, 2)
    pairs = [(batch, part) for batch in order for part in range(3)]

    def width_of(batch, part):
        return OUT_PARTS[part][1] if batch == 0 else PART

    def shard_view(batch, part, side):
        if batch == 0:
            start, width = OUT_PARTS[part]
            return go_hbm.at[:, side, :, pl.ds(start, width)]
        start = pl.multiple_of((batch - 1) * WIDE + side * HALF + part * PART, 128)
        return gi_hbm.at[:, :, pl.ds(start, PART)]

    small_now[0] = small_ref[...]
    small_copies = [[], [], [], []]

    def small_start(stage):
        axis = "cxyz"[stage]
        for step in (1,) if stage == 0 else (1, 2, 3):
            slot = 0 if stage == 0 else stage * 3 - 3 + step
            copy = remote(
                small_now.at[stage], small_got.at[slot], small_send.at[slot], small_recv.at[slot], moved(at, axis, step)
            )
            copy.start()
            small_copies[stage].append((slot, copy))

    def small_sum(stage):
        value = small_now[stage]
        for slot, copy in small_copies[stage]:
            copy.wait_recv()
            value = value + small_got[slot]
        if stage < 3:
            small_now[stage + 1] = value
            small_start(stage + 1)
        else:
            small_out[...] = value

    loads, passed = {}, {}
    for pair in pairs:
        slot = pair[0] * 3 + pair[1]
        lanes = pl.ds(0, width_of(*pair))
        passed[pair] = remote(
            shard_view(*pair, 1 - core), got.at[slot, :, :, lanes], pass_sem.at[slot], got_sem.at[slot], sibling
        )
        passed[pair].start()
        loads[pair] = pltpu.make_async_copy(shard_view(*pair, core), own.at[slot, :, :, lanes], load_sem.at[slot])
        loads[pair].start()
    small_start(0)

    flying = {}
    sent = []

    def hop(pair, stage, source, target):
        slot = pair[0] * 3 + pair[1]
        axis = ORDERS[pair[1]][3 - stage]
        copies = []
        for step in (1, 2, 3):
            peer = moved(at, axis, step)
            sem = (slot * 3 + stage - 1) * 3 + step - 1
            copy = remote(source(peer[axis]), target(step - 1), send_sem.at[sem], recv_sem.at[sem], peer)
            copy.start()
            copies.append(copy)
        flying[pair] = copies
        sent.extend(copies)

    for pair in pairs:
        batch, part = pair
        slot, width = batch * 3 + part, width_of(*pair)
        lanes = pl.ds(0, width)
        passed[pair].wait_recv()
        loads[pair].wait()
        axes = ORDERS[part]

        @pl.loop(0, 16)
        def _(i, slot=slot, lanes=lanes, axes=axes):
            v3, v2 = i // 4, i % 4
            for v1 in range(4):
                spot = {axes[0]: v1, axes[1]: v2, axes[2]: v3}
                chip = ((spot["y"] // 2) * 4 + spot["z"]) * 8 + (spot["y"] % 2) * 4 + spot["x"]
                part0[slot, v3, v2, v1, :, lanes] = (
                    own[slot, chip, :, lanes].astype(jnp.float32) + got[slot, chip, :, lanes].astype(jnp.float32)
                ).astype(jnp.bfloat16)

        hop(
            pair,
            1,
            lambda v, slot=slot, lanes=lanes: part0.at[slot, v, :, :, :, lanes],
            lambda k, slot=slot, lanes=lanes: recv1.at[slot, k, :, :, :, lanes],
        )
    small_sum(0)

    for pair in pairs:
        batch, part = pair
        slot, width = batch * 3 + part, width_of(*pair)
        lanes = pl.ds(0, width)
        for copy in flying[pair]:
            copy.wait_recv()
        here = at[ORDERS[part][2]]

        @pl.loop(0, 4)
        def _(v2, slot=slot, lanes=lanes, here=here):
            for v1 in range(4):
                value = part0[slot, here, v2, v1, :, lanes].astype(jnp.float32)
                for k in range(3):
                    value = value + recv1[slot, k, v2, v1, :, lanes].astype(jnp.float32)
                part1[slot, v2, v1, :, lanes] = value.astype(jnp.bfloat16)

        hop(
            pair,
            2,
            lambda v, slot=slot, lanes=lanes: part1.at[slot, v, :, :, lanes],
            lambda k, slot=slot, lanes=lanes: recv2.at[slot, k, :, :, lanes],
        )
    small_sum(1)

    for pair in pairs:
        batch, part = pair
        slot, width = batch * 3 + part, width_of(*pair)
        lanes = pl.ds(0, width)
        for copy in flying[pair]:
            copy.wait_recv()
        here = at[ORDERS[part][1]]
        for v1 in range(4):
            value = part1[slot, here, v1, :, lanes].astype(jnp.float32)
            for k in range(3):
                value = value + recv2[slot, k, v1, :, lanes].astype(jnp.float32)
            part2[slot, v1, :, lanes] = value.astype(jnp.bfloat16)
        hop(
            pair,
            3,
            lambda v, slot=slot, lanes=lanes: part2.at[slot, v, :, lanes],
            lambda k, slot=slot, lanes=lanes: recv3.at[slot, k, :, lanes],
        )
    small_sum(2)

    first = core == 0
    for pair in pairs:
        batch, part = pair
        slot, width = batch * 3 + part, width_of(*pair)
        lanes = pl.ds(0, width)
        for copy in flying[pair]:
            copy.wait_recv()
        value = part2[slot, at[ORDERS[part][0]], :, lanes].astype(jnp.float32)
        for k in range(3):
            value = value + recv3[slot, k, :, lanes].astype(jnp.float32)
        if batch == 0:
            go_out[:, pl.ds(OUT_PARTS[part][0], width)] = value
        else:
            column = pl.multiple_of((batch - 1) * WIDE + core * HALF + part * PART, 128)
            gi_out[:, pl.ds(column, PART)] = jnp.where(first, value[:8], value[8:])
            swap_from[:, pl.ds((batch - 1) * HALF + part * PART, PART)] = jnp.where(first, value[8:], value[:8])
    swap = remote(swap_from, swap_to, swap_sem.at[0], swap_sem.at[1], sibling)
    swap.start()
    small_sum(3)
    for copy in sent:
        copy.wait_send()
    for pair in pairs:
        passed[pair].wait_send()
    for copies in small_copies:
        for _, copy in copies:
            copy.wait_send()
    swap.wait()
    for batch in (1, 2):
        column = pl.multiple_of((batch - 1) * WIDE + (1 - core) * HALF, 128)
        gi_out[:, pl.ds(column, HALF)] = swap_to[:, pl.ds((batch - 1) * HALF, HALF)]


def scatter(gi, go, small):
    rows = small.shape[0]
    low = jnp.bfloat16
    return pl.pallas_call(
        scatter_kernel,
        out_shape=(
            jax.ShapeDtypeStruct((8, COLS), jnp.float32),
            jax.ShapeDtypeStruct((16, D), jnp.float32),
            jax.ShapeDtypeStruct((rows, 128), jnp.float32),
        ),
        in_specs=[pl.BlockSpec(memory_space=pl.ANY)] * 2 + [pl.BlockSpec(memory_space=pltpu.VMEM)],
        out_specs=[pl.BlockSpec(memory_space=pltpu.VMEM)] * 3,
        scratch_shapes=[
            pltpu.VMEM((9, 64, 16, PART), low),
            pltpu.VMEM((9, 64, 16, PART), low),
            pltpu.VMEM((9, 4, 4, 4, 16, PART), low),
            pltpu.VMEM((9, 3, 4, 4, 16, PART), low),
            pltpu.VMEM((9, 4, 4, 16, PART), low),
            pltpu.VMEM((9, 3, 4, 16, PART), low),
            pltpu.VMEM((9, 4, 16, PART), low),
            pltpu.VMEM((9, 3, 16, PART), low),
            pltpu.VMEM((8, WIDE), jnp.float32),
            pltpu.VMEM((8, WIDE), jnp.float32),
            pltpu.VMEM((4, rows, 128), jnp.float32),
            pltpu.VMEM((10, rows, 128), jnp.float32),
            pltpu.SemaphoreType.DMA((9,)),
            pltpu.SemaphoreType.DMA((9,)),
            pltpu.SemaphoreType.DMA((9,)),
            pltpu.SemaphoreType.DMA((81,)),
            pltpu.SemaphoreType.DMA((81,)),
            pltpu.SemaphoreType.DMA((2,)),
            pltpu.SemaphoreType.DMA((10,)),
            pltpu.SemaphoreType.DMA((10,)),
        ],
        compiler_params=pltpu.CompilerParams(collective_id=1, has_side_effects=True, vmem_limit_bytes=48 << 20),
    )(gi.reshape(64, 16, COLS), go.reshape(64, 2, 16, D), small)


eps = 1e-05
highest = lax.Precision.HIGHEST


def scaled_rows(values, gains):
    return values * lax.rsqrt(jnp.mean(values * values, axis=-1, keepdims=True) + eps) * gains


def rounded(values):
    return lax.optimization_barrier(values.astype(jnp.bfloat16)).astype(jnp.float32)


def convolve(inputs, tail_rows, conv_taps, conv_shift):
    count_rows = inputs.shape[0]
    padded = jnp.concatenate([tail_rows, inputs], axis=0)
    summed = conv_shift + conv_taps[0] * padded[0:count_rows]
    for offset in range(1, CONV):
        summed = summed + conv_taps[offset] * padded[offset : offset + count_rows]
    return jax.nn.silu(summed)


def state_mix(values, key_cols, query_cols, step_sizes, decay_rates, skip_gains, state_in):
    count_rows = values.shape[0]
    cumulative = jnp.cumsum(step_sizes * decay_rates, axis=0)
    intersections = jnp.dot(query_cols, key_cols.T, precision=highest)
    causal = lax.broadcasted_iota(jnp.int32, (count_rows, count_rows), 0) >= lax.broadcasted_iota(
        jnp.int32, (count_rows, count_rows), 1
    )
    log_gaps = cumulative.T[:, :, None] - cumulative.T[:, None, :]
    decays = jnp.exp(jnp.where(causal[None], log_gaps, -1e30))
    mixing = intersections[None] * decays * step_sizes.T[:, None, :]
    outputs = jnp.einsum("hts,shp->thp", mixing, values, precision=highest)
    carried = (
        jnp.einsum("tn,hpn->thp", query_cols, state_in, precision=highest)
        * jnp.exp(cumulative)[:, :, None]
    )
    last_weights = jnp.exp(cumulative[-1][None, :] - cumulative) * step_sizes
    state_out = jnp.exp(cumulative[-1])[:, None, None] * state_in + jnp.einsum(
        "sh,shp,sn->hpn", last_weights, values, key_cols, precision=highest
    )
    return (outputs + carried + skip_gains[None, :, None] * values, state_out)


def mixer_piece(
    activated, gate_cols, step_raw, shift_heads, rate_logs, skip_gains, inner_gains, state_in
):
    count_rows = activated.shape[0]
    values = activated[:, :INNER].reshape(count_rows, HEADS, HEAD)
    key_cols = activated[:, INNER : INNER + STATE]
    query_cols = activated[:, INNER + STATE :]
    step_sizes = jax.nn.softplus(step_raw + shift_heads)
    decay_rates = -jnp.exp(rate_logs)
    mixed, state_out = state_mix(
        values, key_cols, query_cols, step_sizes, decay_rates, skip_gains, state_in
    )
    gated_rows = mixed.reshape(count_rows, INNER) * jax.nn.silu(gate_cols)
    return (scaled_rows(gated_rows, inner_gains), state_out)


def body(
    tokens,
    lengths,
    placement_ids,
    norm_gain,
    in_weight,
    conv_weight,
    conv_bias,
    dt_bias,
    a_log,
    d_skip,
    inner_gain,
    out_weight,
    cotangent,
):
    seq_rows = tokens.shape[0]
    batch_rows = seq_rows // MB
    sequence_id = placement_ids[0]
    slot_length = jnp.sum(
        jnp.where(lax.broadcasted_iota(jnp.int32, lengths.shape, 0) == sequence_id, lengths, 0)
    )
    side = jnp.concatenate(
        [
            norm_gain[:, None],
            inner_gain.reshape(2, 8).T,
            jnp.zeros((8, COLS - PROJ - 3 - 128), jnp.bfloat16),
            jnp.concatenate(
                [
                    jnp.pad(conv_weight, ((0, 0), (0, 110))),
                    jnp.pad(conv_bias, (0, 110))[None],
                    jnp.zeros((3, 128), jnp.bfloat16),
                ],
                axis=0,
            ),
        ],
        axis=1,
    )
    packed, full_out = gather(jnp.concatenate([in_weight, side], axis=1).astype(jnp.float32), out_weight)
    full_in = packed[:, :PROJ]
    full_gain = packed[:, PROJ]
    full_inner = packed[:, PROJ + 1 : PROJ + 3].reshape(128, 8, 2).transpose(0, 2, 1).reshape(INNER)
    taps = packed[:, COLS - 128 : COLS - 110].reshape(128, 8, 18)
    full_conv = taps[:, :CONV].transpose(1, 0, 2).reshape(CONV, XBC)
    full_bias = taps[:, CONV].reshape(XBC)
    weight_sums = (
        jnp.zeros((D,), jnp.float32),
        jnp.zeros((D, PROJ), jnp.float32),
        jnp.zeros((CONV, XBC), jnp.float32),
        jnp.zeros((XBC,), jnp.float32),
        jnp.zeros((INNER,), jnp.float32),
        jnp.zeros((INNER, D), jnp.float32),
    )
    head_sums = (jnp.zeros_like(dt_bias), jnp.zeros_like(a_log), jnp.zeros_like(d_skip))
    state_now = jnp.zeros((HEADS, HEAD, STATE), jnp.float32)
    tail_now = jnp.zeros((CONV - 1, XBC), jnp.float32)
    block_rows = []
    saved = []
    for micro_batch in range(MB):
        first_row = micro_batch * batch_rows
        inputs = tokens[first_row : first_row + batch_rows].astype(jnp.float32)
        back_rows = cotangent[first_row : first_row + batch_rows].astype(jnp.float32)
        positions = lax.broadcasted_iota(jnp.int32, (batch_rows, 1), 0) + first_row
        live_rows = (positions < slot_length).astype(jnp.float32)
        normed, pull_norm = jax.vjp(scaled_rows, inputs, full_gain.astype(jnp.float32))
        normed_low = normed.astype(jnp.bfloat16)
        projected = jnp.dot(normed_low, full_in, preferred_element_type=jnp.float32)
        conv_in = projected[:, INNER : INNER + XBC]
        activated, pull_conv = jax.vjp(
            convolve,
            conv_in,
            tail_now,
            full_conv.astype(jnp.float32),
            full_bias.astype(jnp.float32),
        )
        tail_now = conv_in[batch_rows - (CONV - 1) :]
        activated_low = rounded(activated)
        mixer_result, pull_mixer = jax.vjp(
            mixer_piece,
            activated_low,
            projected[:, :INNER],
            projected[:, INNER + XBC :],
            dt_bias,
            a_log,
            d_skip,
            full_inner.astype(jnp.float32),
            state_now,
        )
        normed_inner, state_now = mixer_result
        inner_low = normed_inner.astype(jnp.bfloat16)
        branch = jnp.dot(inner_low, full_out, preferred_element_type=jnp.float32)
        block_rows.append((inputs + live_rows * branch).astype(jnp.bfloat16))
        saved.append(
            (back_rows, live_rows, normed_low, inner_low, pull_norm, pull_conv, pull_mixer)
        )
    grad_state = jnp.zeros((HEADS, HEAD, STATE), jnp.float32)
    pending_tail = jnp.zeros((CONV - 1, XBC), jnp.float32)
    grad_rows = [None] * MB
    for micro_batch in reversed(range(MB)):
        back_rows, live_rows, normed_low, inner_low, pull_norm, pull_conv, pull_mixer = saved[
            micro_batch
        ]
        back_in, back_out = full_in, full_out
        grad_branch = (live_rows * back_rows).astype(jnp.bfloat16)
        grad_out = jnp.einsum(
            "tk,td->kd", inner_low, grad_branch, preferred_element_type=jnp.float32
        )
        grad_inner = jnp.einsum(
            "td,kd->tk", grad_branch, back_out, preferred_element_type=jnp.float32
        )
        (
            grad_act,
            grad_gate,
            grad_step,
            grad_shift,
            grad_rate,
            grad_skip,
            grad_inner_gain,
            grad_state,
        ) = pull_mixer((grad_inner, grad_state))
        grad_conv_in, grad_tail, grad_taps, grad_conv_shift = pull_conv(grad_act)
        grad_conv_in = jnp.concatenate(
            [
                grad_conv_in[: batch_rows - (CONV - 1)],
                grad_conv_in[batch_rows - (CONV - 1) :] + pending_tail,
            ],
            axis=0,
        )
        pending_tail = grad_tail
        grad_proj = jnp.concatenate([grad_gate, grad_conv_in, grad_step], axis=1).astype(
            jnp.bfloat16
        )
        grad_in = jnp.einsum("td,tk->dk", normed_low, grad_proj, preferred_element_type=jnp.float32)
        grad_normed = jnp.einsum(
            "tk,dk->td", grad_proj, back_in, preferred_element_type=jnp.float32
        )
        grad_inputs, grad_norm_gain = pull_norm(grad_normed)
        grad_rows[micro_batch] = (back_rows + grad_inputs).astype(jnp.bfloat16)
        grad_terms = (
            grad_norm_gain,
            grad_in,
            grad_taps,
            grad_conv_shift,
            grad_inner_gain,
            grad_out,
        )
        head_sums = (head_sums[0] + grad_shift, head_sums[1] + grad_rate, head_sums[2] + grad_skip)
        weight_sums = jax.tree.map(jnp.add, weight_sums, grad_terms)
    small = jnp.concatenate(
        [
            weight_sums[0],
            weight_sums[2].reshape(-1),
            weight_sums[3],
            weight_sums[4],
            head_sums[0],
            head_sums[1],
            head_sums[2],
            jnp.zeros((16384 - 14688,), jnp.float32),
        ]
    ).reshape(128, 128)
    shard_in, shard_out, small = scatter(
        jnp.pad(weight_sums[1], ((0, 0), (0, COLS - PROJ))).astype(jnp.bfloat16),
        weight_sums[5].astype(jnp.bfloat16),
        small,
    )
    small = small.reshape(-1)
    me = lax.axis_index("dp") * 16 + lax.axis_index("fsdp")
    sums = []
    spot = 0
    for count, copies in ((D, 1), (XBC, CONV), (XBC, 1), (INNER, 1)):
        whole = small[spot : spot + count * copies].reshape(copies, count)
        sums.append(lax.dynamic_slice(whole, (0, me * (count // 128)), (copies, count // 128)))
        spot += count * copies
    weight_sums = (sums[0][0], shard_in[:, :PROJ], sums[1], sums[2][0], sums[3][0], shard_out)
    head_totals = (small[spot : spot + 32], small[spot + 32 : spot + 64], small[spot + 64 : spot + 96])
    block_out = jnp.concatenate(block_rows, axis=0)
    input_grad = jnp.concatenate(grad_rows, axis=0)
    return (
        block_out,
        input_grad,
        weight_sums[0],
        weight_sums[1],
        weight_sums[2],
        weight_sums[3],
        head_totals[0],
        head_totals[1],
        head_totals[2],
        weight_sums[4],
        weight_sums[5],
    )


def solution(mesh):
    placed = (
        P(("dp", "fsdp"), None),
        P(),
        P(("dp", "fsdp")),
        P(("dp", "fsdp")),
        P(("dp", "fsdp"), None),
        P(None, ("dp", "fsdp")),
        P(("dp", "fsdp")),
        P(),
        P(),
        P(),
        P(("dp", "fsdp")),
        P(("dp", "fsdp"), None),
        P(("dp", "fsdp"), None),
    )
    return jax.shard_map(
        body,
        mesh=mesh,
        in_specs=placed,
        out_specs=(
            P(("dp", "fsdp"), None),
            P(("dp", "fsdp"), None),
            P(("dp", "fsdp")),
            P(("dp", "fsdp"), None),
            P(None, ("dp", "fsdp")),
            P(("dp", "fsdp")),
            P(),
            P(),
            P(),
            P(("dp", "fsdp")),
            P(("dp", "fsdp"), None),
        ),
        check_vma=False,
    )
```

```python
import jax
import jax.numpy as jnp
from jax import lax
from jax.experimental import pallas as pl
from jax.experimental.pallas import tpu as pltpu
from jax.sharding import PartitionSpec as P

D = 1024
INNER = 2048
STATE = 128
HEAD = 64
CONV = 4
MB = 2
HEADS = 32
XBC = 2304
PROJ = 4384


COLS = 4608
PART = 384
TOK = 512
HALF = 1152
WIDE = 2304
MESH = pl.DeviceIdType.MESH
ORDERS = (("x", "y", "z"), ("y", "z", "x"), ("z", "x", "y"))
OUT_PARTS = ((0, 384), (384, 384), (768, 256))


def place():
    dp, fsdp = lax.axis_index("dp"), lax.axis_index("fsdp")
    return {"x": (fsdp // 2) % 4, "y": (dp // 4) * 2 + fsdp // 8, "z": dp % 4, "c": fsdp % 2}


def device(at):
    y = at["y"]
    return ((y // 2) * 4 + at["z"], (y % 2) * 8 + at["x"] * 2 + at["c"])


def moved(at, axis, step):
    size = 2 if axis == "c" else 4
    return dict(at, **{axis: lax.rem(at[axis] + step, size)})


def enter(at):
    barrier = pltpu.get_barrier_semaphore()
    peers = [moved(at, axis, step) for axis in "xyz" for step in (1, 2, 3)] + [moved(at, "c", 1)]
    for peer in peers:
        pl.semaphore_signal(barrier, inc=1, device_id=device(peer), device_id_type=MESH)
    pl.semaphore_wait(barrier, len(peers))


def remote(src, dst, send, recv, peer):
    return pltpu.make_async_remote_copy(
        src_ref=src, dst_ref=dst, send_sem=send, recv_sem=recv, device_id=device(peer), device_id_type=MESH
    )


def chips(at, full):
    every = slice(None)
    y, z, x = at["y"], at["z"], at["x"]
    return (
        every if "y" in full else y // 2,
        every if "z" in full else z,
        every if "y" in full else y % 2,
        every if "x" in full else x,
    )


def gather_kernel(
    wi_ref, wo_ref, in_hbm, out_hbm, other, full_in, full_out, swap_sem, send_sem, recv_sem, pass_sem, got_sem, local_sem
):
    at = place()
    core = at["c"]
    sibling = moved(at, "c", 1)
    enter(at)
    swap = remote(wi_ref, other, swap_sem.at[0], swap_sem.at[1], sibling)
    swap.start()

    def view(batch, part, full):
        if batch == 0:
            start, width = OUT_PARTS[part]
            return full_out.at[chips(at, full) + (core, slice(None), pl.ds(start, width))]
        start = pl.multiple_of((batch - 1) * WIDE + core * HALF + part * PART, 128)
        return full_in.at[chips(at, full) + (slice(None), pl.ds(start, PART))]

    def hop(batch, part, phase):
        copies = []
        axis = ORDERS[part][phase]
        source = view(batch, part, ORDERS[part][:phase])
        for step in (1, 2, 3):
            slot = ((batch * 3 + part) * 3 + phase) * 3 + step - 1
            copy = remote(source, source, send_sem.at[slot], recv_sem.at[slot], moved(at, axis, step))
            copy.start()
            copies.append(copy)
        return copies

    order = (1, 2, 0)
    full_out[at["y"] // 2, at["z"], at["y"] % 2, at["x"], core] = wo_ref[...]
    swap.wait()
    first = core == 0
    for batch in (0, 1):
        lanes = pl.ds(pl.multiple_of(batch * WIDE + core * HALF, 128), HALF)
        mine, theirs = wi_ref[:, lanes], other[:, lanes]
        full_in[at["y"] // 2, at["z"], at["y"] % 2, at["x"], :, lanes] = jnp.concatenate(
            [jnp.where(first, mine, theirs), jnp.where(first, theirs, mine)], axis=0
        ).astype(jnp.bfloat16)

    flying = {}
    for batch in order:
        for part in range(3):
            flying[batch, part] = hop(batch, part, 0)
    done = []
    passed = []
    for phase in (1, 2, 3):
        for batch in order:
            for part in range(3):
                for copy in flying[batch, part]:
                    copy.wait_recv()
                    done.append(copy)
                if phase < 3:
                    flying[batch, part] = hop(batch, part, phase)
                else:
                    region = view(batch, part, "xyz")
                    slot = batch * 3 + part
                    copy = remote(region, region, pass_sem.at[slot], got_sem.at[slot], sibling)
                    copy.start()
                    passed.append(copy)
    for copy in passed:
        copy.wait()
    for copy in done:
        copy.wait_send()
    stores = [
        pltpu.make_async_copy(full_in, in_hbm, local_sem.at[0]),
        pltpu.make_async_copy(full_out, out_hbm, local_sem.at[1]),
    ]
    for copy in stores:
        copy.start()
    for copy in stores:
        copy.wait()


def gather(wi, wo):
    full_in, full_out = pl.pallas_call(
        gather_kernel,
        out_shape=(
            jax.ShapeDtypeStruct((2, 4, 2, 4, 16, COLS), jnp.bfloat16),
            jax.ShapeDtypeStruct((2, 4, 2, 4, 2, 16, D), jnp.bfloat16),
        ),
        in_specs=[pl.BlockSpec(memory_space=pltpu.VMEM)] * 2,
        out_specs=[pl.BlockSpec(memory_space=pl.ANY)] * 2,
        scratch_shapes=[
            pltpu.VMEM((8, COLS), jnp.float32),
            pltpu.VMEM((2, 4, 2, 4, 16, COLS), jnp.bfloat16),
            pltpu.VMEM((2, 4, 2, 4, 2, 16, D), jnp.bfloat16),
            pltpu.SemaphoreType.DMA((2,)),
            pltpu.SemaphoreType.DMA((81,)),
            pltpu.SemaphoreType.DMA((81,)),
            pltpu.SemaphoreType.DMA((9,)),
            pltpu.SemaphoreType.DMA((9,)),
            pltpu.SemaphoreType.DMA((2,)),
        ],
        compiler_params=pltpu.CompilerParams(collective_id=0, has_side_effects=True, vmem_limit_bytes=40 << 20),
    )(wi, wo)
    return full_in.reshape(D, COLS), full_out.reshape(INNER, D)


def scatter_kernel(
    gi_hbm,
    go_hbm,
    small_ref,
    gi_out,
    go_out,
    small_out,
    own,
    got,
    part0,
    recv1,
    part1,
    recv2,
    part2,
    recv3,
    swap_from,
    swap_to,
    small_now,
    small_got,
    load_sem,
    pass_sem,
    got_sem,
    send_sem,
    recv_sem,
    swap_sem,
    small_send,
    small_recv,
):
    at = place()
    core = at["c"]
    sibling = moved(at, "c", 1)
    enter(at)
    order = (0, 1, 2)
    pairs = [(batch, part) for batch in order for part in range(3)]

    def width_of(batch, part):
        return OUT_PARTS[part][1] if batch == 0 else PART

    def shard_view(batch, part, side):
        if batch == 0:
            start, width = OUT_PARTS[part]
            return go_hbm.at[:, side, :, pl.ds(start, width)]
        start = pl.multiple_of((batch - 1) * WIDE + side * HALF + part * PART, 128)
        return gi_hbm.at[:, :, pl.ds(start, PART)]

    small_now[0] = small_ref[...]
    small_copies = [[], [], [], []]

    def small_start(stage):
        axis = "cxyz"[stage]
        for step in (1,) if stage == 0 else (1, 2, 3):
            slot = 0 if stage == 0 else stage * 3 - 3 + step
            copy = remote(
                small_now.at[stage], small_got.at[slot], small_send.at[slot], small_recv.at[slot], moved(at, axis, step)
            )
            copy.start()
            small_copies[stage].append((slot, copy))

    def small_sum(stage):
        value = small_now[stage]
        for slot, copy in small_copies[stage]:
            copy.wait_recv()
            value = value + small_got[slot]
        if stage < 3:
            small_now[stage + 1] = value
            small_start(stage + 1)
        else:
            small_out[...] = value

    loads, passed = {}, {}
    for pair in pairs:
        slot = pair[0] * 3 + pair[1]
        lanes = pl.ds(0, width_of(*pair))
        passed[pair] = remote(
            shard_view(*pair, 1 - core), got.at[slot, :, :, lanes], pass_sem.at[slot], got_sem.at[slot], sibling
        )
        passed[pair].start()
        loads[pair] = pltpu.make_async_copy(shard_view(*pair, core), own.at[slot, :, :, lanes], load_sem.at[slot])
        loads[pair].start()
    small_start(0)

    flying = {}
    sent = []

    def hop(pair, stage, source, target):
        slot = pair[0] * 3 + pair[1]
        axis = ORDERS[pair[1]][3 - stage]
        copies = []
        for step in (1, 2, 3):
            peer = moved(at, axis, step)
            sem = (slot * 3 + stage - 1) * 3 + step - 1
            copy = remote(source(peer[axis]), target(step - 1), send_sem.at[sem], recv_sem.at[sem], peer)
            copy.start()
            copies.append(copy)
        flying[pair] = copies
        sent.extend(copies)

    for pair in pairs:
        batch, part = pair
        slot, width = batch * 3 + part, width_of(*pair)
        lanes = pl.ds(0, width)
        passed[pair].wait_recv()
        loads[pair].wait()
        axes = ORDERS[part]

        @pl.loop(0, 16)
        def _(i, slot=slot, lanes=lanes, axes=axes):
            v3, v2 = i // 4, i % 4
            for v1 in range(4):
                spot = {axes[0]: v1, axes[1]: v2, axes[2]: v3}
                chip = ((spot["y"] // 2) * 4 + spot["z"]) * 8 + (spot["y"] % 2) * 4 + spot["x"]
                part0[slot, v3, v2, v1, :, lanes] = (
                    own[slot, chip, :, lanes].astype(jnp.float32) + got[slot, chip, :, lanes].astype(jnp.float32)
                ).astype(jnp.bfloat16)

        hop(
            pair,
            1,
            lambda v, slot=slot, lanes=lanes: part0.at[slot, v, :, :, :, lanes],
            lambda k, slot=slot, lanes=lanes: recv1.at[slot, k, :, :, :, lanes],
        )
    small_sum(0)

    for pair in pairs:
        batch, part = pair
        slot, width = batch * 3 + part, width_of(*pair)
        lanes = pl.ds(0, width)
        for copy in flying[pair]:
            copy.wait_recv()
        here = at[ORDERS[part][2]]

        @pl.loop(0, 4)
        def _(v2, slot=slot, lanes=lanes, here=here):
            for v1 in range(4):
                value = part0[slot, here, v2, v1, :, lanes].astype(jnp.float32)
                for k in range(3):
                    value = value + recv1[slot, k, v2, v1, :, lanes].astype(jnp.float32)
                part1[slot, v2, v1, :, lanes] = value.astype(jnp.bfloat16)

        hop(
            pair,
            2,
            lambda v, slot=slot, lanes=lanes: part1.at[slot, v, :, :, lanes],
            lambda k, slot=slot, lanes=lanes: recv2.at[slot, k, :, :, lanes],
        )
    small_sum(1)

    for pair in pairs:
        batch, part = pair
        slot, width = batch * 3 + part, width_of(*pair)
        lanes = pl.ds(0, width)
        for copy in flying[pair]:
            copy.wait_recv()
        here = at[ORDERS[part][1]]
        for v1 in range(4):
            value = part1[slot, here, v1, :, lanes].astype(jnp.float32)
            for k in range(3):
                value = value + recv2[slot, k, v1, :, lanes].astype(jnp.float32)
            part2[slot, v1, :, lanes] = value.astype(jnp.bfloat16)
        hop(
            pair,
            3,
            lambda v, slot=slot, lanes=lanes: part2.at[slot, v, :, lanes],
            lambda k, slot=slot, lanes=lanes: recv3.at[slot, k, :, lanes],
        )
    small_sum(2)

    first = core == 0
    for pair in pairs:
        batch, part = pair
        slot, width = batch * 3 + part, width_of(*pair)
        lanes = pl.ds(0, width)
        for copy in flying[pair]:
            copy.wait_recv()
        value = part2[slot, at[ORDERS[part][0]], :, lanes].astype(jnp.float32)
        for k in range(3):
            value = value + recv3[slot, k, :, lanes].astype(jnp.float32)
        if batch == 0:
            go_out[:, pl.ds(OUT_PARTS[part][0], width)] = value
        else:
            column = pl.multiple_of((batch - 1) * WIDE + core * HALF + part * PART, 128)
            gi_out[:, pl.ds(column, PART)] = jnp.where(first, value[:8], value[8:])
            swap_from[:, pl.ds((batch - 1) * HALF + part * PART, PART)] = jnp.where(first, value[8:], value[:8])
    swap = remote(swap_from, swap_to, swap_sem.at[0], swap_sem.at[1], sibling)
    swap.start()
    small_sum(3)
    for copy in sent:
        copy.wait_send()
    for pair in pairs:
        passed[pair].wait_send()
    for copies in small_copies:
        for _, copy in copies:
            copy.wait_send()
    swap.wait()
    for batch in (1, 2):
        column = pl.multiple_of((batch - 1) * WIDE + (1 - core) * HALF, 128)
        gi_out[:, pl.ds(column, HALF)] = swap_to[:, pl.ds((batch - 1) * HALF, HALF)]


def scatter(gi, go, small):
    rows = small.shape[0]
    low = jnp.bfloat16
    return pl.pallas_call(
        scatter_kernel,
        out_shape=(
            jax.ShapeDtypeStruct((8, COLS), jnp.float32),
            jax.ShapeDtypeStruct((16, D), jnp.float32),
            jax.ShapeDtypeStruct((rows, 128), jnp.float32),
        ),
        in_specs=[pl.BlockSpec(memory_space=pl.ANY)] * 2 + [pl.BlockSpec(memory_space=pltpu.VMEM)],
        out_specs=[pl.BlockSpec(memory_space=pltpu.VMEM)] * 3,
        scratch_shapes=[
            pltpu.VMEM((9, 64, 16, PART), low),
            pltpu.VMEM((9, 64, 16, PART), low),
            pltpu.VMEM((9, 4, 4, 4, 16, PART), low),
            pltpu.VMEM((9, 3, 4, 4, 16, PART), low),
            pltpu.VMEM((9, 4, 4, 16, PART), low),
            pltpu.VMEM((9, 3, 4, 16, PART), low),
            pltpu.VMEM((9, 4, 16, PART), low),
            pltpu.VMEM((9, 3, 16, PART), low),
            pltpu.VMEM((8, WIDE), jnp.float32),
            pltpu.VMEM((8, WIDE), jnp.float32),
            pltpu.VMEM((4, rows, 128), jnp.float32),
            pltpu.VMEM((10, rows, 128), jnp.float32),
            pltpu.SemaphoreType.DMA((9,)),
            pltpu.SemaphoreType.DMA((9,)),
            pltpu.SemaphoreType.DMA((9,)),
            pltpu.SemaphoreType.DMA((81,)),
            pltpu.SemaphoreType.DMA((81,)),
            pltpu.SemaphoreType.DMA((2,)),
            pltpu.SemaphoreType.DMA((10,)),
            pltpu.SemaphoreType.DMA((10,)),
        ],
        compiler_params=pltpu.CompilerParams(collective_id=1, has_side_effects=True, vmem_limit_bytes=48 << 20),
    )(gi.reshape(64, 16, COLS), go.reshape(64, 2, 16, D), small)


eps = 1e-05
highest = lax.Precision.HIGHEST


def rolled_down(x, step):
    zeros = jnp.zeros((8, x.shape[1]), x.dtype)
    return pltpu.roll(jnp.concatenate([zeros, x], axis=0), step, axis=0)[8:]


def rolled_up(x, step):
    rows = x.shape[0]
    zeros = jnp.zeros((8, x.shape[1]), x.dtype)
    return pltpu.roll(jnp.concatenate([x, zeros], axis=0), rows + 8 - step, axis=0)[:rows]


def tile(j, base=0):
    return pl.ds(pl.multiple_of(base + j * 128, 128), 128)


def dot_nt(a, b):
    return lax.dot_general(a, b, (((1,), (1,)), ((), ())), preferred_element_type=jnp.float32)


def dot(a, b, **more):
    return jnp.dot(a, b, preferred_element_type=jnp.float32, **more)


def row_sum(x):
    return jnp.sum(x, axis=1, keepdims=True)


def col_sum(x):
    return jnp.sum(x, axis=0, keepdims=True)


def mix_kernel(
    length_ref,
    proj,
    taps,
    gain,
    skip,
    heads,
    wout,
    tokens,
    cotangent,
    block_out,
    inner,
    back,
    dproj,
    gtaps,
    ggain,
    gskip,
    gheads,
    act,
    dsilu,
    y_ref,
    dinner,
    mix,
    mix_t,
    dmix_t,
    cum_ref,
    cum_t,
    step_ref,
    q_ref,
    m_ref,
    dcum_ref,
    dstep_ref,
):
    low, full = jnp.bfloat16, jnp.float32
    lane = lax.broadcasted_iota(jnp.int32, (TOK, 128), 1)
    left = lane < HEAD
    row = lax.broadcasted_iota(jnp.int32, (TOK, TOK), 0)
    column = lax.broadcasted_iota(jnp.int32, (TOK, TOK), 1)

    @pl.loop(0, XBC // 128)
    def _(j):
        cols = tile(j)
        x = proj[:, tile(j, INNER)]
        pre = taps[4:5, cols] + taps[3:4, cols] * x
        for step in (1, 2, 3):
            pre = pre + taps[3 - step : 4 - step, cols] * rolled_down(x, step)
        sig = jax.nn.sigmoid(pre)
        act[:, cols] = (pre * sig).astype(low)
        dsilu[:, cols] = sig * (1.0 + pre * (1.0 - sig))

    raw = proj[:, INNER + XBC : INNER + XBC + 128] + heads[0:1, :]
    grown = jnp.exp(-jnp.abs(raw))
    more = 1.0 + grown
    logged = jnp.where(more == 1.0, grown, jnp.log(more) * grown / jnp.where(more == 1.0, 1.0, more - 1.0))
    steps = jnp.where(lane < HEADS, jnp.maximum(raw, 0.0) + logged, 0.0)
    rate = -jnp.exp(heads[1:2, :])
    cum = dot((row >= column).astype(full), steps * rate, precision=highest)
    step_ref[...] = steps
    cum_ref[...] = cum
    turned = cum.T
    for head in range(HEADS):
        cum_t[head] = turned[head : head + 1]
    keys = act[:, INNER : INNER + STATE]
    reads = act[:, INNER + STATE :]
    mixed = jnp.where(row >= column, dot_nt(reads, keys), 0.0)
    mix[...] = mixed
    mix_t[...] = mixed.T
    dmix_t[...] = jnp.zeros_like(dmix_t)
    q_ref[...] = jnp.zeros_like(q_ref)
    m_ref[...] = jnp.zeros_like(m_ref)
    dcum_ref[...] = jnp.zeros_like(dcum_ref)
    dstep_ref[...] = jnp.zeros_like(dstep_ref)

    def pair(j):
        turn = lax.rem(128 - 2 * j, 128)
        cums = pltpu.roll(cum_ref[...], turn, axis=1)
        sizes = pltpu.roll(step_ref[...], turn, axis=1)
        wide = jnp.where(left, sizes[:, 0:1], sizes[:, 1:2])
        values = act[:, tile(j)].astype(full)
        return cums, wide, values, (values * wide).astype(low)

    @pl.loop(0, HEADS // 2)
    def _(j):
        cols = tile(j)
        cums, _, values, scaled = pair(j)
        for block in range(TOK // 128):
            first, last = block * 128, block * 128 + 128
            found = []
            for e in (0, 1):
                pieces = []
                for other in range(block + 1):
                    span = slice(other * 128, other * 128 + 128)
                    gap = cums[first:last, e : e + 1] - cum_t[2 * j + e, :, span]
                    if other == block:
                        gap = jnp.minimum(gap, 0.0)
                    pieces.append((mix[first:last, span] * jnp.exp(gap)).astype(low))
                found.append(dot(jnp.concatenate(pieces, axis=1), scaled[:last]))
            y = jnp.where(left[:128], found[0], found[1]) + skip[:, cols] * values[first:last]
            y_ref[first:last, cols] = y
            gate = proj[first:last, cols]
            gated = y * gate * jax.nn.sigmoid(gate)
            q_ref[first:last] += gated * gated

    q_ref[...] = jnp.broadcast_to(lax.rsqrt(row_sum(q_ref[...]) / INNER + eps), (TOK, 128))

    @pl.loop(0, INNER // 128)
    def _(j):
        cols = tile(j)
        gate = proj[:, cols]
        gated = y_ref[:, cols] * gate * jax.nn.sigmoid(gate)
        inner[:, cols] = (gated * q_ref[...] * gain[:, cols]).astype(low)

    live = (lax.broadcasted_iota(jnp.int32, (TOK, 256), 0) < length_ref[0, 0]).astype(full)

    @pl.loop(0, D // 256)
    def _(j):
        cols = pl.ds(pl.multiple_of(j * 256, 256), 256)
        branch = dot(inner[...], wout[:, cols])
        block_out[:, cols] = (tokens[:, cols].astype(full) + live * branch).astype(low)
        back[:, cols] = (live * cotangent[:, cols].astype(full)).astype(low)

    @pl.loop(0, INNER // 256)
    def _(j):
        cols = pl.ds(pl.multiple_of(j * 256, 256), 256)
        dinner[:, cols] = dot_nt(back[...], wout[cols, :])

    @pl.loop(0, INNER // 128)
    def _(j):
        cols = tile(j)
        gate = proj[:, cols]
        u = y_ref[:, cols] * gate * jax.nn.sigmoid(gate) * q_ref[...]
        du = dinner[:, cols] * u
        ggain[:, cols] = col_sum(du)
        m_ref[...] += du * gain[:, cols]

    m_ref[...] = jnp.broadcast_to(row_sum(m_ref[...]) / INNER, (TOK, 128))

    def conv_back(dact, j):
        cols = tile(j)
        x = proj[:, tile(j, INNER)]
        dpre = dact * dsilu[:, cols]
        gtaps[4:5, cols] = col_sum(dpre)
        gtaps[3:4, cols] = col_sum(dpre * x)
        dx = taps[3:4, cols] * dpre
        for step in (1, 2, 3):
            moved_up = rolled_up(dpre, step)
            gtaps[3 - step : 4 - step, cols] = col_sum(moved_up * x)
            dx = dx + taps[3 - step : 4 - step, cols] * moved_up
        dproj[:, tile(j, INNER)] = dx.astype(low)

    @pl.loop(0, HEADS // 2)
    def _(j):
        cols = tile(j)
        cums, wide, values, scaled = pair(j)
        y, gate, q = y_ref[:, cols], proj[:, cols], q_ref[...]
        sig = jax.nn.sigmoid(gate)
        silu = gate * sig
        du = dinner[:, cols] * gain[:, cols]
        dgated = q * (du - y * silu * q * m_ref[...])
        dproj[:, cols] = (dgated * y * sig * (1.0 + gate * (1.0 - sig))).astype(low)
        dy = dgated * silu
        dy_low = dy.astype(low)
        gskip[j] = col_sum(dy * values)
        own = (jnp.where(left, scaled, jnp.zeros_like(scaled)), jnp.where(left, jnp.zeros_like(scaled), scaled))
        found = []
        for block in range(TOK // 128):
            first, last = block * 128, block * 128 + 128
            both = []
            total = None
            for e in (0, 1):
                dm = dot_nt(own[e][first:last], dy_low[first:])
                pieces, shares = [], []
                for other in range(block, TOK // 128):
                    span = slice(other * 128, other * 128 + 128)
                    gap = cum_t[2 * j + e, :, span] - cums[first:last, e : e + 1]
                    if other == block:
                        gap = jnp.minimum(gap, 0.0)
                    decay = jnp.exp(gap)
                    pieces.append((mix_t[first:last, span] * decay).astype(low))
                    shares.append(dm[:, (other - block) * 128 : (other - block + 1) * 128] * decay)
                both.append(dot(jnp.concatenate(pieces, axis=1), dy_low[first:]))
                share = jnp.concatenate(shares, axis=1)
                total = share if total is None else total + share
            dmix_t[first:last, first:] += total
            found.append(jnp.where(left[:128], both[0], both[1]))
        taken = jnp.concatenate(found, axis=0)
        direct = values * taken
        crossing = dy_low.astype(full) * (y - skip[:, cols] * values) - scaled.astype(full) * taken
        for e in (0, 1):
            mine = left if e == 0 else jnp.logical_not(left)
            here = lane == 2 * j + e
            dcum_ref[...] = jnp.where(here, row_sum(jnp.where(mine, crossing, 0.0)), dcum_ref[...])
            dstep_ref[...] = jnp.where(here, row_sum(jnp.where(mine, direct, 0.0)), dstep_ref[...])
        conv_back(wide * taken + skip[:, cols] * dy, j)

    masked = jnp.where(row <= column, dmix_t[...], 0.0)
    conv_back(dot(masked.astype(low), act[:, INNER + STATE :]), INNER // 128)
    conv_back(dot(masked.T.astype(low), act[:, INNER : INNER + STATE]), INNER // 128 + 1)
    dacc = dot((row <= column).astype(full), dcum_ref[...], precision=highest)
    dstep = dstep_ref[...] + dacc * rate
    draw = jnp.where(
        lane < HEADS, dstep * jax.nn.sigmoid(proj[:, INNER + XBC : INNER + XBC + 128] + heads[0:1, :]), 0.0
    )
    dproj[:, INNER + XBC : INNER + XBC + 128] = draw.astype(low)
    dproj[:, INNER + XBC + 128 :] = jnp.zeros((TOK, 128), low)
    gheads[...] = jnp.zeros_like(gheads)
    gheads[0:1, :] = col_sum(draw)
    gheads[1:2, :] = rate * col_sum(dacc * step_ref[...])


def mixer(length, proj, taps, gain, skip, heads, wout, tokens, cotangent):
    full, low = jnp.float32, jnp.bfloat16
    vmem = pl.BlockSpec(memory_space=pltpu.VMEM)
    return pl.pallas_call(
        mix_kernel,
        out_shape=(
            jax.ShapeDtypeStruct((TOK, D), low),
            jax.ShapeDtypeStruct((TOK, INNER), low),
            jax.ShapeDtypeStruct((TOK, D), low),
            jax.ShapeDtypeStruct((TOK, COLS), low),
            jax.ShapeDtypeStruct((8, XBC), full),
            jax.ShapeDtypeStruct((1, INNER), full),
            jax.ShapeDtypeStruct((16, 1, 128), full),
            jax.ShapeDtypeStruct((8, 128), full),
        ),
        in_specs=[pl.BlockSpec(memory_space=pltpu.SMEM)] + [vmem] * 8,
        out_specs=[vmem] * 8,
        scratch_shapes=[
            pltpu.VMEM((TOK, XBC), low),
            pltpu.VMEM((TOK, XBC), full),
            pltpu.VMEM((TOK, INNER), full),
            pltpu.VMEM((TOK, INNER), full),
            pltpu.VMEM((TOK, TOK), full),
            pltpu.VMEM((TOK, TOK), full),
            pltpu.VMEM((TOK, TOK), full),
            pltpu.VMEM((TOK, 128), full),
            pltpu.VMEM((HEADS, 1, TOK), full),
            pltpu.VMEM((TOK, 128), full),
            pltpu.VMEM((TOK, 128), full),
            pltpu.VMEM((TOK, 128), full),
            pltpu.VMEM((TOK, 128), full),
            pltpu.VMEM((TOK, 128), full),
        ],
        compiler_params=pltpu.CompilerParams(vmem_limit_bytes=60 << 20),
    )(length, proj, taps, gain, skip, heads, wout, tokens, cotangent)


def scaled_rows(values, gains):
    return values * lax.rsqrt(jnp.mean(values * values, axis=-1, keepdims=True) + eps) * gains


def body(
    tokens,
    lengths,
    placement_ids,
    norm_gain,
    in_weight,
    conv_weight,
    conv_bias,
    dt_bias,
    a_log,
    d_skip,
    inner_gain,
    out_weight,
    cotangent,
):
    full = jnp.float32
    sequence_id = placement_ids[0]
    slot_length = jnp.sum(
        jnp.where(lax.broadcasted_iota(jnp.int32, lengths.shape, 0) == sequence_id, lengths, 0)
    )
    side = jnp.concatenate(
        [
            norm_gain[:, None],
            inner_gain.reshape(2, 8).T,
            jnp.zeros((8, COLS - PROJ - 3 - 128), jnp.bfloat16),
            jnp.concatenate(
                [
                    jnp.pad(conv_weight, ((0, 0), (0, 110))),
                    jnp.pad(conv_bias, (0, 110))[None],
                    jnp.zeros((3, 128), jnp.bfloat16),
                ],
                axis=0,
            ),
        ],
        axis=1,
    )
    packed, full_out = gather(jnp.concatenate([in_weight, side], axis=1).astype(jnp.float32), out_weight)
    full_in = packed[:, :PROJ]
    full_gain = packed[:, PROJ]
    full_inner = packed[:, PROJ + 1 : PROJ + 3].reshape(128, 8, 2).transpose(0, 2, 1).reshape(INNER)
    taps = packed[:, COLS - 128 : COLS - 110].reshape(128, 8, 18)
    full_conv = taps[:, :CONV].transpose(1, 0, 2).reshape(CONV, XBC)
    full_bias = taps[:, CONV].reshape(XBC)
    normed, pull_norm = jax.vjp(scaled_rows, tokens.astype(full), full_gain.astype(full))
    normed_low = normed.astype(jnp.bfloat16)
    projected = jnp.dot(normed_low, packed, preferred_element_type=full)
    heads = jnp.pad(jnp.stack([dt_bias, a_log]), ((0, 6), (0, 96)))
    block_out, inner_low, grad_branch, grad_proj, grad_taps, grad_gain, grad_skip, grad_heads = mixer(
        slot_length.reshape(1, 1),
        projected,
        jnp.pad(jnp.concatenate([full_conv, full_bias[None]], axis=0), ((0, 3), (0, 0))).astype(full),
        full_inner.astype(full)[None],
        jnp.repeat(d_skip, HEAD)[None],
        heads,
        full_out,
        tokens,
        cotangent,
    )
    grad_out = jnp.einsum("tk,td->kd", inner_low, grad_branch, preferred_element_type=full)
    grad_in = jnp.einsum("td,tk->dk", normed_low, grad_proj, preferred_element_type=full)
    grad_normed = jnp.einsum("tk,dk->td", grad_proj, packed, preferred_element_type=full)
    grad_inputs, grad_norm_gain = pull_norm(grad_normed)
    input_grad = (cotangent.astype(full) + grad_inputs).astype(jnp.bfloat16)
    small = jnp.concatenate(
        [
            grad_norm_gain,
            grad_taps[:5].reshape(-1),
            grad_gain[0],
            grad_heads[0, :HEADS],
            grad_heads[1, :HEADS],
            jnp.sum(grad_skip.reshape(HEADS, HEAD), axis=1),
            jnp.zeros((16384 - 14688,), full),
        ]
    ).reshape(128, 128)
    shard_in, shard_out, small = scatter(grad_in.astype(jnp.bfloat16), grad_out.astype(jnp.bfloat16), small)
    small = small.reshape(-1)
    me = lax.axis_index("dp") * 16 + lax.axis_index("fsdp")
    sums = []
    spot = 0
    for count, copies in ((D, 1), (XBC, CONV), (XBC, 1), (INNER, 1)):
        whole = small[spot : spot + count * copies].reshape(copies, count)
        sums.append(lax.dynamic_slice(whole, (0, me * (count // 128)), (copies, count // 128)))
        spot += count * copies
    weight_sums = (sums[0][0], shard_in[:, :PROJ], sums[1], sums[2][0], sums[3][0], shard_out)
    head_totals = (small[spot : spot + 32], small[spot + 32 : spot + 64], small[spot + 64 : spot + 96])
    return (
        block_out,
        input_grad,
        weight_sums[0],
        weight_sums[1],
        weight_sums[2],
        weight_sums[3],
        head_totals[0],
        head_totals[1],
        head_totals[2],
        weight_sums[4],
        weight_sums[5],
    )


def solution(mesh):
    placed = (
        P(("dp", "fsdp"), None),
        P(),
        P(("dp", "fsdp")),
        P(("dp", "fsdp")),
        P(("dp", "fsdp"), None),
        P(None, ("dp", "fsdp")),
        P(("dp", "fsdp")),
        P(),
        P(),
        P(),
        P(("dp", "fsdp")),
        P(("dp", "fsdp"), None),
        P(("dp", "fsdp"), None),
    )
    return jax.shard_map(
        body,
        mesh=mesh,
        in_specs=placed,
        out_specs=(
            P(("dp", "fsdp"), None),
            P(("dp", "fsdp"), None),
            P(("dp", "fsdp")),
            P(("dp", "fsdp"), None),
            P(None, ("dp", "fsdp")),
            P(("dp", "fsdp")),
            P(),
            P(),
            P(),
            P(("dp", "fsdp")),
            P(("dp", "fsdp"), None),
        ),
        check_vma=False,
    )
```

```python
import jax
import jax.numpy as jnp
import numpy as np
from jax import lax
from jax.experimental import pallas as pl
from jax.experimental.pallas import tpu as pltpu
from jax.sharding import PartitionSpec as P

D = 1024
INNER = 2048
STATE = 128
HEAD = 64
CONV = 4
HEADS = 32
XBC = 2304
PROJ = 4384
TOK = 512
CHIPS = 64
COLS = 4608
SIDE = 3328
MESH = pl.DeviceIdType.MESH
ORDERS = (("x", "y", "z"), ("y", "z", "x"), ("z", "x", "y"))
OUT, GATE, REST = 0, 1, 2
EVEN = ((0, 384), (384, 384), (768, 256))
PARTS = {OUT: EVEN, GATE: EVEN, REST: ((0, 512), (512, 384), (896, 384))}
LOCAL = {OUT: 0, GATE: 1024, REST: 2048}
WIDTH = {GATE: 1024, REST: 1280}

eps = 1e-05
highest = lax.Precision.HIGHEST


def place():
    dp, fsdp = lax.axis_index("dp"), lax.axis_index("fsdp")
    return {"x": (fsdp // 2) % 4, "y": (dp // 4) * 2 + fsdp // 8, "z": dp % 4, "c": fsdp % 2}


def device(at):
    y = at["y"]
    return ((y // 2) * 4 + at["z"], (y % 2) * 8 + at["x"] * 2 + at["c"])


def moved(at, axis, step):
    size = 2 if axis == "c" else 4
    return dict(at, **{axis: lax.rem(at[axis] + step, size)})


def enter(at):
    barrier = pltpu.get_barrier_semaphore()
    peers = [moved(at, axis, step) for axis in "xyz" for step in (1, 2, 3)] + [moved(at, "c", 1)]
    for peer in peers:
        pl.semaphore_signal(barrier, inc=1, device_id=device(peer), device_id_type=MESH)
    pl.semaphore_wait(barrier, len(peers))


def remote(src, dst, send, recv, peer):
    return pltpu.make_async_remote_copy(
        src_ref=src, dst_ref=dst, send_sem=send, recv_sem=recv, device_id=device(peer), device_id_type=MESH
    )


def chips(at, full):
    every = slice(None)
    y, z, x = at["y"], at["z"], at["x"]
    return (
        every if "y" in full else y // 2,
        every if "z" in full else z,
        every if "y" in full else y % 2,
        every if "x" in full else x,
    )


def rolled_down(x, step):
    zeros = jnp.zeros((8, x.shape[1]), x.dtype)
    return pltpu.roll(jnp.concatenate([zeros, x], axis=0), step, axis=0)[8:]


def rolled_up(x, step):
    rows = x.shape[0]
    zeros = jnp.zeros((8, x.shape[1]), x.dtype)
    return pltpu.roll(jnp.concatenate([x, zeros], axis=0), rows + 8 - step, axis=0)[:rows]


def tile(j, base=0, size=128):
    return pl.ds(pl.multiple_of(base + j * size, 128), size)


def dot_nt(a, b):
    return lax.dot_general(a, b, (((1,), (1,)), ((), ())), preferred_element_type=jnp.float32)


def dot(a, b, **more):
    return jnp.dot(a, b, preferred_element_type=jnp.float32, **more)


def row_sum(x):
    return jnp.sum(x, axis=1, keepdims=True)


def col_sum(x):
    return jnp.sum(x, axis=0, keepdims=True)


def block_kernel(
    wi,
    wo,
    tokens,
    cotangent,
    live,
    heads,
    skip,
    spots,
    block_out,
    input_grad,
    gi_out,
    go_out,
    small_out,
    full_in,
    other,
    blk,
    full_out,
    work,
    proj,
    act,
    dsilu,
    y_ref,
    dinner,
    dproj,
    inner_t,
    normed,
    normed_t,
    mix,
    mix_t,
    cum_ref,
    cum_t,
    step_ref,
    q_ref,
    m_ref,
    dcum_ref,
    dstep_ref,
    taps,
    gain,
    norm_gain,
    part0,
    recv1,
    part1,
    recv2,
    part2,
    recv3,
    swap_from,
    swap_to,
    small_now,
    small_got,
    swap_sem,
    local_sem,
    ag_send,
    ag_recv,
    ag_pass,
    ag_got,
    rs_send,
    rs_recv,
    rs_pass,
    rs_got,
    small_send,
    small_recv,
):
    low, full = jnp.bfloat16, jnp.float32
    at = place()
    core = at["c"]
    first = core == 0
    sibling = moved(at, "c", 1)
    here = chips(at, ())
    enter(at)

    swap = remote(wi, other, swap_sem.at[0], swap_sem.at[1], sibling)
    swap.start()
    full_out[here + (core,)] = wo[...]

    def held(batch, part, reach):
        start, width = PARTS[batch][part]
        if batch == OUT:
            return full_out.at[chips(at, reach) + (core, slice(None), pl.ds(start, width))]
        column = core * WIDTH[batch] + start + (INNER if batch == REST else 0)
        return full_in.at[chips(at, reach) + (slice(None), pl.ds(pl.multiple_of(column, 128), width))]

    flying = {}
    drained = []

    def hop(batch, part, phase):
        target = held(batch, part, ORDERS[part][:phase])
        source = target
        if phase == 0 and batch != OUT:
            start, width = PARTS[batch][part]
            source = blk.at[:, pl.ds((INNER // 2 if batch == REST else 0) + start, width)]
        flying[batch, part] = []
        for step in (1, 2, 3):
            slot = ((batch * 3 + part) * 3 + phase) * 3 + step - 1
            copy = remote(source, target, ag_send.at[slot], ag_recv.at[slot], moved(at, ORDERS[part][phase], step))
            copy.start()
            flying[batch, part].append(copy)
            drained.append(copy)

    def landed(batch, part):
        for copy in flying[batch, part]:
            copy.wait_recv()

    given = {}

    def give(batch):
        for part in range(3):
            landed(batch, part)
            region = held(batch, part, "xyz")
            slot = batch * 3 + part
            given[batch, part] = remote(region, region, ag_pass.at[slot], ag_got.at[slot], sibling)
            given[batch, part].start()
            drained.append(given[batch, part])

    def taken(batch):
        for part in range(3):
            given[batch, part].wait_recv()

    swap.wait()
    for batch, base in ((GATE, 0), (REST, INNER)):
        width = WIDTH[batch]
        lanes = pl.ds(pl.multiple_of(base + core * width, 128), width)
        mine, theirs = wi[:, lanes], other[:, lanes]
        blk[:, base // 2 : base // 2 + width] = jnp.concatenate(
            [jnp.where(first, mine, theirs), jnp.where(first, theirs, mine)], axis=0
        ).astype(low)
    stores = []
    for batch, base in ((REST, INNER), (GATE, 0)):
        width = WIDTH[batch]
        lanes = pl.ds(pl.multiple_of(base + core * width, 128), width)
        copy = pltpu.make_async_copy(
            blk.at[:, pl.ds(base // 2, width)], full_in.at[here + (slice(None), lanes)], local_sem.at[len(stores)]
        )
        copy.start()
        stores.append(copy)
    for batch in (REST, GATE, OUT):
        for part in range(3):
            hop(batch, part, 0)
    for copy in stores:
        copy.wait()
    for phase in (1, 2):
        for batch in (REST, GATE, OUT):
            for part in range(3):
                landed(batch, part)
                hop(batch, part, phase)

    lane = lax.broadcasted_iota(jnp.int32, (TOK, 128), 1)
    left = lane < HEAD
    row = lax.broadcasted_iota(jnp.int32, (TOK, TOK), 0)
    column = lax.broadcasted_iota(jnp.int32, (TOK, TOK), 1)
    m_ref[...] = jnp.zeros_like(m_ref)
    for j in range(D // 128):
        x = tokens[:, j * 128 : j * 128 + 128].astype(full)
        m_ref[...] += x * x
    token_scale = lax.rsqrt(row_sum(m_ref[...]) / D + eps)

    def loaded(slot, column, width):
        return pltpu.make_async_copy(
            full_in.at[:, :, :, :, :, pl.ds(column, width)],
            work.reshape(4, 4, 2, 4, 16, 512).at[pl.ds(2 * slot, 2), :, :, :, :, pl.ds(0, width)],
            local_sem.at[2 + slot],
        )

    def streamed(columns, use):
        copies = [loaded(i % 2, column, width) for i, (column, width) in enumerate(columns)]
        copies[0].start()
        for i, (column, width) in enumerate(columns):
            if i + 1 < len(columns):
                copies[i + 1].start()
            copies[i].wait()
            use(column, width, work[pl.ds(CHIPS * (i % 2), CHIPS), :, :width].reshape(D, width))

    give(REST)
    taken(REST)
    load = loaded(1, COLS - 128, 128)
    load.start()
    load.wait()
    packed = work[CHIPS:, :, :128].reshape(D, 128)
    pick = lax.broadcasted_iota(jnp.int32, (128, D), 0) * 8 == lax.broadcasted_iota(jnp.int32, (128, D), 1)
    shared = dot(pick.astype(low), packed).astype(low)

    def spread(base, lanes, owners):
        count = lanes.shape[1]
        line = lax.broadcasted_iota(jnp.int32, (128, count), 0)
        found = dot(shared, (line == lanes + base).astype(low))
        return col_sum(jnp.where(line == owners, found, 0.0))

    count = lax.broadcasted_iota(jnp.int32, (1, INNER), 1)
    norm_gain[...] = spread(0, count[:, :D] & 7, count[:, :D] >> 3)
    gain[...] = spread(8, count & 15, count >> 4)
    taps[...] = jnp.zeros_like(taps)
    taps[4:5, :] = spread(24, spots[0:1, :], spots[1:2, :])
    for k in range(CONV):
        taps[k : k + 1, :] = spread(42 + 18 * k, spots[0:1, :], spots[1:2, :])

    for j in range(D // 128):
        cols = slice(j * 128, j * 128 + 128)
        value = (tokens[:, cols].astype(full) * token_scale * norm_gain[:, cols]).astype(low)
        normed[:, cols] = value
        normed_t[j * 8 : j * 8 + 8] = value.T.reshape(8, 16, TOK)

    def project(column, width, weight):
        proj[:, column : column + width] = dot(normed[...], weight)

    streamed([(INNER + 512 * i, 512) for i in range(4)] + [(COLS - 512, 384)], project)
    give(GATE)

    @pl.loop(0, XBC // 128)
    def _(j):
        cols = tile(j)
        x = proj[:, tile(j, INNER)]
        pre = taps[4:5, cols] + taps[3:4, cols] * x
        for step in (1, 2, 3):
            pre = pre + taps[3 - step : 4 - step, cols] * rolled_down(x, step)
        sig = jax.nn.sigmoid(pre)
        act[:, cols] = (pre * sig).astype(low)
        dsilu[:, cols] = (sig * (1.0 + pre * (1.0 - sig))).astype(low)

    raw = proj[:, INNER + XBC : INNER + XBC + 128] + heads[0:1, :]
    grown = jnp.exp(-jnp.abs(raw))
    more = 1.0 + grown
    logged = jnp.where(more == 1.0, grown, jnp.log(more) * grown / jnp.where(more == 1.0, 1.0, more - 1.0))
    steps = jnp.where(lane < HEADS, jnp.maximum(raw, 0.0) + logged, 0.0)
    rate = -jnp.exp(heads[1:2, :])
    cum = dot((row >= column).astype(full), steps * rate, precision=highest)
    step_ref[...] = steps
    cum_ref[...] = cum
    turned = cum.T
    for head in range(HEADS):
        cum_t[head] = turned[head : head + 1]
    mixed = jnp.where(row >= column, dot_nt(act[:, INNER + STATE :], act[:, INNER : INNER + STATE]), 0.0)
    mix[...] = mixed
    mix_t[...] = mixed.T

    taken(GATE)
    streamed([(512 * i, 512) for i in range(4)], project)
    give(OUT)
    q_ref[...] = jnp.zeros_like(q_ref)
    dcum_ref[...] = jnp.zeros_like(dcum_ref)
    dstep_ref[...] = jnp.zeros_like(dstep_ref)

    def pair(j):
        turn = lax.rem(128 - 2 * j, 128)
        cums = pltpu.roll(cum_ref[...], turn, axis=1)
        sizes = pltpu.roll(step_ref[...], turn, axis=1)
        wide = jnp.where(left, sizes[:, 0:1], sizes[:, 1:2])
        values = act[:, tile(j)].astype(full)
        return cums, wide, values, (values * wide).astype(low)

    @pl.loop(0, HEADS // 2)
    def _(j):
        cols = tile(j)
        cums, _, values, scaled = pair(j)
        for block in range(TOK // 128):
            start, last = block * 128, block * 128 + 128
            found = []
            for e in (0, 1):
                pieces = []
                for past in range(block + 1):
                    span = slice(past * 128, past * 128 + 128)
                    gap = cums[start:last, e : e + 1] - cum_t[2 * j + e, :, span]
                    if past == block:
                        gap = jnp.minimum(gap, 0.0)
                    pieces.append((mix[start:last, span] * jnp.exp(gap)).astype(low))
                found.append(dot(jnp.concatenate(pieces, axis=1), scaled[:last]))
            y = jnp.where(left[:128], found[0], found[1]) + skip[:, cols] * values[start:last]
            y_ref[start:last, cols] = y
            gate = proj[start:last, cols]
            gated = y * gate * jax.nn.sigmoid(gate)
            q_ref[start:last] += gated * gated

    q_ref[...] = jnp.broadcast_to(lax.rsqrt(row_sum(q_ref[...]) / INNER + eps), (TOK, 128))
    mix[...] = jnp.zeros_like(mix)

    @pl.loop(0, INNER // 128)
    def _(j):
        cols = tile(j)
        gate = proj[:, cols]
        gated = y_ref[:, cols] * gate * jax.nn.sigmoid(gate)
        value = (gated * q_ref[...] * gain[:, cols]).astype(low)
        dproj[:, cols] = value
        inner_t[pl.ds(4 * j, 4)] = value.T.reshape(4, 2, 16, TOK)

    for j in range(D // 128):
        cols = slice(j * 128, j * 128 + 128)
        normed[:, cols] = (live[...] * cotangent[:, cols].astype(full)).astype(low)

    def grads(batch, part, side, half):
        start, width = PARTS[batch][part]
        if batch == OUT:
            lhs = inner_t[pl.ds(32 * half, 32), side].reshape(TOK, TOK)
            rhs = normed[:, start : start + width]
        else:
            lhs = normed_t[pl.ds(32 * half, 32)].reshape(TOK, TOK)
            base = (INNER if batch == REST else 0) + start
            rhs = dproj[:, pl.ds(pl.multiple_of(base + side * WIDTH[batch], 128), width)]
        return dot(lhs, rhs)

    def spot_of(part, half, m):
        spot = {"y": 2 * half + (m // 4) % 2, "z": m // 8, "x": m % 4}
        axes = ORDERS[part]
        return spot[axes[2]] * 16 + spot[axes[1]] * 4 + spot[axes[0]]

    users = [None, None]

    def rs_give(batch, part, slot):
        if users[slot] is not None:
            users[slot].wait_send()
        width = PARTS[batch][part][1]
        for half in (0, 1):
            value = grads(batch, part, 1 - core, half).astype(low)
            for m in range(32):
                work[CHIPS * slot + spot_of(part, half, m), :, :width] = value[16 * m : 16 * m + 16]
        copy = rs_pass_copy(batch, part, slot)
        copy.start()
        users[slot] = copy

    def rs_pass_copy(batch, part, slot):
        width = PARTS[batch][part][1]
        sem = batch * 3 + part
        return remote(
            work.at[pl.ds(CHIPS * slot, CHIPS), :, pl.ds(0, width)],
            part0.at[:, :, lanes_of(batch, part)],
            rs_pass.at[sem],
            rs_got.at[sem],
            sibling,
        )

    def lanes_of(batch, part):
        start, width = PARTS[batch][part]
        return pl.ds(LOCAL[batch] + start, width)

    def rs_copies(batch, part, stage):
        lanes = lanes_of(batch, part)
        axis = ORDERS[part][3 - stage]
        copies = []
        for step in (1, 2, 3):
            peer = moved(at, axis, step)
            there, slot = peer[axis], pl.ds(step - 1, 1)
            if stage == 1:
                source, target = part0.at[pl.ds(there * 16, 16), :, lanes], recv1.at[pl.ds(16 * step - 16, 16), :, lanes]
            elif stage == 2:
                source, target = part1.at[pl.ds(there * 4, 4), :, lanes], recv2.at[pl.ds(4 * step - 4, 4), :, lanes]
            else:
                source, target = part2.at[pl.ds(there, 1), :, lanes], recv3.at[slot, :, lanes]
            sem = ((batch * 3 + part) * 3 + stage - 1) * 3 + step - 1
            copies.append(remote(source, target, rs_send.at[sem], rs_recv.at[sem], peer))
        return copies

    def rs_hop(batch, part, stage):
        for copy in rs_copies(batch, part, stage):
            copy.start()

    def rs_landed(batch, part, stage):
        for copy in rs_copies(batch, part, stage):
            copy.wait_recv()

    def rs_own(batch, part):
        lanes = lanes_of(batch, part)
        rs_pass_copy(batch, part, 0).wait_recv()
        for half in (0, 1):
            value = grads(batch, part, core, half)
            for m in range(32):
                spot = spot_of(part, half, m)
                now = pl.ds(spot, 1)
                part0[now, :, lanes] = (value[16 * m : 16 * m + 16][None] + part0[now, :, lanes].astype(full)).astype(low)
        rs_hop(batch, part, 1)

    def rs_one(batch, part):
        lanes = lanes_of(batch, part)
        rs_landed(batch, part, 1)
        mine = at[ORDERS[part][2]] * 16
        for i in range(16):
            now = pl.ds(i, 1)
            value = part0[pl.ds(mine + i, 1), :, lanes].astype(full)
            for k in range(3):
                value = value + recv1[pl.ds(16 * k + i, 1), :, lanes].astype(full)
            part1[now, :, lanes] = value.astype(low)
        rs_hop(batch, part, 2)

    def rs_two(batch, part):
        lanes = lanes_of(batch, part)
        rs_landed(batch, part, 2)
        mine = at[ORDERS[part][1]] * 4
        for i in range(4):
            now = pl.ds(i, 1)
            value = part1[pl.ds(mine + i, 1), :, lanes].astype(full)
            for k in range(3):
                value = value + recv2[pl.ds(4 * k + i, 1), :, lanes].astype(full)
            part2[now, :, lanes] = value.astype(low)
        rs_hop(batch, part, 3)

    def rs_three(batch, part):
        lanes = lanes_of(batch, part)
        rs_landed(batch, part, 3)
        value = part2[pl.ds(at[ORDERS[part][0]], 1), :, lanes].astype(full)
        for k in range(3):
            value = value + recv3[pl.ds(k, 1), :, lanes].astype(full)
        value = value[0]
        start, width = PARTS[batch][part]
        if batch == OUT:
            go_out[:, start : start + width] = value
            return
        base = INNER if batch == REST else 0
        at_column = pl.multiple_of(base + core * WIDTH[batch] + start, 128)
        gi_out[:, pl.ds(at_column, width)] = jnp.where(first, value[:8], value[8:])
        swap_from[:, pl.ds(base // 2 + start, width)] = jnp.where(first, value[8:], value[:8])

    taken(OUT)
    wout = full_out.reshape(INNER, D)
    for part in range(2):
        rs_give(OUT, part, part)

    wide_live = jnp.concatenate([live[...], live[...]], axis=1)

    @pl.loop(0, D // 256)
    def _(j):
        cols = tile(j, 0, 256)
        branch = dot(dproj[:, :INNER], wout[:, cols])
        block_out[:, cols] = (tokens[:, cols].astype(full) + wide_live * branch).astype(low)

    rs_give(OUT, 2, 0)

    @pl.loop(0, INNER // 256)
    def _(j):
        cols = tile(j, 0, 256)
        dinner[:, cols] = dot_nt(normed[...], wout[cols, :])

    m_ref[...] = jnp.zeros_like(m_ref)

    @pl.loop(0, INNER // 128)
    def _(j):
        cols = tile(j)
        gate = proj[:, cols]
        u = y_ref[:, cols] * gate * jax.nn.sigmoid(gate) * q_ref[...]
        du = dinner[:, cols] * u
        small_now[0, 5:6, cols] = col_sum(du)
        m_ref[...] += du * gain[:, cols]

    m_ref[...] = jnp.broadcast_to(row_sum(m_ref[...]) / INNER, (TOK, 128))

    @pl.loop(0, INNER // 128)
    def _(j):
        cols = tile(j)
        y, gate, q = y_ref[:, cols], proj[:, cols], q_ref[...]
        sig = jax.nn.sigmoid(gate)
        silu = gate * sig
        dgated = q * (dinner[:, cols] * gain[:, cols] - y * silu * q * m_ref[...])
        dproj[:, cols] = (dgated * y * sig * (1.0 + gate * (1.0 - sig))).astype(low)
        dinner[:, cols] = dgated * silu

    rs_give(GATE, 0, 1)
    for part in range(3):
        rs_own(OUT, part)
    rs_give(GATE, 1, 0)
    rs_give(GATE, 2, 1)

    def conv_back(dact, j):
        cols = tile(j)
        x = proj[:, tile(j, INNER)]
        dpre = dact * dsilu[:, cols].astype(full)
        small_now[0, 4:5, cols] = col_sum(dpre)
        small_now[0, 3:4, cols] = col_sum(dpre * x)
        dx = taps[3:4, cols] * dpre
        for step in (1, 2, 3):
            moved_up = rolled_up(dpre, step)
            small_now[0, 3 - step : 4 - step, cols] = col_sum(moved_up * x)
            dx = dx + taps[3 - step : 4 - step, cols] * moved_up
        dproj[:, tile(j, INNER)] = dx.astype(low)

    @pl.loop(0, HEADS // 2)
    def _(j):
        for turn, work_now in (
            (2, lambda part: rs_own(GATE, part)),
            (5, lambda part: rs_one(OUT, part)),
            (8, lambda part: rs_one(GATE, part)),
            (10, lambda part: rs_two(OUT, part)),
            (12, lambda part: rs_two(GATE, part)),
            (14, lambda part: rs_three(OUT, part)),
        ):

            @pl.when(j == turn)
            def _(work_now=work_now):
                for part in range(3):
                    work_now(part)

        cols = tile(j)
        cums, wide, values, scaled = pair(j)
        y, dy = y_ref[:, cols], dinner[:, cols]
        dy_low = dy.astype(low)
        small_now[0, 7:8, cols] = col_sum(dy * values)
        own = (jnp.where(left, scaled, jnp.zeros_like(scaled)), jnp.where(left, jnp.zeros_like(scaled), scaled))
        found = []
        for block in range(TOK // 128):
            start, last = block * 128, block * 128 + 128
            both = []
            total = None
            for e in (0, 1):
                dm = dot_nt(own[e][start:last], dy_low[start:])
                pieces, shares = [], []
                for later in range(block, TOK // 128):
                    span = slice(later * 128, later * 128 + 128)
                    gap = cum_t[2 * j + e, :, span] - cums[start:last, e : e + 1]
                    if later == block:
                        gap = jnp.minimum(gap, 0.0)
                    decay = jnp.exp(gap)
                    pieces.append((mix_t[start:last, span] * decay).astype(low))
                    shares.append(dm[:, (later - block) * 128 : (later - block + 1) * 128] * decay)
                both.append(dot(jnp.concatenate(pieces, axis=1), dy_low[start:]))
                share = jnp.concatenate(shares, axis=1)
                total = share if total is None else total + share
            mix[start:last, start:] += total
            found.append(jnp.where(left[:128], both[0], both[1]))
        back = jnp.concatenate(found, axis=0)
        direct = values * back
        crossing = dy_low.astype(full) * (y - skip[:, cols] * values) - scaled.astype(full) * back
        for e in (0, 1):
            mine = left if e == 0 else jnp.logical_not(left)
            spot = lane == 2 * j + e
            dcum_ref[...] = jnp.where(spot, row_sum(jnp.where(mine, crossing, 0.0)), dcum_ref[...])
            dstep_ref[...] = jnp.where(spot, row_sum(jnp.where(mine, direct, 0.0)), dstep_ref[...])
        conv_back(wide * back + skip[:, cols] * dy, j)

    masked = jnp.where(row <= column, mix[...], 0.0)
    conv_back(dot(masked.astype(low), act[:, INNER + STATE :]), INNER // 128)
    conv_back(dot(masked.T.astype(low), act[:, INNER : INNER + STATE]), INNER // 128 + 1)
    dacc = dot((row <= column).astype(full), dcum_ref[...], precision=highest)
    dstep = dstep_ref[...] + dacc * rate
    draw = jnp.where(
        lane < HEADS, dstep * jax.nn.sigmoid(proj[:, INNER + XBC : INNER + XBC + 128] + heads[0:1, :]), 0.0
    )
    dproj[:, INNER + XBC : INNER + XBC + 128] = draw.astype(low)
    dproj[:, INNER + XBC + 128 :] = jnp.zeros((TOK, 128), low)
    small_now[0, 6:7, :] = jnp.zeros((1, XBC), full)
    small_now[0, 6:7, D : D + 128] = col_sum(draw)
    small_now[0, 6:7, D + 128 : D + 256] = rate * col_sum(dacc * step_ref[...])
    small_now[0, 5:6, INNER:] = jnp.zeros((1, XBC - INNER), full)
    small_now[0, 7:8, INNER:] = jnp.zeros((1, XBC - INNER), full)

    rs_give(REST, 0, 0)
    rs_give(REST, 1, 1)
    for part in range(3):
        rs_three(GATE, part)
    rs_give(REST, 2, 0)
    for part in range(3):
        rs_own(REST, part)

    for slot in (0, 1):
        users[slot].wait_send()
    dnormed = y_ref.at[:, pl.ds(0, D)]
    dnormed[...] = jnp.zeros((TOK, D), full)

    def unproject(column, width, weight):
        dnormed[...] += dot_nt(dproj[:, column : column + width], weight)

    streamed([(512 * i, 512) for i in range(9)], unproject)
    m_ref[...] = jnp.zeros_like(m_ref)
    for j in range(D // 128):
        cols = slice(j * 128, j * 128 + 128)
        u = tokens[:, cols].astype(full) * token_scale
        du = dnormed[:, cols] * u
        small_now[0, 6:7, cols] = col_sum(du)
        m_ref[...] += du * norm_gain[:, cols]
    mean = row_sum(m_ref[...]) / D

    small_copies = [[], [], [], []]

    def small_start(stage):
        for step in (1,) if stage == 0 else (1, 2, 3):
            slot = 0 if stage == 0 else stage * 3 - 3 + step
            copy = remote(
                small_now.at[stage],
                small_got.at[slot],
                small_send.at[slot],
                small_recv.at[slot],
                moved(at, "cxyz"[stage], step),
            )
            copy.start()
            small_copies[stage].append((slot, copy))
            drained.append(copy)

    def small_sum(stage):
        value = small_now[stage]
        for slot, copy in small_copies[stage]:
            copy.wait_recv()
            value = value + small_got[slot]
        if stage < 3:
            small_now[stage + 1] = value
            small_start(stage + 1)
        else:
            small_out[...] = value

    small_start(0)
    for part in range(3):
        rs_one(REST, part)
    for j in range(D // 128):
        cols = slice(j * 128, j * 128 + 128)
        u = tokens[:, cols].astype(full) * token_scale
        du = dnormed[:, cols] * norm_gain[:, cols]
        normed[:, cols] = (cotangent[:, cols].astype(full) + token_scale * (du - u * mean)).astype(low)
    final = pltpu.make_async_copy(normed, input_grad, local_sem.at[0])
    final.start()
    small_sum(0)
    for part in range(3):
        rs_two(REST, part)
    small_sum(1)
    for part in range(3):
        rs_three(REST, part)
    last = remote(swap_from, swap_to, swap_sem.at[2], swap_sem.at[3], sibling)
    last.start()
    small_sum(2)
    for copy in drained:
        copy.wait_send()
    for batch in (OUT, GATE, REST):
        for part in range(3):
            for stage in (1, 2, 3):
                for copy in rs_copies(batch, part, stage):
                    copy.wait_send()
    last.wait()
    for base, width in ((0, WIDTH[GATE]), (INNER, WIDTH[REST])):
        lanes = pl.ds(pl.multiple_of(base + (1 - core) * width, 128), width)
        gi_out[:, lanes] = swap_to[:, base // 2 : base // 2 + width]
    final.wait()
    small_sum(3)


def block(wi, wo, tokens, cotangent, live, heads, skip, spots):
    full, low = jnp.float32, jnp.bfloat16
    vmem, anywhere = pl.BlockSpec(memory_space=pltpu.VMEM), pl.BlockSpec(memory_space=pl.ANY)
    sems = pltpu.SemaphoreType.DMA
    return pl.pallas_call(
        block_kernel,
        out_shape=(
            jax.ShapeDtypeStruct((TOK, D), low),
            jax.ShapeDtypeStruct((TOK, D), low),
            jax.ShapeDtypeStruct((8, COLS), full),
            jax.ShapeDtypeStruct((16, D), full),
            jax.ShapeDtypeStruct((8, XBC), full),
            jax.ShapeDtypeStruct((2, 4, 2, 4, 16, COLS), low),
        ),
        in_specs=[vmem] * 8,
        out_specs=[vmem, anywhere] + [vmem] * 3 + [anywhere],
        scratch_shapes=[
            pltpu.VMEM((8, COLS), full),
            pltpu.VMEM((16, XBC), low),
            pltpu.VMEM((2, 4, 2, 4, 2, 16, D), low),
            pltpu.VMEM((2 * CHIPS, 16, 512), low),
            pltpu.VMEM((TOK, COLS - 128), full),
            pltpu.VMEM((TOK, XBC), low),
            pltpu.VMEM((TOK, XBC), low),
            pltpu.VMEM((TOK, INNER), full),
            pltpu.VMEM((TOK, INNER), full),
            pltpu.VMEM((TOK, COLS), low),
            pltpu.VMEM((CHIPS, 2, 16, TOK), low),
            pltpu.VMEM((TOK, D), low),
            pltpu.VMEM((CHIPS, 16, TOK), low),
            pltpu.VMEM((TOK, TOK), full),
            pltpu.VMEM((TOK, TOK), full),
            pltpu.VMEM((TOK, 128), full),
            pltpu.VMEM((HEADS, 1, TOK), full),
            pltpu.VMEM((TOK, 128), full),
            pltpu.VMEM((TOK, 128), full),
            pltpu.VMEM((TOK, 128), full),
            pltpu.VMEM((TOK, 128), full),
            pltpu.VMEM((TOK, 128), full),
            pltpu.VMEM((8, XBC), full),
            pltpu.VMEM((1, INNER), full),
            pltpu.VMEM((1, D), full),
            pltpu.VMEM((CHIPS, 16, SIDE), low),
            pltpu.VMEM((48, 16, SIDE), low),
            pltpu.VMEM((16, 16, SIDE), low),
            pltpu.VMEM((12, 16, SIDE), low),
            pltpu.VMEM((4, 16, SIDE), low),
            pltpu.VMEM((3, 16, SIDE), low),
            pltpu.VMEM((8, XBC), full),
            pltpu.VMEM((8, XBC), full),
            pltpu.VMEM((4, 8, XBC), full),
            pltpu.VMEM((10, 8, XBC), full),
            sems((4,)),
            sems((4,)),
            sems((81,)),
            sems((81,)),
            sems((9,)),
            sems((9,)),
            sems((81,)),
            sems((81,)),
            sems((9,)),
            sems((9,)),
            sems((10,)),
            sems((10,)),
        ],
        compiler_params=pltpu.CompilerParams(collective_id=0, has_side_effects=True, vmem_limit_bytes=63 << 20),
    )(wi, wo, tokens, cotangent, live, heads, skip, spots)


def body(
    tokens,
    lengths,
    placement_ids,
    norm_gain,
    in_weight,
    conv_weight,
    conv_bias,
    dt_bias,
    a_log,
    d_skip,
    inner_gain,
    out_weight,
    cotangent,
):
    full = jnp.float32
    sequence_id = placement_ids[0]
    slot_length = jnp.sum(jnp.where(lax.broadcasted_iota(jnp.int32, lengths.shape, 0) == sequence_id, lengths, 0))
    live = (lax.broadcasted_iota(jnp.int32, (TOK, 128), 0) < slot_length).astype(full)
    shared = jnp.concatenate(
        [norm_gain, inner_gain, conv_bias, conv_weight.reshape(-1), jnp.zeros((14,), jnp.bfloat16)]
    )
    wi = jnp.concatenate(
        [
            in_weight,
            jnp.zeros((8, COLS - 128 - PROJ), jnp.bfloat16),
            jnp.pad(shared[None], ((0, 7), (0, 0))),
        ],
        axis=1,
    ).astype(full)
    heads = jnp.pad(jnp.stack([dt_bias, a_log]), ((0, 6), (0, 128 - HEADS)))
    count = np.arange(XBC, dtype=np.int32)
    spots = jnp.asarray(np.stack([count % 18, count // 18] + [count * 0] * 6))
    block_out, input_grad, shard_in, shard_out, small, _ = block(
        wi, out_weight, tokens, cotangent, live, heads, jnp.repeat(d_skip, HEAD)[None], spots
    )
    me = lax.axis_index("dp") * 16 + lax.axis_index("fsdp")
    conv = lax.dynamic_slice(small, (0, me * 18), (5, 18))
    return (
        block_out,
        input_grad,
        lax.dynamic_slice(small, (6, me * 8), (1, 8))[0],
        shard_in[:, :PROJ],
        conv[:CONV],
        conv[CONV],
        small[6, D : D + HEADS],
        small[6, D + 128 : D + 128 + HEADS],
        jnp.sum(small[7, :INNER].reshape(HEADS, HEAD), axis=1),
        lax.dynamic_slice(small, (5, me * 16), (1, 16))[0],
        shard_out,
    )


def solution(mesh):
    placed = (
        P(("dp", "fsdp"), None),
        P(),
        P(("dp", "fsdp")),
        P(("dp", "fsdp")),
        P(("dp", "fsdp"), None),
        P(None, ("dp", "fsdp")),
        P(("dp", "fsdp")),
        P(),
        P(),
        P(),
        P(("dp", "fsdp")),
        P(("dp", "fsdp"), None),
        P(("dp", "fsdp"), None),
    )
    return jax.shard_map(
        body,
        mesh=mesh,
        in_specs=placed,
        out_specs=(
            P(("dp", "fsdp"), None),
            P(("dp", "fsdp"), None),
            P(("dp", "fsdp")),
            P(("dp", "fsdp"), None),
            P(None, ("dp", "fsdp")),
            P(("dp", "fsdp")),
            P(),
            P(),
            P(),
            P(("dp", "fsdp")),
            P(("dp", "fsdp"), None),
        ),
        check_vma=False,
    )
```

```python
import jax
import jax.numpy as jnp
import numpy as np
from jax import lax
from jax.experimental import pallas as pl
from jax.experimental.pallas import tpu as pltpu
from jax.sharding import PartitionSpec as P

D = 1024
INNER = 2048
STATE = 128
HEAD = 64
CONV = 4
HEADS = 32
XBC = 2304
PROJ = 4384
TOK = 512
CHIPS = 64
COLS = 4608
SIDE = 3328
HALF = 1152
THIRD = 384
MESH = pl.DeviceIdType.MESH
ORDERS = (("x", "y", "z"), ("y", "z", "x"), ("z", "x", "y"))
OUT, GATE, EARLY, LATE = 0, 1, 2, 3
PARTS = {
    OUT: ((0, 512), (512, 256), (768, 256)),
    GATE: ((0, 256), (256, 256), (512, 512)),
    EARLY: ((0, 256), (256, 256), (512, 256)),
    LATE: ((0, 128), (128, 256), (384, 128)),
}
GROUPS = {OUT: ((0,), (1, 2)), GATE: ((0, 1), (2,)), EARLY: ((0, 1), (2,)), LATE: ((0, 1, 2),)}
LOCAL = {OUT: 0, GATE: 1024, EARLY: 2048, LATE: 2816}
BASE = {GATE: 0, EARLY: 2048, LATE: 3584}
WIDTH = {GATE: 1024, EARLY: 768, LATE: 512}
SPLIT = 12
eps = 1e-05
LOG2E = 1.4426950408889634
highest = lax.Precision.HIGHEST

TILES = (3584, 4096, 2048, 2560, 3072, 0, 512, 1024, 1536)
BACK_TILES = (0, 512, 1024, 1536, 2048, 2560, 3072, 3584, 4096)
PLAN = (
    (1, (("dn", 0),)),
    (2, (("own", GATE),)),
    (4, (("dn", 1),)),
    (6, (("one", OUT), ("dn", 2))),
    (8, (("dn", 3),)),
    (10, (("one", GATE),)),
    (12, (("two", OUT),)),
    (13, (("give", EARLY),)),
    (14, (("dn", 4),)),
    (15, (("own", EARLY), ("two", GATE))),
)


def place():
    dp, fsdp = lax.axis_index("dp"), lax.axis_index("fsdp")
    return {"x": (fsdp // 2) % 4, "y": (dp // 4) * 2 + fsdp // 8, "z": dp % 4, "c": fsdp % 2}


def device(at):
    y = at["y"]
    return ((y // 2) * 4 + at["z"], (y % 2) * 8 + at["x"] * 2 + at["c"])


def moved(at, axis, step):
    size = 2 if axis == "c" else 4
    return dict(at, **{axis: lax.rem(at[axis] + step, size)})


def greet(at):
    peers = [moved(at, axis, step) for axis in "xyz" for step in (1, 2, 3)] + [moved(at, "c", 1)]
    for peer in peers:
        pl.semaphore_signal(pltpu.get_barrier_semaphore(), inc=1, device_id=device(peer), device_id_type=MESH)


def meet():
    pl.semaphore_wait(pltpu.get_barrier_semaphore(), 10)


def remote(src, dst, send, recv, peer):
    return pltpu.make_async_remote_copy(
        src_ref=src, dst_ref=dst, send_sem=send, recv_sem=recv, device_id=device(peer), device_id_type=MESH
    )


def chips(at, full):
    every = slice(None)
    y, z, x = at["y"], at["z"], at["x"]
    return (
        every if "y" in full else y // 2,
        every if "z" in full else z,
        every if "y" in full else y % 2,
        every if "x" in full else x,
    )


def rolled_down(x, step):
    zeros = jnp.zeros((8, x.shape[1]), x.dtype)
    return pltpu.roll(jnp.concatenate([zeros, x], axis=0), step, axis=0)[8:]


def rolled_up(x, step):
    rows = x.shape[0]
    zeros = jnp.zeros((8, x.shape[1]), x.dtype)
    return pltpu.roll(jnp.concatenate([x, zeros], axis=0), rows + 8 - step, axis=0)[:rows]


def tile(j, base=0, size=128):
    return pl.ds(pl.multiple_of(base + j * size, 128), size)


def dot_nt(a, b):
    return lax.dot_general(a, b, (((1,), (1,)), ((), ())), preferred_element_type=jnp.float32)


def dot(a, b, **more):
    return jnp.dot(a, b, preferred_element_type=jnp.float32, **more)


def row_sum(x):
    return jnp.sum(x, axis=1, keepdims=True)


def col_sum(x):
    return jnp.sum(x, axis=0, keepdims=True)


def block_kernel(
    lengths,
    ids,
    in_shard_hbm,
    wo_hbm,
    tokens_hbm,
    cotangent_hbm,
    params_hbm,
    block_out_hbm,
    input_grad,
    gi_hbm,
    go_hbm,
    small_hbm,
    norm_hbm,
    full_in,
    in_shard,
    wo,
    tokens,
    cotangent,
    params,
    block_out,
    gi_out,
    go_out,
    small_out,
    norm_out,
    wi,
    other,
    blk,
    live,
    skip,
    full_out,
    work,
    proj,
    act,
    dsilu,
    y_ref,
    dinner,
    dproj,
    inner_t,
    normed,
    normed_t,
    mix,
    mix_t,
    cum_parts,
    key_parts,
    cum_t,
    key_t,
    step_ref,
    q_ref,
    m_ref,
    dcum_ref,
    dstep_ref,
    back_ref,
    taps,
    gain,
    norm_gain,
    part0,
    recv1,
    part1,
    recv2,
    part2,
    recv3,
    swap_from,
    swap_to,
    small_now,
    small_other,
    small_half,
    small_got,
    small_last,
    norm_now,
    norm_got,
    swap_sem,
    local_sem,
    edge_sem,
    ag_send,
    ag_recv,
    ag_pass,
    ag_got,
    rs_send,
    rs_recv,
    rs_pass,
    rs_got,
    small_send,
    small_recv,
    norm_send,
    norm_recv,
):
    low, full = jnp.bfloat16, jnp.float32
    at = place()
    core = at["c"]
    first = core == 0
    sibling = moved(at, "c", 1)
    here = chips(at, ())
    inputs = [
        pltpu.make_async_copy(source, target, edge_sem.at[i])
        for i, (source, target) in enumerate(
            (
                (in_shard_hbm, in_shard),
                (params_hbm, params),
                (tokens_hbm, tokens),
                (wo_hbm, wo),
                (cotangent_hbm, cotangent),
            )
        )
    ]
    for copy in inputs:
        copy.start()
    greet(at)

    lane = lax.broadcasted_iota(jnp.int32, (TOK, 128), 1)
    left = lane < HEAD
    row = lax.broadcasted_iota(jnp.int32, (TOK, TOK), 0)
    column = lax.broadcasted_iota(jnp.int32, (TOK, TOK), 1)
    for copy in inputs:
        copy.wait()
    wi[:, COLS - 256 :] = jnp.zeros((8, 256), full)
    wi[:, :PROJ] = in_shard[...].astype(full)
    wi[:, COLS - 128 :] = params[0:8, :]
    full_out[here + (core,)] = wo[...]
    length = lengths[ids[0]]
    live[...] = (lax.broadcasted_iota(jnp.int32, (TOK, 128), 0) < length).astype(full)
    m_ref[...] = jnp.zeros_like(m_ref)
    for j in range(D // 128):
        x = tokens[:, j * 128 : j * 128 + 128].astype(full)
        m_ref[...] += x * x
    token_scale = lax.rsqrt(row_sum(m_ref[...]) / D + eps)
    owner = lax.broadcasted_iota(jnp.int32, (128, INNER), 1) >> 6
    repeats = (lax.broadcasted_iota(jnp.int32, (128, INNER), 0) == owner).astype(full)
    skip[...] = dot(params[8:16, :], repeats, precision=highest)[2:3]
    heads = params[8:16, :]
    meet()

    swap = remote(wi, other, swap_sem.at[0], swap_sem.at[1], sibling)
    swap.start()

    def held(batch, part, reach):
        start, width = PARTS[batch][part]
        if batch == OUT:
            return full_out.at[chips(at, reach) + (core, slice(None), pl.ds(start, width))]
        spot = pl.multiple_of(core * WIDTH[batch] + start + BASE[batch], 128)
        return full_in.at[chips(at, reach) + (slice(None), pl.ds(spot, width))]

    flying = {}
    drained = []

    def hop(batch, part, phase):
        target = held(batch, part, ORDERS[part][:phase])
        source = target
        if phase == 0 and batch != OUT:
            start, width = PARTS[batch][part]
            source = blk.at[:, pl.ds(BASE[batch] // 2 + start, width)]
        flying[batch, part] = []
        for step in (1, 2, 3):
            slot = ((batch * 3 + part) * 3 + phase) * 3 + step - 1
            copy = remote(source, target, ag_send.at[slot], ag_recv.at[slot], moved(at, ORDERS[part][phase], step))
            copy.start()
            flying[batch, part].append(copy)
            drained.append(copy)

    def landed(batch, part):
        for copy in flying[batch, part]:
            copy.wait_recv()

    given = {}

    def give(batch):
        for part in range(3):
            landed(batch, part)
            region = held(batch, part, "xyz")
            slot = batch * 3 + part
            given[batch, part] = remote(region, region, ag_pass.at[slot], ag_got.at[slot], sibling)
            given[batch, part].start()
            drained.append(given[batch, part])

    def taken(batch):
        for part in range(3):
            given[batch, part].wait_recv()

    swap.wait()
    stores = []

    def begin(batch):
        base, width = BASE[batch], WIDTH[batch]
        lanes = pl.ds(pl.multiple_of(base + core * width, 128), width)
        mine, theirs = wi[:, lanes], other[:, lanes]
        blk[:, base // 2 : base // 2 + width] = jnp.concatenate(
            [jnp.where(first, mine, theirs), jnp.where(first, theirs, mine)], axis=0
        ).astype(low)
        launch(batch, 0)
        copy = pltpu.make_async_copy(
            blk.at[:, pl.ds(base // 2, width)], full_in.at[here + (slice(None), lanes)], local_sem.at[len(stores)]
        )
        copy.start()
        stores.append(copy)

    def launch(batch, phase):
        for part in range(3):
            if phase:
                landed(batch, part)
            hop(batch, part, phase)

    begin(LATE)
    begin(EARLY)
    begin(GATE)
    launch(OUT, 0)
    for copy in stores:
        copy.wait()
    launch(LATE, 1)
    launch(EARLY, 1)
    launch(LATE, 2)
    launch(GATE, 1)
    launch(EARLY, 2)
    launch(OUT, 1)

    def slot_of(slot):
        if slot < 2:
            return work.reshape(4, 4, 2, 4, 16, 512).at[pl.ds(2 * slot, 2)]
        return inner_t.reshape(2, 4, 2, 4, 2, 16, 512).at[:, :, :, :, slot - 2]

    def fetched(slot, start):
        source = full_in.at[:, :, :, :, :, pl.ds(start, 512)]
        return pltpu.make_async_copy(source, slot_of(slot), local_sem.at[3 + slot])

    def fetch(i):
        fetched(i % 4, TILES[i]).start()

    def weight(i):
        slot = i % 4
        fetched(slot, TILES[i]).wait()
        if slot < 2:
            return work[pl.ds(CHIPS * slot, CHIPS)].reshape(D, 512)
        return inner_t[:, slot - 2].reshape(D, 512)

    give(LATE)
    launch(GATE, 2)
    taken(LATE)
    fetch(1)
    fetch(0)
    give(EARLY)
    late = weight(1)
    packed = late[:, 384:]

    def spread(r, base, count, each):
        pick = (
            lax.broadcasted_iota(jnp.int32, (128, D), 0) * 8 + r == lax.broadcasted_iota(jnp.int32, (128, D), 1)
        ).astype(low)
        shared = dot(pick, packed).astype(low)
        line = lax.broadcasted_iota(jnp.int32, (128, count), 0).astype(full)
        spot = lax.broadcasted_iota(jnp.int32, (128, count), 1).astype(full) + base
        owner = jnp.floor((spot + 0.5) * (1.0 / each))
        found = dot(shared, (line == spot - owner * each).astype(low))
        return col_sum(jnp.where(line == owner, found, 0.0))

    norm_gain[...] = spread(0, 0, D, 8)
    for j in range(D // 128):
        cols = slice(j * 128, j * 128 + 128)
        value = (tokens[:, cols].astype(full) * token_scale * norm_gain[:, cols]).astype(low)
        normed[:, cols] = value
        normed_t[j * 8 : j * 8 + 8] = value.T.reshape(8, 16, TOK)

    def project(i, weights):
        width = weights.shape[1]
        proj[:, TILES[i] : TILES[i] + width] = dot(normed[...], weights)

    def convolve(begin, end):
        @pl.loop(begin, end)
        def _(j):
            cols = tile(j)
            x = proj[:, tile(j, INNER)]
            pre = taps[4:5, cols] + taps[3:4, cols] * x
            for step in (1, 2, 3):
                pre = pre + taps[3 - step : 4 - step, cols] * rolled_down(x, step)
            sig = jax.nn.sigmoid(pre)
            act[:, cols] = (pre * sig).astype(low)
            dsilu[:, cols] = (sig * (1.0 + pre * (1.0 - sig))).astype(low)

    project(1, late[:, :384])
    project(0, weight(0))
    taps[...] = jnp.zeros_like(taps)
    for base in (0, XBC // 2):
        for k in range(CONV + 1):
            taps[k : k + 1, base : base + XBC // 2] = spread((3, 4, 5, 6, 2)[k], base, XBC // 2, 18)
    gain[...] = spread(1, 0, INNER, 16)
    taken(EARLY)
    for i in (2, 3, 4):
        fetch(i)
    launch(OUT, 2)
    give(GATE)
    convolve(SPLIT, XBC // 128)

    raw = proj[:, INNER + XBC : INNER + XBC + 128] + heads[0:1, :]
    grown = jnp.exp(-jnp.abs(raw))
    more = 1.0 + grown
    logged = jnp.where(more == 1.0, grown, jnp.log(more) * grown / jnp.where(more == 1.0, 1.0, more - 1.0))
    steps = jnp.where(lane < HEADS, jnp.maximum(raw, 0.0) + logged, 0.0)
    rate = -jnp.exp(heads[1:2, :])

    def split(x):
        top = x.astype(low)
        middle = (x - top.astype(full)).astype(low)
        return top, middle, (x - top.astype(full) - middle.astype(full)).astype(low)

    def summed(mask, x):
        found = dot(jnp.where(mask, 1.0, 0.0).astype(low), jnp.concatenate(split(x), axis=1))
        return found[:, :128] + found[:, 128:256] + found[:, 256:]

    cum = summed(row >= column, steps * rate) * LOG2E
    step_ref[...] = steps
    key = cum - jnp.log2(jnp.maximum(steps, 1e-37))
    turned, key_turned = cum.T, key.T
    for head in range(HEADS):
        cum_t[head] = turned[head : head + 1]
        key_t[head] = key_turned[head : head + 1]

    def thirds(x):
        top, middle, rest = [part.astype(full) for part in split(jnp.where(lane < HEADS, x, 0.0))]
        return (top + pltpu.roll(middle, HEADS, axis=1) + pltpu.roll(rest, 2 * HEADS, axis=1)).astype(low)

    cum_parts[...] = thirds(cum)
    key_parts[...] = thirds(key)
    mixed = jnp.where(row >= column, dot_nt(act[:, INNER + STATE :], act[:, INNER : INNER + STATE]), 0.0)
    mix[...] = mixed
    mix_t[...] = mixed.T

    for i in (2, 3, 4):
        project(i, weight(i))
    taken(GATE)
    for i in (5, 6, 7, 8):
        fetch(i)
    convolve(0, SPLIT)
    for i in (5, 6, 7, 8):
        project(i, weight(i))
    give(OUT)
    q_ref[...] = jnp.zeros_like(q_ref)
    dcum_ref[...] = jnp.zeros_like(dcum_ref)
    dstep_ref[...] = jnp.zeros_like(dstep_ref)

    causal = lax.broadcasted_iota(jnp.int32, (128, 128), 0) >= lax.broadcasted_iota(jnp.int32, (128, 128), 1)

    anti = lax.broadcasted_iota(jnp.int32, (128, 128), 0) <= lax.broadcasted_iota(jnp.int32, (128, 128), 1)

    def spread_heads(parts, j):
        line = lax.broadcasted_iota(jnp.int32, (128, 256), 0)
        head = 2 * j + (lax.broadcasted_iota(jnp.int32, (128, 256), 1) >> 7)
        return dot(parts[...], jnp.where(((line & 31) == head) & (line < 96), 1.0, 0.0).astype(low))

    @pl.loop(0, HEADS // 2)
    def _(j):
        cols = tile(j)
        cums = spread_heads(cum_parts, j)
        values = act[:, cols]
        for block in range(TOK // 128):
            start, last = block * 128, block * 128 + 128
            halves = []
            for e in (0, 1):
                pieces = []
                for past in range(block + 1):
                    span = slice(past * 128, past * 128 + 128)
                    gap = cums[start:last, e * 128 : e * 128 + 128] - key_t[2 * j + e, :, span]
                    if past == block:
                        gap = jnp.where(causal, gap, -1e30)
                    pieces.append((mix[start:last, span] * jnp.exp2(gap)).astype(low))
                halves.append(jnp.concatenate(pieces, axis=1))
            found = dot(jnp.concatenate(halves, axis=0), values[:last])
            y = jnp.where(left[:128], found[:128], found[128:]) + skip[:, cols] * values[start:last].astype(full)
            y_ref[start:last, cols] = y
            gate = proj[start:last, cols]
            gated = y * gate * jax.nn.sigmoid(gate)
            q_ref[start:last] += gated * gated

    q_ref[...] = jnp.broadcast_to(lax.rsqrt(row_sum(q_ref[...]) / INNER + eps), (TOK, 128))
    mix[...] = jnp.zeros_like(mix)

    @pl.loop(0, INNER // 128)
    def _(j):
        cols = tile(j)
        gate = proj[:, cols]
        gated = y_ref[:, cols] * gate * jax.nn.sigmoid(gate)
        value = (gated * q_ref[...] * gain[:, cols]).astype(low)
        dproj[:, cols] = value
        inner_t[pl.ds(4 * j, 4)] = value.T.reshape(4, 2, 16, TOK)

    for j in range(D // 128):
        cols = slice(j * 128, j * 128 + 128)
        normed[:, cols] = (live[...] * cotangent[:, cols].astype(full)).astype(low)

    def grads(batch, group, side, half):
        start = PARTS[batch][group[0]][0]
        width = sum(PARTS[batch][part][1] for part in group)
        if batch == OUT:
            lhs = inner_t[pl.ds(32 * half, 32), side].reshape(TOK, TOK)
            rhs = normed[:, start : start + width]
        else:
            lhs = normed_t[pl.ds(32 * half, 32)].reshape(TOK, TOK)
            rhs = dproj[:, pl.ds(pl.multiple_of(BASE[batch] + start + side * WIDTH[batch], 128), width)]
        value = dot(lhs, rhs)
        return [(part, PARTS[batch][part][0] - start, PARTS[batch][part][1], value) for part in group]

    def spot_of(part, half, m):
        spot = {"y": 2 * half + (m // 4) % 2, "z": m // 8, "x": m % 4}
        axes = ORDERS[part]
        return spot[axes[2]] * 16 + spot[axes[1]] * 4 + spot[axes[0]]

    users = [[], []]

    def rs_free():
        for gone in users:
            while gone:
                rs_pass_copy(*gone.pop()).wait_send()

    def rs_give(batch):
        for slot, group in enumerate(GROUPS[batch]):
            while users[slot]:
                rs_pass_copy(*users[slot].pop()).wait_send()
            for half in (0, 1):
                for part, offset, width, value in grads(batch, group, 1 - core, half):
                    value = value[:, offset : offset + width].astype(low)
                    for m in range(32):
                        work[CHIPS * slot + spot_of(part, half, m), :, offset : offset + width] = value[
                            16 * m : 16 * m + 16
                        ]
            for part in group:
                offset = PARTS[batch][part][0] - PARTS[batch][group[0]][0]
                users[slot].append((batch, part, slot, offset))
                rs_pass_copy(batch, part, slot, offset).start()

    def rs_pass_copy(batch, part, slot=0, offset=0):
        width = PARTS[batch][part][1]
        sem = batch * 3 + part
        return remote(
            work.at[pl.ds(CHIPS * slot, CHIPS), :, pl.ds(offset, width)],
            part0.at[:, :, lanes_of(batch, part)],
            rs_pass.at[sem],
            rs_got.at[sem],
            sibling,
        )

    def lanes_of(batch, part):
        start, width = PARTS[batch][part]
        return pl.ds(LOCAL[batch] + start, width)

    def rs_copies(batch, part, stage):
        lanes = lanes_of(batch, part)
        axis = ORDERS[part][3 - stage]
        copies = []
        for step in (1, 2, 3):
            peer = moved(at, axis, step)
            there, slot = peer[axis], pl.ds(step - 1, 1)
            if stage == 1:
                source, target = part0.at[pl.ds(there * 16, 16), :, lanes], recv1.at[pl.ds(16 * step - 16, 16), :, lanes]
            elif stage == 2:
                source, target = part1.at[pl.ds(there * 4, 4), :, lanes], recv2.at[pl.ds(4 * step - 4, 4), :, lanes]
            else:
                source, target = part2.at[pl.ds(there, 1), :, lanes], recv3.at[slot, :, lanes]
            sem = ((batch * 3 + part) * 3 + stage - 1) * 3 + step - 1
            copies.append(remote(source, target, rs_send.at[sem], rs_recv.at[sem], peer))
        return copies

    def rs_hop(batch, part, stage):
        for copy in rs_copies(batch, part, stage):
            copy.start()

    def rs_landed(batch, part, stage):
        for copy in rs_copies(batch, part, stage):
            copy.wait_recv()

    def rs_own(batch):
        for group in GROUPS[batch]:
            for part in group:
                rs_pass_copy(batch, part).wait_recv()
            for half in (0, 1):
                for part, offset, width, value in grads(batch, group, core, half):
                    lanes = lanes_of(batch, part)
                    for m in range(32):
                        now = pl.ds(spot_of(part, half, m), 1)
                        piece = value[16 * m : 16 * m + 16, offset : offset + width][None]
                        part0[now, :, lanes] = (piece + part0[now, :, lanes].astype(full)).astype(low)
            for part in group:
                rs_hop(batch, part, 1)

    def rs_one(batch, part):
        lanes = lanes_of(batch, part)
        rs_landed(batch, part, 1)
        mine = at[ORDERS[part][2]] * 16
        for i in range(16):
            now = pl.ds(i, 1)
            value = part0[pl.ds(mine + i, 1), :, lanes].astype(full)
            for k in range(3):
                value = value + recv1[pl.ds(16 * k + i, 1), :, lanes].astype(full)
            part1[now, :, lanes] = value.astype(low)
        rs_hop(batch, part, 2)

    def rs_two(batch, part):
        lanes = lanes_of(batch, part)
        rs_landed(batch, part, 2)
        mine = at[ORDERS[part][1]] * 4
        for i in range(4):
            now = pl.ds(i, 1)
            value = part1[pl.ds(mine + i, 1), :, lanes].astype(full)
            for k in range(3):
                value = value + recv2[pl.ds(4 * k + i, 1), :, lanes].astype(full)
            part2[now, :, lanes] = value.astype(low)
        rs_hop(batch, part, 3)

    def rs_three(batch, part):
        lanes = lanes_of(batch, part)
        rs_landed(batch, part, 3)
        value = part2[pl.ds(at[ORDERS[part][0]], 1), :, lanes].astype(full)
        for k in range(3):
            value = value + recv3[pl.ds(k, 1), :, lanes].astype(full)
        value = value[0]
        start, width = PARTS[batch][part]
        if batch == OUT:
            go_out[:, start : start + width] = value
            return
        base = BASE[batch]
        at_column = pl.multiple_of(base + core * WIDTH[batch] + start, 128)
        gi_out[:, pl.ds(at_column, width)] = jnp.where(first, value[:8], value[8:])
        swap_from[:, pl.ds(base // 2 + start, width)] = jnp.where(first, value[8:], value[:8])

    rs_give(OUT)
    taken(OUT)
    while drained:
        drained.pop().wait_send()
    wout = full_out.reshape(INNER, D)
    wide_live = jnp.concatenate([live[...], live[...]], axis=1)

    m_ref[...] = jnp.zeros_like(m_ref)

    @pl.loop(0, D // 256)
    def _(j):
        cols = tile(j, 0, 256)
        branch = dot(dproj[:, :INNER], wout[:, cols])
        block_out[:, cols] = (tokens[:, cols].astype(full) + wide_live * branch).astype(low)
        shares = normed[:, cols].astype(full) * branch
        m_ref[...] += shares[:, :128] + shares[:, 128:]

    outputs = [pltpu.make_async_copy(block_out, block_out_hbm, edge_sem.at[5])]
    outputs[0].start()

    m_ref[...] = jnp.broadcast_to(row_sum(m_ref[...]) / INNER, (TOK, 128))

    @pl.loop(0, INNER // 256)
    def _(j):
        wide = tile(j, 0, 256)
        sums = [jnp.zeros((1, 128), full)] * 2
        for rows in (slice(0, 256), slice(256, 512)):
            value = dot_nt(normed[rows, :], wout[wide, :])
            for half in (0, 1):
                cols = tile(2 * j + half)
                inside = value[:, half * 128 : half * 128 + 128]
                y, gate, q = y_ref[rows, cols], proj[rows, cols], q_ref[rows, :]
                sig = jax.nn.sigmoid(gate)
                silu = gate * sig
                u = y * silu * q
                sums[half] = sums[half] + col_sum(inside * u)
                dgated = q * (inside * gain[:, cols] - u * m_ref[rows, :])
                dproj[rows, cols] = (dgated * y * (sig + silu * (1.0 - sig))).astype(low)
                dinner[rows, cols] = dgated * silu
        for half in (0, 1):
            small_now[5:6, tile(2 * j + half)] = sums[half]

    rs_own(OUT)

    rs_give(GATE)

    dnormed = proj.at[:, pl.ds(0, D)]

    def back_load(i):
        fetched(2 + i % 2, BACK_TILES[i]).start()

    def back_tile(i):
        start = BACK_TILES[i]
        fetched(2 + i % 2, start).wait()
        value = dot_nt(dproj[:, start : start + 512], inner_t[:, i % 2].reshape(D, 512))
        dnormed[...] = value if i == 0 else dnormed[...] + value
        if i + 2 < len(BACK_TILES):
            back_load(i + 2)

    back_load(0)
    back_load(1)

    def conv_back(dact, j):
        cols = tile(j)
        x = proj[:, tile(j, INNER)]
        dpre = dact * dsilu[:, cols].astype(full)
        small_now[4:5, cols] = col_sum(dpre)
        small_now[3:4, cols] = col_sum(dpre * x)
        dx = taps[3:4, cols] * dpre
        for step in (1, 2, 3):
            moved_up = rolled_up(dpre, step)
            small_now[3 - step : 4 - step, cols] = col_sum(moved_up * x)
            dx = dx + taps[3 - step : 4 - step, cols] * moved_up
        dproj[:, tile(j, INNER)] = dx.astype(low)

    back_ref[...] = jnp.zeros_like(back_ref)

    def settle(j):
        cols = tile(j)
        values, dy, back = act[:, cols].astype(full), dinner[:, cols], back_ref[...]
        direct = values * back
        crossing = dy.astype(low).astype(full) * (y_ref[:, cols] - skip[:, cols] * values) - direct
        small_now[7:8, cols] = col_sum(dy * values)
        for e in (0, 1):
            mine = left if e == 0 else jnp.logical_not(left)
            spot = lane == 2 * j + e
            dcum_ref[...] = jnp.where(spot, row_sum(jnp.where(mine, crossing, 0.0)), dcum_ref[...])
            dstep_ref[...] = jnp.where(spot, row_sum(jnp.where(mine, direct, 0.0)), dstep_ref[...])
        conv_back(back + skip[:, cols] * dy, j)

    @pl.loop(0, HEADS // 2)
    def _(j):
        for turn, events in PLAN:

            @pl.when(j == turn)
            def _(events=events):
                for action, what in events:
                    if action == "dn":
                        back_tile(what)
                    elif action in ("give", "own"):
                        {"give": rs_give, "own": rs_own}[action](what)
                    else:
                        for part in range(3):
                            {"one": rs_one, "two": rs_two, "three": rs_three}[action](what, part)

        settle(jnp.maximum(j - 1, 0))
        cols = tile(j)
        keys = spread_heads(key_parts, j)
        v_low = act[:, cols]
        dy_low = dinner[:, cols].astype(low)
        own = (jnp.where(left, v_low, jnp.zeros_like(v_low)), jnp.where(left, jnp.zeros_like(v_low), v_low))
        found = []
        for block in range(TOK // 128):
            start, last = block * 128, block * 128 + 128
            both = dot_nt(jnp.concatenate([own[0][start:last], own[1][start:last]], axis=0), dy_low[start:])
            halves = []
            total = None
            for e in (0, 1):
                pieces, shares = [], []
                for later in range(block, TOK // 128):
                    span = slice(later * 128, later * 128 + 128)
                    gap = cum_t[2 * j + e, :, span] - keys[start:last, e * 128 : e * 128 + 128]
                    if later == block:
                        gap = jnp.where(anti, gap, -1e30)
                    decay = jnp.exp2(gap)
                    pieces.append((mix_t[start:last, span] * decay).astype(low))
                    inside = slice((later - block) * 128, (later - block + 1) * 128)
                    shares.append(both[e * 128 : e * 128 + 128, inside] * decay)
                halves.append(jnp.concatenate(pieces, axis=1))
                share = jnp.concatenate(shares, axis=1)
                total = share if total is None else total + share
            mix[start:last, start:] += total
            given_back = dot(jnp.concatenate(halves, axis=0), dy_low[start:])
            found.append(jnp.where(left[:128], given_back[:128], given_back[128:]))
        for block, value in enumerate(found):
            back_ref[block * 128 : block * 128 + 128] = value

    settle(HEADS // 2 - 1)
    masked = jnp.where(row <= column, mix[...], 0.0)
    conv_back(dot(masked.astype(low), act[:, INNER + STATE :]), INNER // 128)
    conv_back(dot(masked.T.astype(low), act[:, INNER : INNER + STATE]), INNER // 128 + 1)
    dacc = summed(row <= column, dcum_ref[...])
    sig = jax.nn.sigmoid(proj[:, INNER + XBC : INNER + XBC + 128] + heads[0:1, :])
    steps = step_ref[...]
    ratio = jnp.where(steps > 1e-30, sig / jnp.maximum(steps, 1e-30), 1.0)
    draw = jnp.where(lane < HEADS, dstep_ref[...] * ratio + dacc * rate * sig, 0.0)
    dproj[:, INNER + XBC : INNER + XBC + 128] = draw.astype(low)
    dproj[:, INNER + XBC + 128 :] = jnp.zeros((TOK, 128), low)
    small_now[6:7, :] = jnp.zeros((1, XBC), full)
    small_now[6:7, :128] = col_sum(draw)
    small_now[6:7, 128:256] = rate * col_sum(dacc * steps)
    small_now[5:6, INNER:] = jnp.zeros((1, XBC - INNER), full)
    small_now[7:8, INNER:] = jnp.zeros((1, XBC - INNER), full)


    def small_swap():
        away = pl.ds(pl.multiple_of((1 - core) * HALF, 128), HALF)
        return remote(small_now.at[:, away], small_other, small_send.at[0], small_recv.at[0], sibling)

    def small_copies(stage):
        made = []
        for part in range(3):
            lanes = pl.ds(part * THIRD, THIRD)
            axis = ORDERS[part][stage - 1]
            for step in (1, 2, 3):
                slot = (stage - 1) * 3 + step - 1
                sem = slot * 3 + part + 1
                made.append(
                    remote(
                        small_half.at[stage - 1, :, lanes],
                        small_got.at[slot, :, lanes],
                        small_send.at[sem],
                        small_recv.at[sem],
                        moved(at, axis, step),
                    )
                )
        return made

    def small_back():
        return remote(small_half.at[3], small_last, small_send.at[28], small_recv.at[28], sibling)

    def small_add(stage):
        if stage == 0:
            small_swap().wait_recv()
            mine = pl.ds(pl.multiple_of(core * HALF, 128), HALF)
            small_half[0] = small_now[:, mine] + small_other[...]
        else:
            for copy in small_copies(stage):
                copy.wait_recv()
            value = small_half[stage - 1]
            for k in range(3):
                value = value + small_got[(stage - 1) * 3 + k]
            small_half[stage] = value
        for copy in small_copies(stage + 1) if stage < 3 else [small_back()]:
            copy.start()
            drained.append(copy)

    def norm_copies(stage):
        made = []
        for step in (1,) if stage == 0 else (1, 2, 3):
            slot = 0 if stage == 0 else stage * 3 - 3 + step
            peer = moved(at, "cxyz"[stage], step)
            made.append(remote(norm_now.at[stage], norm_got.at[slot], norm_send.at[slot], norm_recv.at[slot], peer))
        return made

    def norm_start(stage):
        for copy in norm_copies(stage):
            copy.start()
            drained.append(copy)

    def norm_add(stage):
        value = norm_now[stage]
        for k, copy in enumerate(norm_copies(stage)):
            copy.wait_recv()
            value = value + norm_got[0 if stage == 0 else stage * 3 - 2 + k]
        if stage == 3:
            norm_out[...] = value
        else:
            norm_now[stage + 1] = value
            norm_start(stage + 1)

    def drain():
        while drained:
            drained.pop().wait_send()

    small_swap().start()
    drained.append(small_swap())
    rs_give(LATE)
    back_tile(5)
    small_add(0)
    back_tile(6)
    rs_own(LATE)
    back_tile(7)
    small_add(1)
    back_tile(8)
    m_ref[...] = jnp.zeros_like(m_ref)
    for j in range(D // 128):
        cols = slice(j * 128, j * 128 + 128)
        u = tokens[:, cols].astype(full) * token_scale
        du = dnormed[:, cols] * u
        norm_now[0, j : j + 1, :] = col_sum(du)
        m_ref[...] += du * norm_gain[:, cols]
    mean = row_sum(m_ref[...]) / D
    norm_start(0)
    for part in range(3):
        rs_one(EARLY, part)
    for j in range(D // 128):
        cols = slice(j * 128, j * 128 + 128)
        u = tokens[:, cols].astype(full) * token_scale
        du = dnormed[:, cols] * norm_gain[:, cols]
        normed[:, cols] = (cotangent[:, cols].astype(full) + token_scale * (du - u * mean)).astype(low)
    final = pltpu.make_async_copy(normed, input_grad, local_sem.at[0])
    final.start()
    norm_add(0)
    for part in range(3):
        rs_three(OUT, part)
    for part in range(3):
        rs_three(GATE, part)
    for batch in (OUT, GATE):
        for part in range(3):
            for stage in (1, 2, 3):
                for copy in rs_copies(batch, part, stage):
                    copy.wait_send()
    small_add(2)
    norm_add(1)
    for part in range(3):
        rs_one(LATE, part)
    for part in range(3):
        rs_two(EARLY, part)
    small_add(3)
    norm_add(2)
    for part in range(3):
        rs_two(LATE, part)
    for part in range(3):
        rs_three(EARLY, part)
    small_back().wait_recv()
    mine = pl.ds(pl.multiple_of(core * HALF, 128), HALF)
    small_out[:, mine] = small_half[3]
    small_out[:, pl.ds(pl.multiple_of((1 - core) * HALF, 128), HALF)] = small_last[...]
    outputs.append(pltpu.make_async_copy(small_out, small_hbm, edge_sem.at[6]))
    outputs.append(pltpu.make_async_copy(go_out, go_hbm, edge_sem.at[7]))
    for copy in outputs[1:]:
        copy.start()
    rs_free()
    norm_add(3)
    outputs.append(pltpu.make_async_copy(norm_out, norm_hbm, edge_sem.at[8]))
    outputs[3].start()
    drain()
    for part in range(3):
        rs_three(LATE, part)
    last = remote(swap_from, swap_to, swap_sem.at[2], swap_sem.at[3], sibling)
    last.start()
    for batch in (EARLY, LATE):
        for part in range(3):
            for stage in (1, 2, 3):
                for copy in rs_copies(batch, part, stage):
                    copy.wait_send()
    final.wait()
    last.wait()
    for batch in (GATE, EARLY, LATE):
        base, width = BASE[batch], WIDTH[batch]
        lanes = pl.ds(pl.multiple_of(base + (1 - core) * width, 128), width)
        gi_out[:, lanes] = swap_to[:, base // 2 : base // 2 + width]
    outputs.append(pltpu.make_async_copy(gi_out, gi_hbm, edge_sem.at[9]))
    outputs[4].start()
    for copy in outputs:
        copy.wait()


def block(lengths, ids, in_shard, wo, tokens, cotangent, params):
    full, low = jnp.float32, jnp.bfloat16
    anywhere = pl.BlockSpec(memory_space=pl.ANY)
    sems = pltpu.SemaphoreType.DMA
    return pl.pallas_call(
        block_kernel,
        out_shape=(
            jax.ShapeDtypeStruct((TOK, D), low),
            jax.ShapeDtypeStruct((TOK, D), low),
            jax.ShapeDtypeStruct((8, COLS), full),
            jax.ShapeDtypeStruct((16, D), full),
            jax.ShapeDtypeStruct((8, XBC), full),
            jax.ShapeDtypeStruct((8, 128), full),
            jax.ShapeDtypeStruct((2, 4, 2, 4, 16, COLS), low),
        ),
        in_specs=[pl.BlockSpec(memory_space=pltpu.SMEM)] * 2 + [anywhere] * 5,
        out_specs=[anywhere] * 7,
        scratch_shapes=[
            pltpu.VMEM((8, PROJ), low),
            pltpu.VMEM((16, D), low),
            pltpu.VMEM((TOK, D), low),
            pltpu.VMEM((TOK, D), low),
            pltpu.VMEM((16, 128), full),
            pltpu.VMEM((TOK, D), low),
            pltpu.VMEM((8, COLS), full),
            pltpu.VMEM((16, D), full),
            pltpu.VMEM((8, XBC), full),
            pltpu.VMEM((8, 128), full),
            pltpu.VMEM((8, COLS), full),
            pltpu.VMEM((8, COLS), full),
            pltpu.VMEM((16, XBC), low),
            pltpu.VMEM((TOK, 128), full),
            pltpu.VMEM((1, INNER), full),
            pltpu.VMEM((2, 4, 2, 4, 2, 16, D), low),
            pltpu.VMEM((2 * CHIPS, 16, 512), low),
            pltpu.VMEM((TOK, COLS - 128), full),
            pltpu.VMEM((TOK, XBC), low),
            pltpu.VMEM((TOK, XBC), low),
            pltpu.VMEM((TOK, INNER), full),
            pltpu.VMEM((TOK, INNER), full),
            pltpu.VMEM((TOK, COLS), low),
            pltpu.VMEM((CHIPS, 2, 16, TOK), low),
            pltpu.VMEM((TOK, D), low),
            pltpu.VMEM((CHIPS, 16, TOK), low),
            pltpu.VMEM((TOK, TOK), full),
            pltpu.VMEM((TOK, TOK), full),
            pltpu.VMEM((TOK, 128), low),
            pltpu.VMEM((TOK, 128), low),
            pltpu.VMEM((HEADS, 1, TOK), full),
            pltpu.VMEM((HEADS, 1, TOK), full),
            pltpu.VMEM((TOK, 128), full),
            pltpu.VMEM((TOK, 128), full),
            pltpu.VMEM((TOK, 128), full),
            pltpu.VMEM((TOK, 128), full),
            pltpu.VMEM((TOK, 128), full),
            pltpu.VMEM((TOK, 128), full),
            pltpu.VMEM((8, XBC), full),
            pltpu.VMEM((1, INNER), full),
            pltpu.VMEM((1, D), full),
            pltpu.VMEM((CHIPS, 16, SIDE), low),
            pltpu.VMEM((48, 16, SIDE), low),
            pltpu.VMEM((16, 16, SIDE), low),
            pltpu.VMEM((12, 16, SIDE), low),
            pltpu.VMEM((4, 16, SIDE), low),
            pltpu.VMEM((3, 16, SIDE), low),
            pltpu.VMEM((8, XBC), full),
            pltpu.VMEM((8, XBC), full),
            pltpu.VMEM((8, XBC), full),
            pltpu.VMEM((8, HALF), full),
            pltpu.VMEM((4, 8, HALF), full),
            pltpu.VMEM((9, 8, HALF), full),
            pltpu.VMEM((8, HALF), full),
            pltpu.VMEM((4, 8, 128), full),
            pltpu.VMEM((10, 8, 128), full),
            sems((4,)),
            sems((7,)),
            sems((10,)),
            sems((108,)),
            sems((108,)),
            sems((12,)),
            sems((12,)),
            sems((108,)),
            sems((108,)),
            sems((12,)),
            sems((12,)),
            sems((29,)),
            sems((29,)),
            sems((10,)),
            sems((10,)),
        ],
        compiler_params=pltpu.CompilerParams(collective_id=0, has_side_effects=True, vmem_limit_bytes=63 << 20),
    )(lengths, ids, in_shard, wo, tokens, cotangent, params)


def finish_kernel(
    out_in,
    grad_in,
    gi_in,
    go_in,
    small_in,
    norm_in,
    out_hbm,
    grad_hbm,
    gain_hbm,
    gi_hbm,
    conv_hbm,
    bias_hbm,
    dt_hbm,
    log_hbm,
    skip_hbm,
    inner_hbm,
    go_hbm,
    small,
    norm,
    gi,
    go,
    out,
    grad,
    gain_out,
    gi_out,
    conv_out,
    bias_out,
    dt_out,
    log_out,
    skip_out,
    inner_out,
    sem,
):
    pairs = ((small_in, small), (norm_in, norm), (gi_in, gi), (go_in, go), (out_in, out), (grad_in, grad))
    copies = [pltpu.make_async_copy(source, target, sem.at[i]) for i, (source, target) in enumerate(pairs)]
    for copy in copies:
        copy.start()
    writes = []

    def write(source, target):
        writes.append(pltpu.make_async_copy(source, target, sem.at[len(copies) + len(writes)]))
        writes[-1].start()

    me = lax.axis_index("dp") * 16 + lax.axis_index("fsdp")
    copies[0].wait()

    def from_lane(count):
        return pltpu.roll(small[...], lax.rem(XBC - count * me, XBC), axis=1)

    conv = from_lane(18)
    conv_out[...] = conv[:CONV, :18]
    write(conv_out, conv_hbm)
    bias_out[...] = conv[CONV : CONV + 1, :18]
    write(bias_out, bias_hbm)
    inner_out[...] = from_lane(16)[5:6, :16]
    write(inner_out, inner_hbm)
    dt_out[...] = small[6:7, :HEADS]
    write(dt_out, dt_hbm)
    log_out[...] = small[6:7, 128 : 128 + HEADS]
    write(log_out, log_hbm)
    copies[4].wait()
    write(out, out_hbm)
    copies[5].wait()
    write(grad, grad_hbm)
    copies[2].wait()
    gi_out[...] = gi[:, :PROJ]
    write(gi_out, gi_hbm)
    copies[3].wait()
    write(go, go_hbm)
    owner = lax.broadcasted_iota(jnp.int32, (INNER, 128), 0) >> 6
    sums = (owner == lax.broadcasted_iota(jnp.int32, (INNER, 128), 1)).astype(jnp.float32)
    skip_out[...] = dot(small[:, :INNER], sums, precision=highest)[7:8, :HEADS]
    write(skip_out, skip_hbm)
    copies[1].wait()
    line = lax.broadcasted_iota(jnp.int32, (8, 128), 0)
    row = jnp.sum(jnp.where(line == me // 16, norm[...], 0.0), axis=0, keepdims=True)
    gain_out[...] = pltpu.roll(row, lax.rem(128 - 8 * lax.rem(me, 16), 128), axis=1)[:, :8]
    write(gain_out, gain_hbm)
    for copy in writes:
        copy.wait()


def finish(out, grad, gi, go, small, norm):
    full = jnp.float32
    anywhere = pl.BlockSpec(memory_space=pl.ANY)
    rest = [(CONV, 18), (1, 18), (1, HEADS), (1, HEADS), (1, HEADS), (1, 16)]
    shapes = [(1, 8), (8, PROJ)] + rest
    return pl.pallas_call(
        finish_kernel,
        out_shape=[jax.ShapeDtypeStruct(out.shape, out.dtype)] * 2
        + [jax.ShapeDtypeStruct(shape, full) for shape in shapes + [(16, D)]],
        in_specs=[anywhere] * 6,
        out_specs=[anywhere] * 11,
        scratch_shapes=[
            pltpu.VMEM(small.shape, full),
            pltpu.VMEM(norm.shape, full),
            pltpu.VMEM(gi.shape, full),
            pltpu.VMEM(go.shape, full),
            pltpu.VMEM(out.shape, out.dtype),
            pltpu.VMEM(out.shape, out.dtype),
        ]
        + [pltpu.VMEM(shape, full) for shape in shapes]
        + [pltpu.SemaphoreType.DMA((17,))],
        compiler_params=pltpu.CompilerParams(vmem_limit_bytes=62 << 20),
    )(out, grad, gi, go, small, norm)


def body(
    tokens,
    lengths,
    placement_ids,
    norm_gain,
    in_weight,
    conv_weight,
    conv_bias,
    dt_bias,
    a_log,
    d_skip,
    inner_gain,
    out_weight,
    cotangent,
):
    full = jnp.float32

    def line(values, first):
        values = values.astype(full).reshape(-1, values.shape[-1])
        rows, lanes = values.shape
        return jnp.pad(values, ((first, 16 - first - rows), (0, 128 - lanes)))

    params = (
        line(norm_gain, 0)
        + line(inner_gain, 1)
        + line(conv_bias, 2)
        + line(conv_weight, 3)
        + line(dt_bias, 8)
        + line(a_log, 9)
        + line(d_skip, 10)
    )
    block_out, input_grad, shard_in, shard_out, small, norm, _ = block(
        lengths, placement_ids, in_weight, out_weight, tokens, cotangent, params
    )
    found = finish(block_out, input_grad, shard_in, shard_out, small, norm)
    flat = [0, 0, 1, 0, 0, 1, 1, 1, 1, 1, 0]
    return tuple(value[0] if one else value for value, one in zip(found, flat))


def solution(mesh):
    placed = (
        P(("dp", "fsdp"), None),
        P(),
        P(("dp", "fsdp")),
        P(("dp", "fsdp")),
        P(("dp", "fsdp"), None),
        P(None, ("dp", "fsdp")),
        P(("dp", "fsdp")),
        P(),
        P(),
        P(),
        P(("dp", "fsdp")),
        P(("dp", "fsdp"), None),
        P(("dp", "fsdp"), None),
    )
    return jax.shard_map(
        body,
        mesh=mesh,
        in_specs=placed,
        out_specs=(
            P(("dp", "fsdp"), None),
            P(("dp", "fsdp"), None),
            P(("dp", "fsdp")),
            P(("dp", "fsdp"), None),
            P(None, ("dp", "fsdp")),
            P(("dp", "fsdp")),
            P(),
            P(),
            P(),
            P(("dp", "fsdp")),
            P(("dp", "fsdp"), None),
        ),
        check_vma=False,
    )
```

```python
import jax
import jax.numpy as jnp
import numpy as np
from jax import lax
from jax.experimental import pallas as pl
from jax.experimental.pallas import tpu as pltpu
from jax.sharding import PartitionSpec as P

D = 1024
INNER = 2048
STATE = 128
HEAD = 64
CONV = 4
HEADS = 32
XBC = 2304
PROJ = 4384
TOK = 512
CHIPS = 64
COLS = 4608
SIDE = 3328
HALF = 1152
THIRD = 384
MESH = pl.DeviceIdType.MESH
ORDERS = (("x", "y", "z"), ("y", "z", "x"), ("z", "x", "y"))
OUT, GATE, EARLY, MID, LATE = 0, 1, 2, 3, 4
GET_PARTS = {
    OUT: ((0, 384), (384, 384), (768, 256)),
    GATE: ((0, 384), (384, 384), (768, 256)),
    EARLY: ((0, 256), (256, 256), (512, 384)),
    LATE: ((0, 128), (128, 128), (256, 128)),
}
GET_BASE = {GATE: 0, EARLY: 2048, LATE: 3840}
GET_WIDTH = {OUT: 1024, GATE: 1024, EARLY: 896, LATE: 384}
SPLIT = 14
TILES = (
    (3840, 512),
    (4352, 256),
    (2048, 512),
    (2560, 512),
    (3072, 512),
    (3584, 256),
    (0, 512),
    (512, 512),
    (1024, 512),
    (1536, 512),
)
PARTS = {
    OUT: ((0, 512), (512, 256), (768, 256)),
    GATE: ((0, 256), (512, 512), (256, 256)),
    EARLY: ((0, 128), (128, 128), (256, 256)),
    MID: ((0, 128), (128, 128), (256, 128)),
    LATE: ((0, 128), (128, 128), (256, 128)),
}
GROUPS = {
    OUT: (((0,), 0), ((1, 2), 1)),
    GATE: (((0, 2), 0), ((1,), 1)),
    EARLY: (((0, 1, 2), 0),),
    MID: (((0, 1, 2), 1),),
    LATE: (((0, 1, 2), 0),),
}
LOCAL = {OUT: 0, GATE: 1024, EARLY: 2048, MID: 2560, LATE: 2944}
BASE = {GATE: 0, EARLY: 2048, MID: 3072, LATE: 3840}
WIDTH = {OUT: 1024, GATE: 1024, EARLY: 512, MID: 384, LATE: 384}
BACK_TILES = (
    (0, 512),
    (512, 512),
    (1024, 512),
    (1536, 512),
    (2048, 512),
    (2560, 512),
    (3072, 512),
    (3584, 256),
    (3840, 512),
    (4352, 256),
)

eps = 1e-05
LOG2E = 1.4426950408889634
highest = lax.Precision.HIGHEST

PLAN = (
    (1, (("dn", 0),)),
    (2, (("own", GATE),)),
    (4, (("dn", 1),)),
    (6, (("dn", 2),)),
    (7, (("one", OUT),)),
    (8, (("dn", 3),)),
    (9, (("give", EARLY),)),
    (11, (("one", GATE), ("own", EARLY))),
    (13, (("two", OUT), ("dn", 4))),
    (14, (("dn", 5),)),
    (15, (("two", GATE), ("give", MID), ("dn", 6))),
)


def place():
    dp, fsdp = lax.axis_index("dp"), lax.axis_index("fsdp")
    return {"x": (fsdp // 2) % 4, "y": (dp // 4) * 2 + fsdp // 8, "z": dp % 4, "c": fsdp % 2}


def device(at):
    y = at["y"]
    return ((y // 2) * 4 + at["z"], (y % 2) * 8 + at["x"] * 2 + at["c"])


def moved(at, axis, step):
    size = 2 if axis == "c" else 4
    return dict(at, **{axis: lax.rem(at[axis] + step, size)})


def greet(at):
    peers = [moved(at, axis, step) for axis in "xyz" for step in (1, 2, 3)] + [moved(at, "c", 1)]
    for peer in peers:
        pl.semaphore_signal(pltpu.get_barrier_semaphore(), inc=1, device_id=device(peer), device_id_type=MESH)


def meet():
    pl.semaphore_wait(pltpu.get_barrier_semaphore(), 10)


def remote(src, dst, send, recv, peer):
    return pltpu.make_async_remote_copy(
        src_ref=src, dst_ref=dst, send_sem=send, recv_sem=recv, device_id=device(peer), device_id_type=MESH
    )


def chips(at, full):
    every = slice(None)
    y, z, x = at["y"], at["z"], at["x"]
    return (
        every if "y" in full else y // 2,
        every if "z" in full else z,
        every if "y" in full else y % 2,
        every if "x" in full else x,
    )


def rolled_down(x, step):
    zeros = jnp.zeros((8, x.shape[1]), x.dtype)
    return pltpu.roll(jnp.concatenate([zeros, x], axis=0), step, axis=0)[8:]


def rolled_up(x, step):
    rows = x.shape[0]
    zeros = jnp.zeros((8, x.shape[1]), x.dtype)
    return pltpu.roll(jnp.concatenate([x, zeros], axis=0), rows + 8 - step, axis=0)[:rows]


def tile(j, base=0, size=128):
    return pl.ds(pl.multiple_of(base + j * size, 128), size)


def dot_nt(a, b):
    return lax.dot_general(a, b, (((1,), (1,)), ((), ())), preferred_element_type=jnp.float32)


def dot(a, b, **more):
    return jnp.dot(a, b, preferred_element_type=jnp.float32, **more)


def row_sum(x):
    return jnp.sum(x, axis=1, keepdims=True)


def col_sum(x):
    return jnp.sum(x, axis=0, keepdims=True)


def block_kernel(
    lengths,
    ids,
    in_shard_hbm,
    wo_hbm,
    tokens_hbm,
    cotangent_hbm,
    params_hbm,
    block_out_hbm,
    input_grad,
    gi_hbm,
    go_hbm,
    small_hbm,
    norm_hbm,
    full_in,
    in_shard,
    wo,
    tokens,
    cotangent,
    params,
    block_out,
    gi_out,
    go_out,
    small_out,
    norm_out,
    wi,
    other,
    blk,
    live,
    skip,
    full_out,
    work,
    proj,
    act,
    dsilu,
    y_ref,
    dinner,
    dproj,
    inner_t,
    normed,
    normed_t,
    mix,
    mix_t,
    cum_parts,
    key_parts,
    cum_t,
    key_t,
    step_ref,
    q_ref,
    m_ref,
    dcum_ref,
    dstep_ref,
    back_ref,
    taps,
    gain,
    norm_gain,
    part0,
    recv1,
    part1,
    recv2,
    part2,
    recv3,
    swap_from,
    swap_to,
    small_now,
    small_other,
    small_half,
    small_got,
    small_last,
    norm_now,
    norm_got,
    swap_sem,
    local_sem,
    edge_sem,
    ag_send,
    ag_recv,
    ag_pass,
    ag_got,
    rs_send,
    rs_recv,
    rs_pass,
    rs_got,
    small_send,
    small_recv,
    norm_send,
    norm_recv,
):
    low, full = jnp.bfloat16, jnp.float32
    at = place()
    core = at["c"]
    first = core == 0
    sibling = moved(at, "c", 1)
    here = chips(at, ())
    inputs = [
        pltpu.make_async_copy(source, target, edge_sem.at[i])
        for i, (source, target) in enumerate(
            (
                (in_shard_hbm, in_shard),
                (params_hbm, params),
                (tokens_hbm, tokens),
                (wo_hbm, wo),
                (cotangent_hbm, cotangent),
            )
        )
    ]
    for copy in inputs:
        copy.start()
    greet(at)

    lane = lax.broadcasted_iota(jnp.int32, (TOK, 128), 1)
    left = lane < HEAD
    row = lax.broadcasted_iota(jnp.int32, (TOK, TOK), 0)
    column = lax.broadcasted_iota(jnp.int32, (TOK, TOK), 1)
    for copy in inputs:
        copy.wait()
    wi[:, COLS - 256 :] = jnp.zeros((8, 256), full)
    wi[:, :PROJ] = in_shard[...].astype(full)
    wi[:, COLS - 128 :] = params[0:8, :]
    full_out[here + (core,)] = wo[...]
    length = lengths[ids[0]]
    live[...] = (lax.broadcasted_iota(jnp.int32, (TOK, 128), 0) < length).astype(full)
    m_ref[...] = jnp.zeros_like(m_ref)
    for j in range(D // 128):
        x = tokens[:, j * 128 : j * 128 + 128].astype(full)
        m_ref[...] += x * x
    token_scale = lax.rsqrt(row_sum(m_ref[...]) / D + eps)
    owner = lax.broadcasted_iota(jnp.int32, (128, INNER), 1) >> 6
    repeats = (lax.broadcasted_iota(jnp.int32, (128, INNER), 0) == owner).astype(full)
    skip[...] = dot(params[8:16, :], repeats, precision=highest)[2:3]
    heads = params[8:16, :]
    meet()

    swap = remote(wi, other, swap_sem.at[0], swap_sem.at[1], sibling)
    swap.start()

    def held(batch, part, reach):
        start, width = GET_PARTS[batch][part]
        if batch == OUT:
            return full_out.at[chips(at, reach) + (core, slice(None), pl.ds(start, width))]
        spot = pl.multiple_of(core * GET_WIDTH[batch] + start + GET_BASE[batch], 128)
        return full_in.at[chips(at, reach) + (slice(None), pl.ds(spot, width))]

    def wait_bytes(blocks, width, sem):
        size = 512 if width % 512 == 0 else 128
        count = blocks * width // size
        if count > 2 * CHIPS:
            size, count = 512, blocks * width // 512
        shape = work.at[pl.ds(0, count), :, pl.ds(0, size)]
        pltpu.make_async_copy(shape, shape, sem).wait()

    drained = []

    def hop(batch, phase):
        slot = batch * 3 + phase
        for part in range(3):
            target = held(batch, part, ORDERS[part][:phase])
            source = target
            if phase == 0 and batch != OUT:
                start, width = GET_PARTS[batch][part]
                source = blk.at[:, pl.ds(GET_BASE[batch] // 2 + start, width)]
            for step in (1, 2, 3):
                peer = moved(at, ORDERS[part][phase], step)
                remote(source, target, ag_send.at[slot], ag_recv.at[slot], peer).start()
        drained.append((3 * 4**phase, GET_WIDTH[batch], ag_send.at[slot]))

    def landed(batch, phase):
        wait_bytes(3 * 4**phase, GET_WIDTH[batch], ag_recv.at[batch * 3 + phase])

    def give(batch):
        landed(batch, 2)
        for part in range(3):
            region = held(batch, part, "xyz")
            remote(region, region, ag_pass.at[batch], ag_got.at[batch], sibling).start()
        drained.append((CHIPS, GET_WIDTH[batch], ag_pass.at[batch]))

    def taken(batch):
        wait_bytes(CHIPS, GET_WIDTH[batch], ag_got.at[batch])

    swap.wait()
    stores = []

    def begin(batch):
        base, width = GET_BASE[batch], GET_WIDTH[batch]
        lanes = pl.ds(pl.multiple_of(base + core * width, 128), width)
        mine, theirs = wi[:, lanes], other[:, lanes]
        blk[:, base // 2 : base // 2 + width] = jnp.concatenate(
            [jnp.where(first, mine, theirs), jnp.where(first, theirs, mine)], axis=0
        ).astype(low)
        launch(batch, 0)
        copy = pltpu.make_async_copy(
            blk.at[:, pl.ds(base // 2, width)], full_in.at[here + (slice(None), lanes)], local_sem.at[len(stores)]
        )
        copy.start()
        stores.append(copy)

    def launch(batch, phase):
        if phase:
            landed(batch, phase - 1)
        hop(batch, phase)

    begin(LATE)
    begin(EARLY)
    begin(GATE)
    launch(OUT, 0)
    for copy in stores:
        copy.wait()
    launch(LATE, 1)
    launch(EARLY, 1)
    launch(LATE, 2)
    launch(GATE, 1)
    launch(EARLY, 2)
    launch(OUT, 1)

    def slot_of(slot):
        if slot < 2:
            return work.reshape(4, 4, 2, 4, 16, 512).at[pl.ds(2 * slot, 2)]
        return inner_t.reshape(2, 4, 2, 4, 2, 16, 512).at[:, :, :, :, slot - 2]

    def fetched(slot, start, width):
        source = full_in.at[:, :, :, :, :, pl.ds(start, width)]
        return pltpu.make_async_copy(source, slot_of(slot).at[:, :, :, :, :, pl.ds(0, width)], local_sem.at[3 + slot])

    def fetch(i):
        fetched(i % 4, *TILES[i]).start()

    def weight(i):
        slot, width = i % 4, TILES[i][1]
        fetched(slot, *TILES[i]).wait()
        if slot < 2:
            return work[pl.ds(CHIPS * slot, CHIPS), :, :width].reshape(D, width)
        return inner_t[:, slot - 2, :, :width].reshape(D, width)

    give(LATE)
    launch(GATE, 2)
    taken(LATE)
    fetch(1)
    fetch(0)
    late = weight(1)
    packed = late[:, 128:]

    def spread(r, base, count, each):
        pick = (
            lax.broadcasted_iota(jnp.int32, (128, D), 0) * 8 + r == lax.broadcasted_iota(jnp.int32, (128, D), 1)
        ).astype(low)
        shared = dot(pick, packed).astype(low)
        line = lax.broadcasted_iota(jnp.int32, (128, count), 0).astype(full)
        spot = lax.broadcasted_iota(jnp.int32, (128, count), 1).astype(full) + base
        owner = jnp.floor((spot + 0.5) * (1.0 / each))
        found = dot(shared, (line == spot - owner * each).astype(low))
        return col_sum(jnp.where(line == owner, found, 0.0))

    norm_gain[...] = spread(0, 0, D, 8)
    for j in range(D // 128):
        cols = slice(j * 128, j * 128 + 128)
        value = (tokens[:, cols].astype(full) * token_scale * norm_gain[:, cols]).astype(low)
        normed[:, cols] = value
        normed_t[j * 8 : j * 8 + 8] = value.T.reshape(8, 16, TOK)

    def project(i, weights):
        start, width = TILES[i][0], weights.shape[1]
        proj[:, start : start + width] = dot(normed[...], weights)

    def convolve(begin, end):
        @pl.loop(begin, end)
        def _(j):
            cols = tile(j)
            x = proj[:, tile(j, INNER)]
            pre = taps[4:5, cols] + taps[3:4, cols] * x
            for step in (1, 2, 3):
                pre = pre + taps[3 - step : 4 - step, cols] * rolled_down(x, step)
            sig = jax.nn.sigmoid(pre)
            act[:, cols] = (pre * sig).astype(low)
            dsilu[:, cols] = (sig * (1.0 + pre * (1.0 - sig))).astype(low)

    project(1, late[:, :128])
    project(0, weight(0))
    give(EARLY)
    taps[...] = jnp.zeros_like(taps)
    for base in (0, XBC // 2):
        for k in range(CONV + 1):
            taps[k : k + 1, base : base + XBC // 2] = spread((3, 4, 5, 6, 2)[k], base, XBC // 2, 18)
    gain[...] = spread(1, 0, INNER, 16)
    launch(OUT, 2)
    taken(EARLY)
    for i in (2, 3, 4, 5):
        fetch(i)
    convolve(SPLIT, XBC // 128)

    raw = proj[:, INNER + XBC : INNER + XBC + 128] + heads[0:1, :]
    grown = jnp.exp(-jnp.abs(raw))
    more = 1.0 + grown
    logged = jnp.where(more == 1.0, grown, jnp.log(more) * grown / jnp.where(more == 1.0, 1.0, more - 1.0))
    steps = jnp.where(lane < HEADS, jnp.maximum(raw, 0.0) + logged, 0.0)
    rate = -jnp.exp(heads[1:2, :])

    def split(x):
        top = x.astype(low)
        middle = (x - top.astype(full)).astype(low)
        return top, middle, (x - top.astype(full) - middle.astype(full)).astype(low)

    def summed(mask, x):
        found = dot(jnp.where(mask, 1.0, 0.0).astype(low), jnp.concatenate(split(x), axis=1))
        return found[:, :128] + found[:, 128:256] + found[:, 256:]

    cum = summed(row >= column, steps * rate) * LOG2E
    step_ref[...] = steps
    key = cum - jnp.log2(jnp.maximum(steps, 1e-37))
    turned, key_turned = cum.T, key.T
    for head in range(HEADS):
        cum_t[head] = turned[head : head + 1]
        key_t[head] = key_turned[head : head + 1]

    def thirds(x):
        top, middle, rest = [part.astype(full) for part in split(jnp.where(lane < HEADS, x, 0.0))]
        return (top + pltpu.roll(middle, HEADS, axis=1) + pltpu.roll(rest, 2 * HEADS, axis=1)).astype(low)

    cum_parts[...] = thirds(cum)
    key_parts[...] = thirds(key)
    mixed = jnp.where(row >= column, dot_nt(act[:, INNER + STATE :], act[:, INNER : INNER + STATE]), 0.0)
    mix[...] = mixed
    mix_t[...] = mixed.T

    for i in (2, 3):
        project(i, weight(i))
    give(GATE)
    for i in (4, 5):
        project(i, weight(i))
    convolve(0, SPLIT)
    taken(GATE)
    for i in (6, 7, 8, 9):
        fetch(i)
    for i in (6, 7, 8, 9):
        project(i, weight(i))
    give(OUT)
    q_ref[...] = jnp.zeros_like(q_ref)
    dcum_ref[...] = jnp.zeros_like(dcum_ref)
    dstep_ref[...] = jnp.zeros_like(dstep_ref)

    causal = lax.broadcasted_iota(jnp.int32, (128, 128), 0) >= lax.broadcasted_iota(jnp.int32, (128, 128), 1)

    anti = lax.broadcasted_iota(jnp.int32, (128, 128), 0) <= lax.broadcasted_iota(jnp.int32, (128, 128), 1)

    def spread_heads(parts, j):
        line = lax.broadcasted_iota(jnp.int32, (128, 256), 0)
        head = 2 * j + (lax.broadcasted_iota(jnp.int32, (128, 256), 1) >> 7)
        return dot(parts[...], jnp.where(((line & 31) == head) & (line < 96), 1.0, 0.0).astype(low))

    @pl.loop(0, HEADS // 2)
    def _(j):
        cols = tile(j)
        cums = spread_heads(cum_parts, j)
        values = act[:, cols]
        for block in range(TOK // 128):
            start, last = block * 128, block * 128 + 128
            halves = []
            for e in (0, 1):
                pieces = []
                for past in range(block + 1):
                    span = slice(past * 128, past * 128 + 128)
                    gap = cums[start:last, e * 128 : e * 128 + 128] - key_t[2 * j + e, :, span]
                    if past == block:
                        gap = jnp.where(causal, gap, -1e30)
                    pieces.append((mix[start:last, span] * jnp.exp2(gap)).astype(low))
                halves.append(jnp.concatenate(pieces, axis=1))
            found = dot(jnp.concatenate(halves, axis=0), values[:last])
            y = jnp.where(left[:128], found[:128], found[128:]) + skip[:, cols] * values[start:last].astype(full)
            y_ref[start:last, cols] = y
            gate = proj[start:last, cols]
            gated = y * gate * jax.nn.sigmoid(gate)
            q_ref[start:last] += gated * gated

    q_ref[...] = jnp.broadcast_to(lax.rsqrt(row_sum(q_ref[...]) / INNER + eps), (TOK, 128))
    mix[...] = jnp.zeros_like(mix)

    @pl.loop(0, INNER // 128)
    def _(j):
        cols = tile(j)
        gate = proj[:, cols]
        gated = y_ref[:, cols] * gate * jax.nn.sigmoid(gate)
        value = (gated * q_ref[...] * gain[:, cols]).astype(low)
        dproj[:, cols] = value
        inner_t[pl.ds(4 * j, 4)] = value.T.reshape(4, 2, 16, TOK)

    for j in range(D // 128):
        cols = slice(j * 128, j * 128 + 128)
        normed[:, cols] = (live[...] * cotangent[:, cols].astype(full)).astype(low)

    def grads(batch, group, side, half):
        start = PARTS[batch][group[0]][0]
        width = sum(PARTS[batch][part][1] for part in group)
        if batch == OUT:
            lhs = inner_t[pl.ds(32 * half, 32), side].reshape(TOK, TOK)
            rhs = normed[:, start : start + width]
        else:
            lhs = normed_t[pl.ds(32 * half, 32)].reshape(TOK, TOK)
            rhs = dproj[:, pl.ds(pl.multiple_of(BASE[batch] + start + side * WIDTH[batch], 128), width)]
        value = dot(lhs, rhs)
        return [(part, PARTS[batch][part][0] - start, PARTS[batch][part][1], value) for part in group]

    def spot_of(part, half, m):
        spot = {"y": 2 * half + (m // 4) % 2, "z": m // 8, "x": m % 4}
        axes = ORDERS[part]
        return spot[axes[2]] * 16 + spot[axes[1]] * 4 + spot[axes[0]]

    users = [[], []]

    def rs_free():
        for gone in users:
            while gone:
                rs_pass_copy(*gone.pop()).wait_send()

    def rs_give(batch):
        for group, slot in GROUPS[batch]:
            while users[slot]:
                rs_pass_copy(*users[slot].pop()).wait_send()
            origin = PARTS[batch][group[0]][0]
            for half in (0, 1):
                for part, offset, width, value in grads(batch, group, 1 - core, half):
                    value = value[:, offset : offset + width].astype(low)
                    for m in range(32):
                        work[CHIPS * slot + spot_of(part, half, m), :, offset : offset + width] = value[
                            16 * m : 16 * m + 16
                        ]
            for part in group:
                offset = PARTS[batch][part][0] - origin
                users[slot].append((batch, part, slot, offset))
                rs_pass_copy(batch, part, slot, offset).start()

    def rs_pass_copy(batch, part, slot=0, offset=0):
        width = PARTS[batch][part][1]
        sem = batch * 3 + part
        return remote(
            work.at[pl.ds(CHIPS * slot, CHIPS), :, pl.ds(offset, width)],
            part0.at[:, :, lanes_of(batch, part)],
            rs_pass.at[sem],
            rs_got.at[batch],
            sibling,
        )

    def lanes_of(batch, part):
        start, width = PARTS[batch][part]
        return pl.ds(LOCAL[batch] + start, width)

    def rs_copies(batch, part, stage):
        lanes = lanes_of(batch, part)
        axis = ORDERS[part][3 - stage]
        copies = []
        for step in (1, 2, 3):
            peer = moved(at, axis, step)
            there, slot = peer[axis], pl.ds(step - 1, 1)
            if stage == 1:
                source, target = part0.at[pl.ds(there * 16, 16), :, lanes], recv1.at[pl.ds(16 * step - 16, 16), :, lanes]
            elif stage == 2:
                source, target = part1.at[pl.ds(there * 4, 4), :, lanes], recv2.at[pl.ds(4 * step - 4, 4), :, lanes]
            else:
                source, target = part2.at[pl.ds(there, 1), :, lanes], recv3.at[slot, :, lanes]
            sem = batch * 3 + stage - 1
            copies.append(remote(source, target, rs_send.at[sem], rs_recv.at[sem], peer))
        return copies

    def rs_hop(batch, part, stage):
        for copy in rs_copies(batch, part, stage):
            copy.start()

    def rs_wait(batch, stage, sems):
        lanes = pl.ds(LOCAL[batch], WIDTH[batch])
        every = (recv1, recv2, recv3)[stage - 1].at[:, :, lanes]
        pltpu.make_async_copy(every, every, sems.at[batch * 3 + stage - 1]).wait()

    def rs_own(batch):
        lanes = pl.ds(LOCAL[batch], WIDTH[batch])
        every = part0.at[:, :, lanes]
        pltpu.make_async_copy(every, every, rs_got.at[batch]).wait()
        for group, _ in GROUPS[batch]:
            for half in (0, 1):
                for part, offset, width, value in grads(batch, group, core, half):
                    lanes = lanes_of(batch, part)
                    for m in range(32):
                        now = pl.ds(spot_of(part, half, m), 1)
                        piece = value[16 * m : 16 * m + 16, offset : offset + width][None]
                        part0[now, :, lanes] = (piece + part0[now, :, lanes].astype(full)).astype(low)
            for part in group:
                rs_hop(batch, part, 1)

    def part_one(batch, part):
        lanes = lanes_of(batch, part)
        mine = at[ORDERS[part][2]] * 16
        for i in range(16):
            now = pl.ds(i, 1)
            value = part0[pl.ds(mine + i, 1), :, lanes].astype(full)
            for k in range(3):
                value = value + recv1[pl.ds(16 * k + i, 1), :, lanes].astype(full)
            part1[now, :, lanes] = value.astype(low)
        rs_hop(batch, part, 2)

    def part_two(batch, part):
        lanes = lanes_of(batch, part)
        mine = at[ORDERS[part][1]] * 4
        for i in range(4):
            now = pl.ds(i, 1)
            value = part1[pl.ds(mine + i, 1), :, lanes].astype(full)
            for k in range(3):
                value = value + recv2[pl.ds(4 * k + i, 1), :, lanes].astype(full)
            part2[now, :, lanes] = value.astype(low)
        rs_hop(batch, part, 3)

    def part_three(batch, part):
        lanes = lanes_of(batch, part)
        value = part2[pl.ds(at[ORDERS[part][0]], 1), :, lanes].astype(full)
        for k in range(3):
            value = value + recv3[pl.ds(k, 1), :, lanes].astype(full)
        value = value[0]
        start, width = PARTS[batch][part]
        if batch == OUT:
            go_out[:, start : start + width] = value
            return
        base = BASE[batch]
        at_column = pl.multiple_of(base + core * WIDTH[batch] + start, 128)
        gi_out[:, pl.ds(at_column, width)] = jnp.where(first, value[:8], value[8:])
        swap_from[:, pl.ds(base // 2 + start, width)] = jnp.where(first, value[8:], value[:8])

    rs_give(OUT)
    taken(OUT)
    while drained:
        wait_bytes(*drained.pop())
    wout = full_out.reshape(INNER, D)
    wide_live = jnp.concatenate([live[...], live[...]], axis=1)

    m_ref[...] = jnp.zeros_like(m_ref)

    @pl.loop(0, D // 256)
    def _(j):
        cols = tile(j, 0, 256)
        branch = dot(dproj[:, :INNER], wout[:, cols])
        block_out[:, cols] = (tokens[:, cols].astype(full) + wide_live * branch).astype(low)
        shares = normed[:, cols].astype(full) * branch
        m_ref[...] += shares[:, :128] + shares[:, 128:]

    outputs = [pltpu.make_async_copy(block_out, block_out_hbm, edge_sem.at[5])]
    outputs[0].start()

    m_ref[...] = jnp.broadcast_to(row_sum(m_ref[...]) / INNER, (TOK, 128))

    @pl.loop(0, INNER // 256)
    def _(j):
        wide = tile(j, 0, 256)
        sums = [jnp.zeros((1, 128), full)] * 2
        for rows in (slice(0, 256), slice(256, 512)):
            value = dot_nt(normed[rows, :], wout[wide, :])
            for half in (0, 1):
                cols = tile(2 * j + half)
                inside = value[:, half * 128 : half * 128 + 128]
                y, gate, q = y_ref[rows, cols], proj[rows, cols], q_ref[rows, :]
                sig = jax.nn.sigmoid(gate)
                silu = gate * sig
                u = y * silu * q
                sums[half] = sums[half] + col_sum(inside * u)
                dgated = q * (inside * gain[:, cols] - u * m_ref[rows, :])
                dproj[rows, cols] = (dgated * y * (sig + silu * (1.0 - sig))).astype(low)
                dinner[rows, cols] = dgated * silu
        for half in (0, 1):
            small_now[5:6, tile(2 * j + half)] = sums[half]

    rs_own(OUT)

    rs_give(GATE)

    dnormed = proj.at[:, pl.ds(0, D)]

    def back_load(i):
        fetched(2 + i % 2, *BACK_TILES[i]).start()

    def back_tile(i):
        start, width = BACK_TILES[i]
        fetched(2 + i % 2, start, width).wait()
        value = dot_nt(dproj[:, start : start + width], inner_t[:, i % 2, :, :width].reshape(D, width))
        dnormed[...] = value if i == 0 else dnormed[...] + value
        if i + 2 < len(BACK_TILES):
            back_load(i + 2)

    back_load(0)
    back_load(1)

    def conv_back(dact, j):
        cols = tile(j)
        x = proj[:, tile(j, INNER)]
        dpre = dact * dsilu[:, cols].astype(full)
        small_now[4:5, cols] = col_sum(dpre)
        small_now[3:4, cols] = col_sum(dpre * x)
        dx = taps[3:4, cols] * dpre
        for step in (1, 2, 3):
            moved_up = rolled_up(dpre, step)
            small_now[3 - step : 4 - step, cols] = col_sum(moved_up * x)
            dx = dx + taps[3 - step : 4 - step, cols] * moved_up
        dproj[:, tile(j, INNER)] = dx.astype(low)

    def rs_one(batch):
        rs_wait(batch, 1, rs_recv)
        for part in range(3):
            part_one(batch, part)

    def rs_two(batch):
        rs_wait(batch, 2, rs_recv)
        for part in range(3):
            part_two(batch, part)

    def rs_three(batch):
        rs_wait(batch, 3, rs_recv)
        for part in range(3):
            part_three(batch, part)

    back_ref[...] = jnp.zeros_like(back_ref)

    def settle(j):
        cols = tile(j)
        values, dy, back = act[:, cols].astype(full), dinner[:, cols], back_ref[...]
        direct = values * back
        crossing = dy.astype(low).astype(full) * (y_ref[:, cols] - skip[:, cols] * values) - direct
        small_now[7:8, cols] = col_sum(dy * values)
        for e in (0, 1):
            mine = left if e == 0 else jnp.logical_not(left)
            spot = lane == 2 * j + e
            dcum_ref[...] = jnp.where(spot, row_sum(jnp.where(mine, crossing, 0.0)), dcum_ref[...])
            dstep_ref[...] = jnp.where(spot, row_sum(jnp.where(mine, direct, 0.0)), dstep_ref[...])
        conv_back(back + skip[:, cols] * dy, j)

    @pl.loop(0, HEADS // 2)
    def _(j):
        for turn, events in PLAN:

            @pl.when(j == turn)
            def _(events=events):
                for action, what in events:
                    if action == "dn":
                        back_tile(what)
                    else:
                        {"give": rs_give, "own": rs_own, "one": rs_one, "two": rs_two}[action](what)

        settle(jnp.maximum(j - 1, 0))
        cols = tile(j)
        keys = spread_heads(key_parts, j)
        v_low = act[:, cols]
        dy_low = dinner[:, cols].astype(low)
        own = (jnp.where(left, v_low, jnp.zeros_like(v_low)), jnp.where(left, jnp.zeros_like(v_low), v_low))
        found = []
        for block in range(TOK // 128):
            start, last = block * 128, block * 128 + 128
            both = dot_nt(jnp.concatenate([own[0][start:last], own[1][start:last]], axis=0), dy_low[start:])
            halves = []
            total = None
            for e in (0, 1):
                pieces, shares = [], []
                for later in range(block, TOK // 128):
                    span = slice(later * 128, later * 128 + 128)
                    gap = cum_t[2 * j + e, :, span] - keys[start:last, e * 128 : e * 128 + 128]
                    if later == block:
                        gap = jnp.where(anti, gap, -1e30)
                    decay = jnp.exp2(gap)
                    pieces.append((mix_t[start:last, span] * decay).astype(low))
                    inside = slice((later - block) * 128, (later - block + 1) * 128)
                    shares.append(both[e * 128 : e * 128 + 128, inside] * decay)
                halves.append(jnp.concatenate(pieces, axis=1))
                share = jnp.concatenate(shares, axis=1)
                total = share if total is None else total + share
            mix[start:last, start:] += total
            given_back = dot(jnp.concatenate(halves, axis=0), dy_low[start:])
            found.append(jnp.where(left[:128], given_back[:128], given_back[128:]))
        for block, value in enumerate(found):
            back_ref[block * 128 : block * 128 + 128] = value

    settle(HEADS // 2 - 1)
    rs_own(MID)
    masked = jnp.where(row <= column, mix[...], 0.0)
    conv_back(dot(masked.astype(low), act[:, INNER + STATE :]), INNER // 128)
    conv_back(dot(masked.T.astype(low), act[:, INNER : INNER + STATE]), INNER // 128 + 1)
    dacc = summed(row <= column, dcum_ref[...])
    sig = jax.nn.sigmoid(proj[:, INNER + XBC : INNER + XBC + 128] + heads[0:1, :])
    steps = step_ref[...]
    ratio = jnp.where(steps > 1e-30, sig / jnp.maximum(steps, 1e-30), 1.0)
    draw = jnp.where(lane < HEADS, dstep_ref[...] * ratio + dacc * rate * sig, 0.0)
    dproj[:, INNER + XBC : INNER + XBC + 128] = draw.astype(low)
    dproj[:, INNER + XBC + 128 :] = jnp.zeros((TOK, 128), low)
    small_now[6:7, :] = jnp.zeros((1, XBC), full)
    small_now[6:7, :128] = col_sum(draw)
    small_now[6:7, 128:256] = rate * col_sum(dacc * steps)
    small_now[5:6, INNER:] = jnp.zeros((1, XBC - INNER), full)
    small_now[7:8, INNER:] = jnp.zeros((1, XBC - INNER), full)


    def small_swap():
        away = pl.ds(pl.multiple_of((1 - core) * HALF, 128), HALF)
        return remote(small_now.at[:, away], small_other, small_send.at[0], small_recv.at[0], sibling)

    def small_copies(stage):
        made = []
        for part in range(3):
            lanes = pl.ds(part * THIRD, THIRD)
            axis = ORDERS[part][stage - 1]
            for step in (1, 2, 3):
                slot = (stage - 1) * 3 + step - 1
                made.append(
                    remote(
                        small_half.at[stage - 1, :, lanes],
                        small_got.at[slot, :, lanes],
                        small_send.at[stage],
                        small_recv.at[stage],
                        moved(at, axis, step),
                    )
                )
        return made

    def small_back():
        return remote(small_half.at[3], small_last, small_send.at[4], small_recv.at[4], sibling)

    def small_wait(stage, sems):
        if stage in (0, 4):
            sems_of = small_other if stage == 0 else small_last
            pltpu.make_async_copy(sems_of, sems_of, sems.at[stage]).wait()
        else:
            every = small_got.at[pl.ds((stage - 1) * 3, 3)]
            pltpu.make_async_copy(every, every, sems.at[stage]).wait()

    def small_add(stage):
        small_wait(stage, small_recv)
        if stage == 0:
            mine = pl.ds(pl.multiple_of(core * HALF, 128), HALF)
            small_half[0] = small_now[:, mine] + small_other[...]
        else:
            value = small_half[stage - 1]
            for k in range(3):
                value = value + small_got[(stage - 1) * 3 + k]
            small_half[stage] = value
        for copy in small_copies(stage + 1) if stage < 3 else [small_back()]:
            copy.start()

    def norm_start(stage):
        for step in (1,) if stage == 0 else (1, 2, 3):
            slot = 0 if stage == 0 else stage * 3 - 3 + step
            peer = moved(at, "cxyz"[stage], step)
            remote(norm_now.at[stage], norm_got.at[slot], norm_send.at[stage], norm_recv.at[stage], peer).start()

    def norm_wait(stage, sems):
        every = norm_got.at[pl.ds(0, 1)] if stage == 0 else norm_got.at[pl.ds(stage * 3 - 2, 3)]
        pltpu.make_async_copy(every, every, sems.at[stage]).wait()

    def norm_add(stage):
        norm_wait(stage, norm_recv)
        value = norm_now[stage]
        for k in range(1 if stage == 0 else 3):
            value = value + norm_got[0 if stage == 0 else stage * 3 - 2 + k]
        if stage == 3:
            norm_out[...] = value
        else:
            norm_now[stage + 1] = value
            norm_start(stage + 1)

    small_swap().start()
    rs_give(LATE)
    back_tile(7)
    small_add(0)
    back_tile(8)
    rs_own(LATE)
    back_tile(9)
    small_add(1)
    m_ref[...] = jnp.zeros_like(m_ref)
    for j in range(D // 128):
        cols = slice(j * 128, j * 128 + 128)
        u = tokens[:, cols].astype(full) * token_scale
        du = dnormed[:, cols] * u
        norm_now[0, j : j + 1, :] = col_sum(du)
        m_ref[...] += du * norm_gain[:, cols]
    mean = row_sum(m_ref[...]) / D
    norm_start(0)
    rs_one(EARLY)
    rs_one(MID)
    for j in range(D // 128):
        cols = slice(j * 128, j * 128 + 128)
        u = tokens[:, cols].astype(full) * token_scale
        du = dnormed[:, cols] * norm_gain[:, cols]
        normed[:, cols] = (cotangent[:, cols].astype(full) + token_scale * (du - u * mean)).astype(low)
    final = pltpu.make_async_copy(normed, input_grad, local_sem.at[0])
    final.start()
    norm_add(0)
    rs_three(OUT)
    rs_three(GATE)
    for batch in (OUT, GATE):
        for stage in (1, 2, 3):
            rs_wait(batch, stage, rs_send)
    small_add(2)
    norm_add(1)
    rs_one(LATE)
    rs_two(EARLY)
    rs_two(MID)
    small_add(3)
    norm_add(2)
    rs_two(LATE)
    rs_three(EARLY)
    rs_three(MID)
    small_wait(4, small_recv)
    mine = pl.ds(pl.multiple_of(core * HALF, 128), HALF)
    small_out[:, mine] = small_half[3]
    small_out[:, pl.ds(pl.multiple_of((1 - core) * HALF, 128), HALF)] = small_last[...]
    outputs.append(pltpu.make_async_copy(small_out, small_hbm, edge_sem.at[6]))
    outputs.append(pltpu.make_async_copy(go_out, go_hbm, edge_sem.at[7]))
    for copy in outputs[1:]:
        copy.start()
    rs_free()
    norm_add(3)
    outputs.append(pltpu.make_async_copy(norm_out, norm_hbm, edge_sem.at[8]))
    outputs[3].start()
    for stage in range(5):
        small_wait(stage, small_send)
    for stage in range(4):
        norm_wait(stage, norm_send)
    rs_three(LATE)
    last = remote(swap_from, swap_to, swap_sem.at[2], swap_sem.at[3], sibling)
    last.start()
    for batch in (EARLY, MID, LATE):
        for stage in (1, 2, 3):
            rs_wait(batch, stage, rs_send)
    final.wait()
    last.wait()
    for batch in (GATE, EARLY, MID, LATE):
        base, width = BASE[batch], WIDTH[batch]
        lanes = pl.ds(pl.multiple_of(base + (1 - core) * width, 128), width)
        gi_out[:, lanes] = swap_to[:, base // 2 : base // 2 + width]
    outputs.append(pltpu.make_async_copy(gi_out, gi_hbm, edge_sem.at[9]))
    outputs[4].start()
    for copy in outputs:
        copy.wait()


def block(lengths, ids, in_shard, wo, tokens, cotangent, params):
    full, low = jnp.float32, jnp.bfloat16
    anywhere = pl.BlockSpec(memory_space=pl.ANY)
    sems = pltpu.SemaphoreType.DMA
    return pl.pallas_call(
        block_kernel,
        out_shape=(
            jax.ShapeDtypeStruct((TOK, D), low),
            jax.ShapeDtypeStruct((TOK, D), low),
            jax.ShapeDtypeStruct((8, COLS), full),
            jax.ShapeDtypeStruct((16, D), full),
            jax.ShapeDtypeStruct((8, XBC), full),
            jax.ShapeDtypeStruct((8, 128), full),
            jax.ShapeDtypeStruct((2, 4, 2, 4, 16, COLS), low),
        ),
        in_specs=[pl.BlockSpec(memory_space=pltpu.SMEM)] * 2 + [anywhere] * 5,
        out_specs=[anywhere] * 7,
        scratch_shapes=[
            pltpu.VMEM((8, PROJ), low),
            pltpu.VMEM((16, D), low),
            pltpu.VMEM((TOK, D), low),
            pltpu.VMEM((TOK, D), low),
            pltpu.VMEM((16, 128), full),
            pltpu.VMEM((TOK, D), low),
            pltpu.VMEM((8, COLS), full),
            pltpu.VMEM((16, D), full),
            pltpu.VMEM((8, XBC), full),
            pltpu.VMEM((8, 128), full),
            pltpu.VMEM((8, COLS), full),
            pltpu.VMEM((8, COLS), full),
            pltpu.VMEM((16, XBC), low),
            pltpu.VMEM((TOK, 128), full),
            pltpu.VMEM((1, INNER), full),
            pltpu.VMEM((2, 4, 2, 4, 2, 16, D), low),
            pltpu.VMEM((2 * CHIPS, 16, 512), low),
            pltpu.VMEM((TOK, COLS - 128), full),
            pltpu.VMEM((TOK, XBC), low),
            pltpu.VMEM((TOK, XBC), low),
            pltpu.VMEM((TOK, INNER), full),
            pltpu.VMEM((TOK, INNER), full),
            pltpu.VMEM((TOK, COLS), low),
            pltpu.VMEM((CHIPS, 2, 16, TOK), low),
            pltpu.VMEM((TOK, D), low),
            pltpu.VMEM((CHIPS, 16, TOK), low),
            pltpu.VMEM((TOK, TOK), full),
            pltpu.VMEM((TOK, TOK), full),
            pltpu.VMEM((TOK, 128), low),
            pltpu.VMEM((TOK, 128), low),
            pltpu.VMEM((HEADS, 1, TOK), full),
            pltpu.VMEM((HEADS, 1, TOK), full),
            pltpu.VMEM((TOK, 128), full),
            pltpu.VMEM((TOK, 128), full),
            pltpu.VMEM((TOK, 128), full),
            pltpu.VMEM((TOK, 128), full),
            pltpu.VMEM((TOK, 128), full),
            pltpu.VMEM((TOK, 128), full),
            pltpu.VMEM((8, XBC), full),
            pltpu.VMEM((1, INNER), full),
            pltpu.VMEM((1, D), full),
            pltpu.VMEM((CHIPS, 16, SIDE), low),
            pltpu.VMEM((48, 16, SIDE), low),
            pltpu.VMEM((16, 16, SIDE), low),
            pltpu.VMEM((12, 16, SIDE), low),
            pltpu.VMEM((4, 16, SIDE), low),
            pltpu.VMEM((3, 16, SIDE), low),
            pltpu.VMEM((8, XBC), full),
            pltpu.VMEM((8, XBC), full),
            pltpu.VMEM((8, XBC), full),
            pltpu.VMEM((8, HALF), full),
            pltpu.VMEM((4, 8, HALF), full),
            pltpu.VMEM((9, 8, HALF), full),
            pltpu.VMEM((8, HALF), full),
            pltpu.VMEM((4, 8, 128), full),
            pltpu.VMEM((10, 8, 128), full),
            sems((4,)),
            sems((7,)),
            sems((10,)),
            sems((15,)),
            sems((15,)),
            sems((5,)),
            sems((5,)),
            sems((15,)),
            sems((15,)),
            sems((15,)),
            sems((5,)),
            sems((5,)),
            sems((5,)),
            sems((4,)),
            sems((4,)),
        ],
        compiler_params=pltpu.CompilerParams(collective_id=0, has_side_effects=True, vmem_limit_bytes=63 << 20),
    )(lengths, ids, in_shard, wo, tokens, cotangent, params)


def finish_kernel(
    out_in,
    grad_in,
    gi_in,
    go_in,
    small_in,
    norm_in,
    out_hbm,
    grad_hbm,
    gain_hbm,
    gi_hbm,
    conv_hbm,
    bias_hbm,
    dt_hbm,
    log_hbm,
    skip_hbm,
    inner_hbm,
    go_hbm,
    small,
    norm,
    gi,
    go,
    out,
    grad,
    gain_out,
    gi_out,
    conv_out,
    bias_out,
    dt_out,
    log_out,
    skip_out,
    inner_out,
    sem,
):
    pairs = ((small_in, small), (norm_in, norm), (gi_in, gi), (go_in, go), (out_in, out), (grad_in, grad))
    copies = [pltpu.make_async_copy(source, target, sem.at[i]) for i, (source, target) in enumerate(pairs)]
    for copy in copies:
        copy.start()
    writes = []

    def write(source, target):
        writes.append(pltpu.make_async_copy(source, target, sem.at[len(copies) + len(writes)]))
        writes[-1].start()

    me = lax.axis_index("dp") * 16 + lax.axis_index("fsdp")
    copies[0].wait()

    def from_lane(count):
        return pltpu.roll(small[...], lax.rem(XBC - count * me, XBC), axis=1)

    conv = from_lane(18)
    conv_out[...] = conv[:CONV, :18]
    write(conv_out, conv_hbm)
    bias_out[...] = conv[CONV : CONV + 1, :18]
    write(bias_out, bias_hbm)
    inner_out[...] = from_lane(16)[5:6, :16]
    write(inner_out, inner_hbm)
    dt_out[...] = small[6:7, :HEADS]
    write(dt_out, dt_hbm)
    log_out[...] = small[6:7, 128 : 128 + HEADS]
    write(log_out, log_hbm)
    copies[4].wait()
    write(out, out_hbm)
    copies[5].wait()
    write(grad, grad_hbm)
    copies[2].wait()
    gi_out[...] = gi[:, :PROJ]
    write(gi_out, gi_hbm)
    copies[3].wait()
    write(go, go_hbm)
    owner = lax.broadcasted_iota(jnp.int32, (INNER, 128), 0) >> 6
    sums = (owner == lax.broadcasted_iota(jnp.int32, (INNER, 128), 1)).astype(jnp.float32)
    skip_out[...] = dot(small[:, :INNER], sums, precision=highest)[7:8, :HEADS]
    write(skip_out, skip_hbm)
    copies[1].wait()
    line = lax.broadcasted_iota(jnp.int32, (8, 128), 0)
    row = jnp.sum(jnp.where(line == me // 16, norm[...], 0.0), axis=0, keepdims=True)
    gain_out[...] = pltpu.roll(row, lax.rem(128 - 8 * lax.rem(me, 16), 128), axis=1)[:, :8]
    write(gain_out, gain_hbm)
    for copy in writes:
        copy.wait()


def finish(out, grad, gi, go, small, norm):
    full = jnp.float32
    anywhere = pl.BlockSpec(memory_space=pl.ANY)
    rest = [(CONV, 18), (1, 18), (1, HEADS), (1, HEADS), (1, HEADS), (1, 16)]
    shapes = [(1, 8), (8, PROJ)] + rest
    return pl.pallas_call(
        finish_kernel,
        out_shape=[jax.ShapeDtypeStruct(out.shape, out.dtype)] * 2
        + [jax.ShapeDtypeStruct(shape, full) for shape in shapes + [(16, D)]],
        in_specs=[anywhere] * 6,
        out_specs=[anywhere] * 11,
        scratch_shapes=[
            pltpu.VMEM(small.shape, full),
            pltpu.VMEM(norm.shape, full),
            pltpu.VMEM(gi.shape, full),
            pltpu.VMEM(go.shape, full),
            pltpu.VMEM(out.shape, out.dtype),
            pltpu.VMEM(out.shape, out.dtype),
        ]
        + [pltpu.VMEM(shape, full) for shape in shapes]
        + [pltpu.SemaphoreType.DMA((17,))],
        compiler_params=pltpu.CompilerParams(vmem_limit_bytes=62 << 20),
    )(out, grad, gi, go, small, norm)


def body(
    tokens,
    lengths,
    placement_ids,
    norm_gain,
    in_weight,
    conv_weight,
    conv_bias,
    dt_bias,
    a_log,
    d_skip,
    inner_gain,
    out_weight,
    cotangent,
):
    full = jnp.float32

    def line(values, first):
        values = values.astype(full).reshape(-1, values.shape[-1])
        rows, lanes = values.shape
        return jnp.pad(values, ((first, 16 - first - rows), (0, 128 - lanes)))

    params = (
        line(norm_gain, 0)
        + line(inner_gain, 1)
        + line(conv_bias, 2)
        + line(conv_weight, 3)
        + line(dt_bias, 8)
        + line(a_log, 9)
        + line(d_skip, 10)
    )
    block_out, input_grad, shard_in, shard_out, small, norm, _ = block(
        lengths, placement_ids, in_weight, out_weight, tokens, cotangent, params
    )
    found = finish(block_out, input_grad, shard_in, shard_out, small, norm)
    flat = [0, 0, 1, 0, 0, 1, 1, 1, 1, 1, 0]
    return tuple(value[0] if one else value for value, one in zip(found, flat))


def solution(mesh):
    placed = (
        P(("dp", "fsdp"), None),
        P(),
        P(("dp", "fsdp")),
        P(("dp", "fsdp")),
        P(("dp", "fsdp"), None),
        P(None, ("dp", "fsdp")),
        P(("dp", "fsdp")),
        P(),
        P(),
        P(),
        P(("dp", "fsdp")),
        P(("dp", "fsdp"), None),
        P(("dp", "fsdp"), None),
    )
    return jax.shard_map(
        body,
        mesh=mesh,
        in_specs=placed,
        out_specs=(
            P(("dp", "fsdp"), None),
            P(("dp", "fsdp"), None),
            P(("dp", "fsdp")),
            P(("dp", "fsdp"), None),
            P(None, ("dp", "fsdp")),
            P(("dp", "fsdp")),
            P(),
            P(),
            P(),
            P(("dp", "fsdp")),
            P(("dp", "fsdp"), None),
        ),
        check_vma=False,
    )
```

```python
import jax
import jax.numpy as jnp
import numpy as np
from jax import lax
from jax.experimental import pallas as pl
from jax.experimental.pallas import tpu as pltpu
from jax.sharding import PartitionSpec as P

D = 1024
INNER = 2048
STATE = 128
HEAD = 64
CONV = 4
HEADS = 32
XBC = 2304
PROJ = 4384
TOK = 512
CHIPS = 64
COLS = 4608
SIDE = 3328
HALF = 1152
THIRD = 384
MESH = pl.DeviceIdType.MESH
ORDERS = (("x", "y", "z"), ("y", "z", "x"), ("z", "x", "y"))
OUT, GATE, EARLY, MID, LATE = 0, 1, 2, 3, 4
GET_PARTS = {
    OUT: ((0, 384), (384, 384), (768, 256)),
    GATE: ((0, 384), (384, 384), (768, 256)),
    EARLY: ((0, 256), (256, 256), (512, 384)),
    LATE: ((0, 128), (128, 128), (256, 128)),
}
GET_BASE = {GATE: 0, EARLY: 2048, LATE: 3840}
GET_WIDTH = {OUT: 1024, GATE: 1024, EARLY: 896, LATE: 384}
SPLIT = 14
TILES = (
    (3840, 512),
    (4352, 256),
    (2048, 512),
    (2560, 512),
    (3072, 512),
    (3584, 256),
    (0, 512),
    (512, 512),
    (1024, 512),
    (1536, 512),
)
PARTS = {
    OUT: ((0, 512), (512, 256), (768, 256)),
    GATE: ((0, 256), (512, 512), (256, 256)),
    EARLY: ((0, 128), (128, 128), (256, 256)),
    MID: ((0, 128), (128, 128), (256, 128)),
    LATE: ((0, 128), (128, 128), (256, 128)),
}
GROUPS = {
    OUT: (((0,), 0), ((1, 2), 1)),
    GATE: (((0, 2), 0), ((1,), 1)),
    EARLY: (((0, 1, 2), 0),),
    MID: (((0, 1, 2), 1),),
    LATE: (((0, 1, 2), 0),),
}
LOCAL = {OUT: 0, GATE: 1024, EARLY: 2048, MID: 2560, LATE: 2944}
BASE = {GATE: 0, EARLY: 2048, MID: 3072, LATE: 3840}
WIDTH = {OUT: 1024, GATE: 1024, EARLY: 512, MID: 384, LATE: 384}
BACK_TILES = (
    (0, 512),
    (512, 512),
    (1024, 512),
    (1536, 512),
    (2048, 512),
    (2560, 512),
    (3072, 512),
    (3584, 256),
    (3840, 512),
    (4352, 256),
)

eps = 1e-05
LOG2E = 1.4426950408889634
highest = lax.Precision.HIGHEST

PLAN = (
    (1, (("dn", 0),)),
    (2, (("own", GATE), ("dn", 1))),
    (4, (("dn", 2), ("dn", 3), ("one", OUT))),
    (5, (("give", EARLY),)),
    (6, (("own", EARLY), ("dn", 4), ("one", GATE))),
    (7, (("dn", 5), ("two", OUT))),
    (8, (("give", MID), ("dn", 6))),
)


def place():
    dp, fsdp = lax.axis_index("dp"), lax.axis_index("fsdp")
    return {"x": (fsdp // 2) % 4, "y": (dp // 4) * 2 + fsdp // 8, "z": dp % 4, "c": fsdp % 2}


def device(at):
    y = at["y"]
    return ((y // 2) * 4 + at["z"], (y % 2) * 8 + at["x"] * 2 + at["c"])


def moved(at, axis, step):
    size = 2 if axis == "c" else 4
    return dict(at, **{axis: lax.rem(at[axis] + step, size)})


def greet(at):
    peers = [moved(at, axis, step) for axis in "xyz" for step in (1, 2, 3)] + [moved(at, "c", 1)]
    for peer in peers:
        pl.semaphore_signal(pltpu.get_barrier_semaphore(), inc=1, device_id=device(peer), device_id_type=MESH)


def meet():
    pl.semaphore_wait(pltpu.get_barrier_semaphore(), 10)


def remote(src, dst, send, recv, peer):
    return pltpu.make_async_remote_copy(
        src_ref=src, dst_ref=dst, send_sem=send, recv_sem=recv, device_id=device(peer), device_id_type=MESH
    )


def chips(at, full):
    every = slice(None)
    y, z, x = at["y"], at["z"], at["x"]
    return (
        every if "y" in full else y // 2,
        every if "z" in full else z,
        every if "y" in full else y % 2,
        every if "x" in full else x,
    )


def rolled_down(x, step):
    zeros = jnp.zeros((8, x.shape[1]), x.dtype)
    return pltpu.roll(jnp.concatenate([zeros, x], axis=0), step, axis=0)[8:]


def rolled_up(x, step):
    rows = x.shape[0]
    zeros = jnp.zeros((8, x.shape[1]), x.dtype)
    return pltpu.roll(jnp.concatenate([x, zeros], axis=0), rows + 8 - step, axis=0)[:rows]


def tile(j, base=0, size=128):
    return pl.ds(pl.multiple_of(base + j * size, 128), size)


def dot_nt(a, b):
    return lax.dot_general(a, b, (((1,), (1,)), ((), ())), preferred_element_type=jnp.float32)


def dot(a, b, **more):
    return jnp.dot(a, b, preferred_element_type=jnp.float32, **more)


def row_sum(x):
    return jnp.sum(x, axis=1, keepdims=True)


def col_sum(x):
    return jnp.sum(x, axis=0, keepdims=True)


def block_kernel(
    lengths,
    ids,
    in_shard_hbm,
    wo_hbm,
    tokens_hbm,
    cotangent_hbm,
    params_hbm,
    block_out_hbm,
    input_grad,
    gi_hbm,
    go_hbm,
    small_hbm,
    norm_hbm,
    full_in,
    in_shard,
    wo,
    tokens,
    cotangent,
    params,
    block_out,
    gi_out,
    go_out,
    small_out,
    norm_out,
    wi,
    other,
    blk,
    skip,
    full_out,
    work,
    proj,
    act,
    dsilu,
    y_ref,
    dinner,
    dproj,
    inner_t,
    normed,
    normed_t,
    mix,
    mix_t,
    cum_parts,
    key_parts,
    cum_t,
    key_t,
    step_ref,
    q_ref,
    m_ref,
    dcum_ref,
    dstep_ref,
    back_ref,
    taps,
    gain,
    norm_gain,
    part0,
    recv1,
    part1,
    recv2,
    part2,
    recv3,
    swap_from,
    swap_to,
    small_now,
    small_other,
    small_half,
    small_got,
    small_last,
    norm_now,
    norm_got,
    swap_sem,
    local_sem,
    edge_sem,
    ag_send,
    ag_recv,
    ag_pass,
    ag_got,
    rs_send,
    rs_recv,
    rs_pass,
    rs_got,
    small_send,
    small_recv,
    norm_send,
    norm_recv,
):
    low, full = jnp.bfloat16, jnp.float32
    at = place()
    core = at["c"]
    first = core == 0
    sibling = moved(at, "c", 1)
    here = chips(at, ())
    inputs = [
        pltpu.make_async_copy(source, target, edge_sem.at[i])
        for i, (source, target) in enumerate(
            (
                (in_shard_hbm, in_shard),
                (params_hbm, params),
                (tokens_hbm, tokens),
                (wo_hbm, wo),
                (cotangent_hbm, cotangent),
            )
        )
    ]
    for copy in inputs:
        copy.start()
    greet(at)

    lane = lax.broadcasted_iota(jnp.int32, (TOK, 128), 1)
    left = lane < HEAD
    row = lax.broadcasted_iota(jnp.int32, (TOK, TOK), 0)
    column = lax.broadcasted_iota(jnp.int32, (TOK, TOK), 1)
    for copy in inputs[:2]:
        copy.wait()
    wi[:, COLS - 256 :] = jnp.zeros((8, 256), full)
    wi[:, :PROJ] = in_shard[...].astype(full)
    wi[:, COLS - 128 :] = params[0:8, :]
    meet()

    swap = remote(wi, other, swap_sem.at[0], swap_sem.at[1], sibling)
    swap.start()
    for copy in inputs[2:]:
        copy.wait()
    full_out[here + (core,)] = wo[...]

    def held(batch, part, reach):
        start, width = GET_PARTS[batch][part]
        if batch == OUT:
            return full_out.at[chips(at, reach) + (core, slice(None), pl.ds(start, width))]
        spot = pl.multiple_of(core * GET_WIDTH[batch] + start + GET_BASE[batch], 128)
        return full_in.at[chips(at, reach) + (slice(None), pl.ds(spot, width))]

    def wait_bytes(blocks, width, sem):
        size = 512 if width % 512 == 0 else 128
        count = blocks * width // size
        if count > 2 * CHIPS:
            size, count = 512, blocks * width // 512
        shape = work.at[pl.ds(0, count), :, pl.ds(0, size)]
        pltpu.make_async_copy(shape, shape, sem).wait()

    drained = []

    def hop(batch, phase):
        slot = batch * 3 + phase
        for part in range(3):
            target = held(batch, part, ORDERS[part][:phase])
            source = target
            if phase == 0 and batch != OUT:
                start, width = GET_PARTS[batch][part]
                source = blk.at[:, pl.ds(GET_BASE[batch] // 2 + start, width)]
            for step in (1, 2, 3):
                peer = moved(at, ORDERS[part][phase], step)
                remote(source, target, ag_send.at[slot], ag_recv.at[slot], peer).start()
        drained.append((3 * 4**phase, GET_WIDTH[batch], ag_send.at[slot]))

    def landed(batch, phase):
        wait_bytes(3 * 4**phase, GET_WIDTH[batch], ag_recv.at[batch * 3 + phase])

    def give(batch):
        landed(batch, 2)
        for part in range(3):
            region = held(batch, part, "xyz")
            remote(region, region, ag_pass.at[batch], ag_got.at[batch], sibling).start()
        drained.append((CHIPS, GET_WIDTH[batch], ag_pass.at[batch]))

    def taken(batch):
        wait_bytes(CHIPS, GET_WIDTH[batch], ag_got.at[batch])

    swap.wait()
    stores = []

    def begin(batch):
        base, width = GET_BASE[batch], GET_WIDTH[batch]
        lanes = pl.ds(pl.multiple_of(base + core * width, 128), width)
        mine, theirs = wi[:, lanes], other[:, lanes]
        blk[:, base // 2 : base // 2 + width] = jnp.concatenate(
            [jnp.where(first, mine, theirs), jnp.where(first, theirs, mine)], axis=0
        ).astype(low)
        launch(batch, 0)
        copy = pltpu.make_async_copy(
            blk.at[:, pl.ds(base // 2, width)], full_in.at[here + (slice(None), lanes)], local_sem.at[len(stores)]
        )
        copy.start()
        stores.append(copy)

    def launch(batch, phase):
        if phase:
            landed(batch, phase - 1)
        if phase == 1 and batch != OUT:
            stores.pop(0).wait()
        hop(batch, phase)

    begin(LATE)
    begin(EARLY)
    begin(GATE)
    launch(OUT, 0)
    length = lengths[ids[0]]

    def live(width):
        return (lax.broadcasted_iota(jnp.int32, (TOK, width), 0) < length).astype(full)

    m_ref[...] = jnp.zeros_like(m_ref)
    for j in range(D // 128):
        x = tokens[:, j * 128 : j * 128 + 128].astype(full)
        m_ref[...] += x * x
    token_scale = lax.rsqrt(row_sum(m_ref[...]) / D + eps)
    owner = lax.broadcasted_iota(jnp.int32, (128, INNER), 1) >> 6
    repeats = (lax.broadcasted_iota(jnp.int32, (128, INNER), 0) == owner).astype(full)
    skip[...] = dot(params[8:16, :], repeats, precision=highest)[2:3]
    heads = params[8:16, :]
    launch(LATE, 1)
    launch(EARLY, 1)
    launch(LATE, 2)
    launch(GATE, 1)
    launch(EARLY, 2)
    launch(OUT, 1)

    def slot_of(slot):
        if slot < 2:
            return work.reshape(4, 4, 2, 4, 16, 512).at[pl.ds(2 * slot, 2)]
        return inner_t.reshape(2, 4, 2, 4, 2, 16, 512).at[:, :, :, :, slot - 2]

    def fetched(slot, start, width):
        source = full_in.at[:, :, :, :, :, pl.ds(start, width)]
        return pltpu.make_async_copy(source, slot_of(slot).at[:, :, :, :, :, pl.ds(0, width)], local_sem.at[3 + slot])

    def fetch(i):
        fetched(i % 4, *TILES[i]).start()

    def weight(i):
        slot, width = i % 4, TILES[i][1]
        fetched(slot, *TILES[i]).wait()
        if slot < 2:
            return work[pl.ds(CHIPS * slot, CHIPS), :, :width].reshape(D, width)
        return inner_t[:, slot - 2, :, :width].reshape(D, width)

    give(LATE)
    launch(GATE, 2)
    taken(LATE)
    fetch(1)
    fetch(0)
    late = weight(1)
    packed = late[:, 128:]

    def spread(r, base, count, each):
        pick = (
            lax.broadcasted_iota(jnp.int32, (128, D), 0) * 8 + r == lax.broadcasted_iota(jnp.int32, (128, D), 1)
        ).astype(low)
        shared = dot(pick, packed).astype(low)
        line = lax.broadcasted_iota(jnp.int32, (128, count), 0).astype(full)
        spot = lax.broadcasted_iota(jnp.int32, (128, count), 1).astype(full) + base
        owner = jnp.floor((spot + 0.5) * (1.0 / each))
        found = dot(shared, (line == spot - owner * each).astype(low))
        return col_sum(jnp.where(line == owner, found, 0.0))

    norm_gain[...] = spread(0, 0, D, 8)
    for j in range(D // 128):
        cols = slice(j * 128, j * 128 + 128)
        value = (tokens[:, cols].astype(full) * token_scale * norm_gain[:, cols]).astype(low)
        normed[:, cols] = value
        normed_t[j * 8 : j * 8 + 8] = value.T.reshape(8, 16, TOK)

    def project(i, weights):
        start, width = TILES[i][0], weights.shape[1]
        proj[:, start : start + width] = dot(normed[...], weights)

    def convolve(begin, end):
        @pl.loop(begin, end)
        def _(j):
            cols = tile(j)
            x = proj[:, tile(j, INNER)]
            pre = taps[4:5, cols] + taps[3:4, cols] * x
            for step in (1, 2, 3):
                pre = pre + taps[3 - step : 4 - step, cols] * rolled_down(x, step)
            sig = jax.nn.sigmoid(pre)
            act[:, cols] = (pre * sig).astype(low)
            dsilu[:, cols] = (sig * (1.0 + pre * (1.0 - sig))).astype(low)

    project(1, late[:, :128])
    project(0, weight(0))
    taps[...] = jnp.zeros_like(taps)
    for base in (0, XBC // 2):
        for k in range(CONV + 1):
            taps[k : k + 1, base : base + XBC // 2] = spread((3, 4, 5, 6, 2)[k], base, XBC // 2, 18)
    give(EARLY)
    convolve(SPLIT, XBC // 128)

    raw = proj[:, INNER + XBC : INNER + XBC + 128] + heads[0:1, :]
    grown = jnp.exp(-jnp.abs(raw))
    more = 1.0 + grown
    logged = jnp.where(more == 1.0, grown, jnp.log(more) * grown / jnp.where(more == 1.0, 1.0, more - 1.0))
    steps = jnp.where(lane < HEADS, jnp.maximum(raw, 0.0) + logged, 0.0)
    rate = -jnp.exp(heads[1:2, :])

    def split(x):
        top = x.astype(low)
        middle = (x - top.astype(full)).astype(low)
        return top, middle, (x - top.astype(full) - middle.astype(full)).astype(low)

    def summed(mask, x):
        found = dot(jnp.where(mask, 1.0, 0.0).astype(low), jnp.concatenate(split(x), axis=1))
        return found[:, :128] + found[:, 128:256] + found[:, 256:]

    cum = summed(row >= column, steps * rate) * LOG2E
    step_ref[...] = steps
    key = cum - jnp.log2(jnp.maximum(steps, 1e-37))
    turned, key_turned = cum.T, key.T
    for head in range(HEADS):
        cum_t[head] = turned[head : head + 1]
        key_t[head] = key_turned[head : head + 1]

    def thirds(x):
        top, middle, rest = [part.astype(full) for part in split(jnp.where(lane < HEADS, x, 0.0))]
        return (top + pltpu.roll(middle, HEADS, axis=1) + pltpu.roll(rest, 2 * HEADS, axis=1)).astype(low)

    cum_parts[...] = thirds(cum)
    key_parts[...] = thirds(key)
    mixed = jnp.where(row >= column, dot_nt(act[:, INNER + STATE :], act[:, INNER : INNER + STATE]), 0.0)
    mix[...] = mixed
    mix_t[...] = mixed.T

    taken(EARLY)
    for i in (2, 3, 4):
        fetch(i)
    gain[...] = spread(1, 0, INNER, 16)
    fetch(5)
    launch(OUT, 2)
    for i in (2, 3):
        project(i, weight(i))
    give(GATE)
    for i in (4, 5):
        project(i, weight(i))
    convolve(0, 10)
    taken(GATE)
    for i in (6, 7, 8, 9):
        fetch(i)
    convolve(10, SPLIT)
    for i in (6, 7, 8, 9):
        project(i, weight(i))
    give(OUT)
    q_ref[...] = jnp.zeros_like(q_ref)
    dcum_ref[...] = jnp.zeros_like(dcum_ref)
    dstep_ref[...] = jnp.zeros_like(dstep_ref)

    causal = lax.broadcasted_iota(jnp.int32, (128, 128), 0) >= lax.broadcasted_iota(jnp.int32, (128, 128), 1)

    anti = lax.broadcasted_iota(jnp.int32, (128, 128), 0) <= lax.broadcasted_iota(jnp.int32, (128, 128), 1)

    def spread_heads(parts, j):
        line = lax.broadcasted_iota(jnp.int32, (128, 256), 0)
        head = 2 * j + (lax.broadcasted_iota(jnp.int32, (128, 256), 1) >> 7)
        return dot(parts[...], jnp.where(((line & 31) == head) & (line < 96), 1.0, 0.0).astype(low))

    @pl.loop(0, HEADS // 2)
    def _(j):
        cols = tile(j)
        cums = spread_heads(cum_parts, j)
        values = act[:, cols]
        for block in range(TOK // 128):
            start, last = block * 128, block * 128 + 128
            halves = []
            for e in (0, 1):
                pieces = []
                for past in range(block + 1):
                    span = slice(past * 128, past * 128 + 128)
                    gap = cums[start:last, e * 128 : e * 128 + 128] - key_t[2 * j + e, :, span]
                    if past == block:
                        gap = jnp.where(causal, gap, -1e30)
                    pieces.append((mix[start:last, span] * jnp.exp2(gap)).astype(low))
                halves.append(jnp.concatenate(pieces, axis=1))
            found = dot(jnp.concatenate(halves, axis=0), values[:last])
            y = jnp.where(left[:128], found[:128], found[128:]) + skip[:, cols] * values[start:last].astype(full)
            y_ref[start:last, cols] = y
            gate = proj[start:last, cols]
            gated = y * gate * jax.nn.sigmoid(gate)
            q_ref[start:last] += gated * gated

    q_ref[...] = jnp.broadcast_to(lax.rsqrt(row_sum(q_ref[...]) / INNER + eps), (TOK, 128))
    mix[...] = jnp.zeros_like(mix)

    @pl.loop(0, INNER // 128)
    def _(j):
        cols = tile(j)
        gate = proj[:, cols]
        gated = y_ref[:, cols] * gate * jax.nn.sigmoid(gate)
        value = (gated * q_ref[...] * gain[:, cols]).astype(low)
        dproj[:, cols] = value
        inner_t[pl.ds(4 * j, 4)] = value.T.reshape(4, 2, 16, TOK)

    for j in range(D // 128):
        cols = slice(j * 128, j * 128 + 128)
        normed[:, cols] = (live(128) * cotangent[:, cols].astype(full)).astype(low)

    def grads(batch, group, side, half):
        start = PARTS[batch][group[0]][0]
        width = sum(PARTS[batch][part][1] for part in group)
        if batch == OUT:
            lhs = inner_t[pl.ds(32 * half, 32), side].reshape(TOK, TOK)
            rhs = normed[:, start : start + width]
        else:
            lhs = normed_t[pl.ds(32 * half, 32)].reshape(TOK, TOK)
            rhs = dproj[:, pl.ds(pl.multiple_of(BASE[batch] + start + side * WIDTH[batch], 128), width)]
        value = dot(lhs, rhs)
        return [(part, PARTS[batch][part][0] - start, PARTS[batch][part][1], value) for part in group]

    def spot_of(part, half, m):
        spot = {"y": 2 * half + (m // 4) % 2, "z": m // 8, "x": m % 4}
        axes = ORDERS[part]
        return spot[axes[2]] * 16 + spot[axes[1]] * 4 + spot[axes[0]]

    users = [[], []]

    def rs_free():
        for gone in users:
            while gone:
                rs_pass_copy(*gone.pop()).wait_send()

    def rs_give(batch):
        for group, slot in GROUPS[batch]:
            while users[slot]:
                rs_pass_copy(*users[slot].pop()).wait_send()
            origin = PARTS[batch][group[0]][0]
            for half in (0, 1):
                for part, offset, width, value in grads(batch, group, 1 - core, half):
                    value = value[:, offset : offset + width].astype(low)
                    for m in range(32):
                        work[CHIPS * slot + spot_of(part, half, m), :, offset : offset + width] = value[
                            16 * m : 16 * m + 16
                        ]
            for part in group:
                offset = PARTS[batch][part][0] - origin
                users[slot].append((batch, part, slot, offset))
                rs_pass_copy(batch, part, slot, offset).start()

    def rs_pass_copy(batch, part, slot=0, offset=0):
        width = PARTS[batch][part][1]
        sem = batch * 3 + part
        return remote(
            work.at[pl.ds(CHIPS * slot, CHIPS), :, pl.ds(offset, width)],
            part0.at[:, :, lanes_of(batch, part)],
            rs_pass.at[sem],
            rs_got.at[batch],
            sibling,
        )

    def lanes_of(batch, part):
        start, width = PARTS[batch][part]
        return pl.ds(LOCAL[batch] + start, width)

    def rs_copies(batch, part, stage):
        lanes = lanes_of(batch, part)
        axis = ORDERS[part][3 - stage]
        copies = []
        for step in (1, 2, 3):
            peer = moved(at, axis, step)
            there, slot = peer[axis], pl.ds(step - 1, 1)
            if stage == 1:
                source, target = part0.at[pl.ds(there * 16, 16), :, lanes], recv1.at[pl.ds(16 * step - 16, 16), :, lanes]
            elif stage == 2:
                source, target = part1.at[pl.ds(there * 4, 4), :, lanes], recv2.at[pl.ds(4 * step - 4, 4), :, lanes]
            else:
                source, target = part2.at[pl.ds(there, 1), :, lanes], recv3.at[slot, :, lanes]
            sem = batch * 3 + stage - 1
            copies.append(remote(source, target, rs_send.at[sem], rs_recv.at[sem], peer))
        return copies

    def rs_hop(batch, part, stage):
        for copy in rs_copies(batch, part, stage):
            copy.start()

    def rs_wait(batch, stage, sems):
        lanes = pl.ds(LOCAL[batch], WIDTH[batch])
        every = (recv1, recv2, recv3)[stage - 1].at[:, :, lanes]
        pltpu.make_async_copy(every, every, sems.at[batch * 3 + stage - 1]).wait()

    def rs_own(batch):
        lanes = pl.ds(LOCAL[batch], WIDTH[batch])
        every = part0.at[:, :, lanes]
        pltpu.make_async_copy(every, every, rs_got.at[batch]).wait()
        for group, _ in GROUPS[batch]:
            for half in (0, 1):
                for part, offset, width, value in grads(batch, group, core, half):
                    lanes = lanes_of(batch, part)
                    for m in range(32):
                        now = pl.ds(spot_of(part, half, m), 1)
                        piece = value[16 * m : 16 * m + 16, offset : offset + width][None]
                        part0[now, :, lanes] = (piece + part0[now, :, lanes].astype(full)).astype(low)
            for part in group:
                rs_hop(batch, part, 1)

    def part_one(batch, part):
        lanes = lanes_of(batch, part)
        mine = at[ORDERS[part][2]] * 16
        for i in range(16):
            now = pl.ds(i, 1)
            value = part0[pl.ds(mine + i, 1), :, lanes].astype(full)
            for k in range(3):
                value = value + recv1[pl.ds(16 * k + i, 1), :, lanes].astype(full)
            part1[now, :, lanes] = value.astype(low)
        rs_hop(batch, part, 2)

    def part_two(batch, part):
        lanes = lanes_of(batch, part)
        mine = at[ORDERS[part][1]] * 4
        for i in range(4):
            now = pl.ds(i, 1)
            value = part1[pl.ds(mine + i, 1), :, lanes].astype(full)
            for k in range(3):
                value = value + recv2[pl.ds(4 * k + i, 1), :, lanes].astype(full)
            part2[now, :, lanes] = value.astype(low)
        rs_hop(batch, part, 3)

    def part_three(batch, part):
        lanes = lanes_of(batch, part)
        value = part2[pl.ds(at[ORDERS[part][0]], 1), :, lanes].astype(full)
        for k in range(3):
            value = value + recv3[pl.ds(k, 1), :, lanes].astype(full)
        value = value[0]
        start, width = PARTS[batch][part]
        if batch == OUT:
            go_out[:, start : start + width] = value
            return
        base = BASE[batch]
        at_column = pl.multiple_of(base + core * WIDTH[batch] + start, 128)
        gi_out[:, pl.ds(at_column, width)] = jnp.where(first, value[:8], value[8:])
        swap_from[:, pl.ds(base // 2 + start, width)] = jnp.where(first, value[8:], value[:8])

    rs_give(OUT)
    taken(OUT)
    while drained:
        wait_bytes(*drained.pop())
    wout = full_out.reshape(INNER, D)

    m_ref[...] = jnp.zeros_like(m_ref)

    @pl.loop(0, D // 256)
    def _(j):
        cols = tile(j, 0, 256)
        branch = dot(dproj[:, :INNER], wout[:, cols])
        block_out[:, cols] = (tokens[:, cols].astype(full) + live(256) * branch).astype(low)
        shares = normed[:, cols].astype(full) * branch
        m_ref[...] += shares[:, :128] + shares[:, 128:]

    outputs = [pltpu.make_async_copy(block_out, block_out_hbm, edge_sem.at[5])]
    outputs[0].start()

    m_ref[...] = jnp.broadcast_to(row_sum(m_ref[...]) / INNER, (TOK, 128))

    @pl.loop(0, INNER // 256)
    def _(j):
        wide = tile(j, 0, 256)
        sums = [jnp.zeros((1, 128), full)] * 2
        for rows in (slice(0, 256), slice(256, 512)):
            value = dot_nt(normed[rows, :], wout[wide, :])
            for half in (0, 1):
                cols = tile(2 * j + half)
                inside = value[:, half * 128 : half * 128 + 128]
                y, gate, q = y_ref[rows, cols], proj[rows, cols], q_ref[rows, :]
                sig = jax.nn.sigmoid(gate)
                silu = gate * sig
                u = y * silu * q
                sums[half] = sums[half] + col_sum(inside * u)
                dgated = q * (inside * gain[:, cols] - u * m_ref[rows, :])
                dproj[rows, cols] = (dgated * y * (sig + silu * (1.0 - sig))).astype(low)
                dinner[rows, cols] = dgated * silu
        for half in (0, 1):
            small_now[5:6, tile(2 * j + half)] = sums[half]

    rs_own(OUT)

    rs_give(GATE)

    dnormed = proj.at[:, pl.ds(0, D)]

    def back_load(i):
        fetched(2 + i % 2, *BACK_TILES[i]).start()

    def back_tile(i):
        start, width = BACK_TILES[i]
        fetched(2 + i % 2, start, width).wait()
        value = dot_nt(dproj[:, start : start + width], inner_t[:, i % 2, :, :width].reshape(D, width))
        dnormed[...] = value if i == 0 else dnormed[...] + value
        if i + 2 < len(BACK_TILES):
            back_load(i + 2)

    back_load(0)
    back_load(1)

    def conv_back(dact, j):
        cols = tile(j)
        x = proj[:, tile(j, INNER)]
        dpre = dact * dsilu[:, cols].astype(full)
        small_now[4:5, cols] = col_sum(dpre)
        small_now[3:4, cols] = col_sum(dpre * x)
        dx = taps[3:4, cols] * dpre
        for step in (1, 2, 3):
            moved_up = rolled_up(dpre, step)
            small_now[3 - step : 4 - step, cols] = col_sum(moved_up * x)
            dx = dx + taps[3 - step : 4 - step, cols] * moved_up
        dproj[:, tile(j, INNER)] = dx.astype(low)

    def rs_one(batch):
        rs_wait(batch, 1, rs_recv)
        for part in range(3):
            part_one(batch, part)

    def rs_two(batch):
        rs_wait(batch, 2, rs_recv)
        for part in range(3):
            part_two(batch, part)

    def rs_three(batch):
        rs_wait(batch, 3, rs_recv)
        for part in range(3):
            part_three(batch, part)

    back_ref[...] = jnp.zeros_like(back_ref)

    def settle(j):
        cols = tile(j)
        values, dy, back = act[:, cols].astype(full), dinner[:, cols], back_ref[...]
        direct = values * back
        crossing = dy.astype(low).astype(full) * (y_ref[:, cols] - skip[:, cols] * values) - direct
        small_now[7:8, cols] = col_sum(dy * values)
        for e in (0, 1):
            mine = left if e == 0 else jnp.logical_not(left)
            spot = lane == 2 * j + e
            dcum_ref[...] = jnp.where(spot, row_sum(jnp.where(mine, crossing, 0.0)), dcum_ref[...])
            dstep_ref[...] = jnp.where(spot, row_sum(jnp.where(mine, direct, 0.0)), dstep_ref[...])
        conv_back(back + skip[:, cols] * dy, j)

    @pl.loop(0, HEADS // 4 + 1)
    def _(run):
        for turn, events in PLAN:

            @pl.when(run == turn)
            def _(events=events):
                for action, what in events:
                    if action == "dn":
                        back_tile(what)
                    else:
                        {"give": rs_give, "own": rs_own, "one": rs_one, "two": rs_two}[action](what)

        @pl.loop(jnp.maximum(2 * run - 1, 0), jnp.minimum(2 * run + 1, HEADS // 2))
        def _(j):
            settle(jnp.maximum(j - 1, 0))
            cols = tile(j)
            keys = spread_heads(key_parts, j)
            v_low = act[:, cols]
            dy_low = dinner[:, cols].astype(low)
            own = (jnp.where(left, v_low, jnp.zeros_like(v_low)), jnp.where(left, jnp.zeros_like(v_low), v_low))
            found = []
            for block in range(TOK // 128):
                start, last = block * 128, block * 128 + 128
                both = dot_nt(jnp.concatenate([own[0][start:last], own[1][start:last]], axis=0), dy_low[start:])
                halves = []
                total = None
                for e in (0, 1):
                    pieces, shares = [], []
                    for later in range(block, TOK // 128):
                        span = slice(later * 128, later * 128 + 128)
                        gap = cum_t[2 * j + e, :, span] - keys[start:last, e * 128 : e * 128 + 128]
                        if later == block:
                            gap = jnp.where(anti, gap, -1e30)
                        decay = jnp.exp2(gap)
                        pieces.append((mix_t[start:last, span] * decay).astype(low))
                        inside = slice((later - block) * 128, (later - block + 1) * 128)
                        shares.append(both[e * 128 : e * 128 + 128, inside] * decay)
                    halves.append(jnp.concatenate(pieces, axis=1))
                    share = jnp.concatenate(shares, axis=1)
                    total = share if total is None else total + share
                mix[start:last, start:] += total
                given_back = dot(jnp.concatenate(halves, axis=0), dy_low[start:])
                found.append(jnp.where(left[:128], given_back[:128], given_back[128:]))
            for block, value in enumerate(found):
                back_ref[block * 128 : block * 128 + 128] = value

    settle(HEADS // 2 - 1)
    rs_own(MID)
    masked = jnp.where(row <= column, mix[...], 0.0)
    conv_back(dot(masked.astype(low), act[:, INNER + STATE :]), INNER // 128)
    conv_back(dot(masked.T.astype(low), act[:, INNER : INNER + STATE]), INNER // 128 + 1)
    dacc = summed(row <= column, dcum_ref[...])
    sig = jax.nn.sigmoid(proj[:, INNER + XBC : INNER + XBC + 128] + heads[0:1, :])
    steps = step_ref[...]
    ratio = jnp.where(steps > 1e-30, sig / jnp.maximum(steps, 1e-30), 1.0)
    draw = jnp.where(lane < HEADS, dstep_ref[...] * ratio + dacc * rate * sig, 0.0)
    dproj[:, INNER + XBC : INNER + XBC + 128] = draw.astype(low)
    dproj[:, INNER + XBC + 128 :] = jnp.zeros((TOK, 128), low)
    small_now[6:7, :] = jnp.zeros((1, XBC), full)
    small_now[6:7, :128] = col_sum(draw)
    small_now[6:7, 128:256] = rate * col_sum(dacc * steps)
    small_now[5:6, INNER:] = jnp.zeros((1, XBC - INNER), full)
    small_now[7:8, INNER:] = jnp.zeros((1, XBC - INNER), full)


    def small_swap():
        away = pl.ds(pl.multiple_of((1 - core) * HALF, 128), HALF)
        return remote(small_now.at[:, away], small_other, small_send.at[0], small_recv.at[0], sibling)

    def small_copies(stage):
        made = []
        for part in range(3):
            lanes = pl.ds(part * THIRD, THIRD)
            axis = ORDERS[part][stage - 1]
            for step in (1, 2, 3):
                slot = (stage - 1) * 3 + step - 1
                made.append(
                    remote(
                        small_half.at[stage - 1, :, lanes],
                        small_got.at[slot, :, lanes],
                        small_send.at[stage],
                        small_recv.at[stage],
                        moved(at, axis, step),
                    )
                )
        return made

    def small_back():
        return remote(small_half.at[3], small_last, small_send.at[4], small_recv.at[4], sibling)

    def small_wait(stage, sems):
        if stage in (0, 4):
            sems_of = small_other if stage == 0 else small_last
            pltpu.make_async_copy(sems_of, sems_of, sems.at[stage]).wait()
        else:
            every = small_got.at[pl.ds((stage - 1) * 3, 3)]
            pltpu.make_async_copy(every, every, sems.at[stage]).wait()

    def small_add(stage):
        small_wait(stage, small_recv)
        if stage == 0:
            mine = pl.ds(pl.multiple_of(core * HALF, 128), HALF)
            small_half[0] = small_now[:, mine] + small_other[...]
        else:
            value = small_half[stage - 1]
            for k in range(3):
                value = value + small_got[(stage - 1) * 3 + k]
            small_half[stage] = value
        for copy in small_copies(stage + 1) if stage < 3 else [small_back()]:
            copy.start()

    def norm_start(stage):
        for step in (1,) if stage == 0 else (1, 2, 3):
            slot = 0 if stage == 0 else stage * 3 - 3 + step
            peer = moved(at, "cxyz"[stage], step)
            remote(norm_now.at[stage], norm_got.at[slot], norm_send.at[stage], norm_recv.at[stage], peer).start()

    def norm_wait(stage, sems):
        every = norm_got.at[pl.ds(0, 1)] if stage == 0 else norm_got.at[pl.ds(stage * 3 - 2, 3)]
        pltpu.make_async_copy(every, every, sems.at[stage]).wait()

    def norm_add(stage):
        norm_wait(stage, norm_recv)
        value = norm_now[stage]
        for k in range(1 if stage == 0 else 3):
            value = value + norm_got[0 if stage == 0 else stage * 3 - 2 + k]
        if stage == 3:
            norm_out[...] = value
        else:
            norm_now[stage + 1] = value
            norm_start(stage + 1)

    small_swap().start()
    rs_give(LATE)
    back_tile(7)
    small_add(0)
    back_tile(8)
    back_tile(9)
    rs_own(LATE)
    rs_two(GATE)
    m_ref[...] = jnp.zeros_like(m_ref)
    for j in range(D // 128):
        cols = slice(j * 128, j * 128 + 128)
        u = tokens[:, cols].astype(full) * token_scale
        du = dnormed[:, cols] * u
        norm_now[0, j : j + 1, :] = col_sum(du)
        m_ref[...] += du * norm_gain[:, cols]
    mean = row_sum(m_ref[...]) / D
    norm_start(0)
    small_add(1)
    rs_one(EARLY)
    rs_one(MID)
    for j in range(D // 128):
        cols = slice(j * 128, j * 128 + 128)
        u = tokens[:, cols].astype(full) * token_scale
        du = dnormed[:, cols] * norm_gain[:, cols]
        normed[:, cols] = (cotangent[:, cols].astype(full) + token_scale * (du - u * mean)).astype(low)
    final = pltpu.make_async_copy(normed, input_grad, local_sem.at[0])
    final.start()
    norm_add(0)
    rs_three(OUT)
    small_add(2)
    rs_one(LATE)
    rs_three(GATE)
    for batch in (OUT, GATE):
        for stage in (1, 2, 3):
            rs_wait(batch, stage, rs_send)
    norm_add(1)
    rs_two(EARLY)
    rs_two(MID)
    small_add(3)
    rs_two(LATE)
    norm_add(2)
    rs_three(EARLY)
    rs_three(MID)
    small_wait(4, small_recv)
    mine = pl.ds(pl.multiple_of(core * HALF, 128), HALF)
    small_out[:, mine] = small_half[3]
    small_out[:, pl.ds(pl.multiple_of((1 - core) * HALF, 128), HALF)] = small_last[...]
    outputs.append(pltpu.make_async_copy(small_out, small_hbm, edge_sem.at[6]))
    outputs.append(pltpu.make_async_copy(go_out, go_hbm, edge_sem.at[7]))
    for copy in outputs[1:]:
        copy.start()
    rs_free()
    for stage in range(5):
        small_wait(stage, small_send)
    for batch in (EARLY, MID):
        for stage in (1, 2, 3):
            rs_wait(batch, stage, rs_send)
    rs_three(LATE)
    last = remote(swap_from, swap_to, swap_sem.at[2], swap_sem.at[3], sibling)
    last.start()
    norm_add(3)
    outputs.append(pltpu.make_async_copy(norm_out, norm_hbm, edge_sem.at[8]))
    outputs[3].start()
    for stage in range(4):
        norm_wait(stage, norm_send)
    for stage in (1, 2, 3):
        rs_wait(LATE, stage, rs_send)
    final.wait()
    last.wait()
    for batch in (GATE, EARLY, MID, LATE):
        base, width = BASE[batch], WIDTH[batch]
        lanes = pl.ds(pl.multiple_of(base + (1 - core) * width, 128), width)
        gi_out[:, lanes] = swap_to[:, base // 2 : base // 2 + width]
    outputs.append(pltpu.make_async_copy(gi_out, gi_hbm, edge_sem.at[9]))
    outputs[4].start()
    for copy in outputs:
        copy.wait()


def block(lengths, ids, in_shard, wo, tokens, cotangent, params):
    full, low = jnp.float32, jnp.bfloat16
    anywhere = pl.BlockSpec(memory_space=pl.ANY)
    sems = pltpu.SemaphoreType.DMA
    return pl.pallas_call(
        block_kernel,
        out_shape=(
            jax.ShapeDtypeStruct((TOK, D), low),
            jax.ShapeDtypeStruct((TOK, D), low),
            jax.ShapeDtypeStruct((8, COLS), full),
            jax.ShapeDtypeStruct((16, D), full),
            jax.ShapeDtypeStruct((8, XBC), full),
            jax.ShapeDtypeStruct((8, 128), full),
            jax.ShapeDtypeStruct((2, 4, 2, 4, 16, COLS), low),
        ),
        in_specs=[pl.BlockSpec(memory_space=pltpu.SMEM)] * 2 + [anywhere] * 5,
        out_specs=[anywhere] * 7,
        scratch_shapes=[
            pltpu.VMEM((8, PROJ), low),
            pltpu.VMEM((16, D), low),
            pltpu.VMEM((TOK, D), low),
            pltpu.VMEM((TOK, D), low),
            pltpu.VMEM((16, 128), full),
            pltpu.VMEM((TOK, D), low),
            pltpu.VMEM((8, COLS), full),
            pltpu.VMEM((16, D), full),
            pltpu.VMEM((8, XBC), full),
            pltpu.VMEM((8, 128), full),
            pltpu.VMEM((8, COLS), full),
            pltpu.VMEM((8, COLS), full),
            pltpu.VMEM((16, XBC), low),
            pltpu.VMEM((1, INNER), full),
            pltpu.VMEM((2, 4, 2, 4, 2, 16, D), low),
            pltpu.VMEM((2 * CHIPS, 16, 512), low),
            pltpu.VMEM((TOK, COLS - 128), full),
            pltpu.VMEM((TOK, XBC), low),
            pltpu.VMEM((TOK, XBC), low),
            pltpu.VMEM((TOK, INNER), full),
            pltpu.VMEM((TOK, INNER), full),
            pltpu.VMEM((TOK, COLS), low),
            pltpu.VMEM((CHIPS, 2, 16, TOK), low),
            pltpu.VMEM((TOK, D), low),
            pltpu.VMEM((CHIPS, 16, TOK), low),
            pltpu.VMEM((TOK, TOK), full),
            pltpu.VMEM((TOK, TOK), full),
            pltpu.VMEM((TOK, 128), low),
            pltpu.VMEM((TOK, 128), low),
            pltpu.VMEM((HEADS, 1, TOK), full),
            pltpu.VMEM((HEADS, 1, TOK), full),
            pltpu.VMEM((TOK, 128), full),
            pltpu.VMEM((TOK, 128), full),
            pltpu.VMEM((TOK, 128), full),
            pltpu.VMEM((TOK, 128), full),
            pltpu.VMEM((TOK, 128), full),
            pltpu.VMEM((TOK, 128), full),
            pltpu.VMEM((8, XBC), full),
            pltpu.VMEM((1, INNER), full),
            pltpu.VMEM((1, D), full),
            pltpu.VMEM((CHIPS, 16, SIDE), low),
            pltpu.VMEM((48, 16, SIDE), low),
            pltpu.VMEM((16, 16, SIDE), low),
            pltpu.VMEM((12, 16, SIDE), low),
            pltpu.VMEM((4, 16, SIDE), low),
            pltpu.VMEM((3, 16, SIDE), low),
            pltpu.VMEM((8, XBC), full),
            pltpu.VMEM((8, XBC), full),
            pltpu.VMEM((8, XBC), full),
            pltpu.VMEM((8, HALF), full),
            pltpu.VMEM((4, 8, HALF), full),
            pltpu.VMEM((9, 8, HALF), full),
            pltpu.VMEM((8, HALF), full),
            pltpu.VMEM((4, 8, 128), full),
            pltpu.VMEM((10, 8, 128), full),
            sems((4,)),
            sems((7,)),
            sems((10,)),
            sems((15,)),
            sems((15,)),
            sems((5,)),
            sems((5,)),
            sems((15,)),
            sems((15,)),
            sems((15,)),
            sems((5,)),
            sems((5,)),
            sems((5,)),
            sems((4,)),
            sems((4,)),
        ],
        compiler_params=pltpu.CompilerParams(collective_id=0, has_side_effects=True, vmem_limit_bytes=63 << 20),
    )(lengths, ids, in_shard, wo, tokens, cotangent, params)


def finish_kernel(
    out_in,
    grad_in,
    gi_in,
    go_in,
    small_in,
    norm_in,
    out_hbm,
    grad_hbm,
    gain_hbm,
    gi_hbm,
    conv_hbm,
    bias_hbm,
    dt_hbm,
    log_hbm,
    skip_hbm,
    inner_hbm,
    go_hbm,
    small,
    norm,
    gi,
    go,
    out,
    grad,
    gain_out,
    gi_out,
    conv_out,
    bias_out,
    dt_out,
    log_out,
    skip_out,
    inner_out,
    sem,
):
    pairs = ((small_in, small), (norm_in, norm), (gi_in, gi), (go_in, go), (out_in, out), (grad_in, grad))
    copies = [pltpu.make_async_copy(source, target, sem.at[i]) for i, (source, target) in enumerate(pairs)]
    for copy in copies:
        copy.start()
    writes = []

    def write(source, target):
        writes.append(pltpu.make_async_copy(source, target, sem.at[len(copies) + len(writes)]))
        writes[-1].start()

    me = lax.axis_index("dp") * 16 + lax.axis_index("fsdp")
    copies[0].wait()

    def from_lane(count):
        return pltpu.roll(small[...], lax.rem(XBC - count * me, XBC), axis=1)

    conv = from_lane(18)
    conv_out[...] = conv[:CONV, :18]
    write(conv_out, conv_hbm)
    bias_out[...] = conv[CONV : CONV + 1, :18]
    write(bias_out, bias_hbm)
    inner_out[...] = from_lane(16)[5:6, :16]
    write(inner_out, inner_hbm)
    dt_out[...] = small[6:7, :HEADS]
    write(dt_out, dt_hbm)
    log_out[...] = small[6:7, 128 : 128 + HEADS]
    write(log_out, log_hbm)
    copies[4].wait()
    write(out, out_hbm)
    copies[5].wait()
    write(grad, grad_hbm)
    copies[2].wait()
    gi_out[...] = gi[:, :PROJ]
    write(gi_out, gi_hbm)
    copies[3].wait()
    write(go, go_hbm)
    owner = lax.broadcasted_iota(jnp.int32, (INNER, 128), 0) >> 6
    sums = (owner == lax.broadcasted_iota(jnp.int32, (INNER, 128), 1)).astype(jnp.float32)
    skip_out[...] = dot(small[:, :INNER], sums, precision=highest)[7:8, :HEADS]
    write(skip_out, skip_hbm)
    copies[1].wait()
    line = lax.broadcasted_iota(jnp.int32, (8, 128), 0)
    row = jnp.sum(jnp.where(line == me // 16, norm[...], 0.0), axis=0, keepdims=True)
    gain_out[...] = pltpu.roll(row, lax.rem(128 - 8 * lax.rem(me, 16), 128), axis=1)[:, :8]
    write(gain_out, gain_hbm)
    for copy in writes:
        copy.wait()


def finish(out, grad, gi, go, small, norm):
    full = jnp.float32
    anywhere = pl.BlockSpec(memory_space=pl.ANY)
    rest = [(CONV, 18), (1, 18), (1, HEADS), (1, HEADS), (1, HEADS), (1, 16)]
    shapes = [(1, 8), (8, PROJ)] + rest
    return pl.pallas_call(
        finish_kernel,
        out_shape=[jax.ShapeDtypeStruct(out.shape, out.dtype)] * 2
        + [jax.ShapeDtypeStruct(shape, full) for shape in shapes + [(16, D)]],
        in_specs=[anywhere] * 6,
        out_specs=[anywhere] * 11,
        scratch_shapes=[
            pltpu.VMEM(small.shape, full),
            pltpu.VMEM(norm.shape, full),
            pltpu.VMEM(gi.shape, full),
            pltpu.VMEM(go.shape, full),
            pltpu.VMEM(out.shape, out.dtype),
            pltpu.VMEM(out.shape, out.dtype),
        ]
        + [pltpu.VMEM(shape, full) for shape in shapes]
        + [pltpu.SemaphoreType.DMA((17,))],
        compiler_params=pltpu.CompilerParams(vmem_limit_bytes=62 << 20),
    )(out, grad, gi, go, small, norm)


def body(
    tokens,
    lengths,
    placement_ids,
    norm_gain,
    in_weight,
    conv_weight,
    conv_bias,
    dt_bias,
    a_log,
    d_skip,
    inner_gain,
    out_weight,
    cotangent,
):
    full = jnp.float32

    def line(values, first):
        values = values.astype(full).reshape(-1, values.shape[-1])
        rows, lanes = values.shape
        return jnp.pad(values, ((first, 16 - first - rows), (0, 128 - lanes)))

    params = (
        line(norm_gain, 0)
        + line(inner_gain, 1)
        + line(conv_bias, 2)
        + line(conv_weight, 3)
        + line(dt_bias, 8)
        + line(a_log, 9)
        + line(d_skip, 10)
    )
    block_out, input_grad, shard_in, shard_out, small, norm, _ = block(
        lengths, placement_ids, in_weight, out_weight, tokens, cotangent, params
    )
    found = finish(block_out, input_grad, shard_in, shard_out, small, norm)
    flat = [0, 0, 1, 0, 0, 1, 1, 1, 1, 1, 0]
    return tuple(value[0] if one else value for value, one in zip(found, flat))


def solution(mesh):
    placed = (
        P(("dp", "fsdp"), None),
        P(),
        P(("dp", "fsdp")),
        P(("dp", "fsdp")),
        P(("dp", "fsdp"), None),
        P(None, ("dp", "fsdp")),
        P(("dp", "fsdp")),
        P(),
        P(),
        P(),
        P(("dp", "fsdp")),
        P(("dp", "fsdp"), None),
        P(("dp", "fsdp"), None),
    )
    return jax.shard_map(
        body,
        mesh=mesh,
        in_specs=placed,
        out_specs=(
            P(("dp", "fsdp"), None),
            P(("dp", "fsdp"), None),
            P(("dp", "fsdp")),
            P(("dp", "fsdp"), None),
            P(None, ("dp", "fsdp")),
            P(("dp", "fsdp")),
            P(),
            P(),
            P(),
            P(("dp", "fsdp")),
            P(("dp", "fsdp"), None),
        ),
        check_vma=False,
    )
```

```python
import jax
import jax.numpy as jnp
import numpy as np
from jax import lax
from jax.experimental import pallas as pl
from jax.experimental.pallas import tpu as pltpu
from jax.sharding import PartitionSpec as P

D = 1024
INNER = 2048
STATE = 128
HEAD = 64
CONV = 4
HEADS = 32
XBC = 2304
PROJ = 4384
TOK = 512
CHIPS = 64
COLS = 4608
SIDE = 3328
HALF = 1152
THIRD = 384
MESH = pl.DeviceIdType.MESH
ORDERS = (("x", "y", "z"), ("y", "z", "x"), ("z", "x", "y"))
OUT, GATE, EARLY, MID, LATE = 0, 1, 2, 3, 4
GET_PARTS = {
    OUT: ((0, 384), (384, 384), (768, 256)),
    GATE: ((0, 384), (384, 384), (768, 256)),
    EARLY: ((0, 256), (256, 256), (512, 384)),
    LATE: ((0, 128), (128, 128), (256, 128)),
}
GET_BASE = {GATE: 0, EARLY: 2048, LATE: 3840}
GET_WIDTH = {OUT: 1024, GATE: 1024, EARLY: 896, LATE: 384}
SPLIT = 14
TILES = (
    (3840, 512),
    (4352, 256),
    (2048, 512),
    (2560, 512),
    (3072, 512),
    (3584, 256),
    (0, 512),
    (512, 512),
    (1024, 512),
    (1536, 512),
)
PARTS = {
    OUT: ((0, 512), (512, 256), (768, 256)),
    GATE: ((0, 256), (512, 512), (256, 256)),
    EARLY: ((0, 128), (128, 128), (256, 256)),
    MID: ((0, 128), (128, 128), (256, 128)),
    LATE: ((0, 128), (128, 128), (256, 128)),
}
GROUPS = {
    OUT: (((0,), 0), ((1, 2), 1)),
    GATE: (((0, 2), 0), ((1,), 1)),
    EARLY: (((0, 1, 2), 0),),
    MID: (((0, 1, 2), 1),),
    LATE: (((0, 1, 2), 0),),
}
LOCAL = {OUT: 0, GATE: 1024, EARLY: 2048, MID: 2560, LATE: 2944}
BASE = {GATE: 0, EARLY: 2048, MID: 3072, LATE: 3840}
WIDTH = {OUT: 1024, GATE: 1024, EARLY: 512, MID: 384, LATE: 384}
BACK_TILES = (
    (0, 512),
    (512, 512),
    (1024, 512),
    (1536, 512),
    (2048, 512),
    (2560, 512),
    (3072, 512),
    (3584, 256),
    (3840, 512),
    (4352, 256),
)

eps = 1e-05
LOG2E = 1.4426950408889634
highest = lax.Precision.HIGHEST

PLAN = (
    (1, (("dn", 0),)),
    (2, (("own", GATE), ("dn", 1))),
    (4, (("dn", 2), ("dn", 3), ("one", OUT))),
    (5, (("give", EARLY),)),
    (6, (("own", EARLY), ("dn", 4), ("one", GATE))),
    (7, (("dn", 5), ("two", OUT))),
    (8, (("give", MID), ("dn", 6))),
)


def place():
    dp, fsdp = lax.axis_index("dp"), lax.axis_index("fsdp")
    return {"x": (fsdp // 2) % 4, "y": (dp // 4) * 2 + fsdp // 8, "z": dp % 4, "c": fsdp % 2}


def device(at):
    y = at["y"]
    return ((y // 2) * 4 + at["z"], (y % 2) * 8 + at["x"] * 2 + at["c"])


def moved(at, axis, step):
    size = 2 if axis == "c" else 4
    return dict(at, **{axis: lax.rem(at[axis] + step, size)})


def greet(at):
    peers = [moved(at, axis, step) for axis in "xyz" for step in (1, 2, 3)] + [moved(at, "c", 1)]
    for peer in peers:
        pl.semaphore_signal(pltpu.get_barrier_semaphore(), inc=1, device_id=device(peer), device_id_type=MESH)


def meet():
    pl.semaphore_wait(pltpu.get_barrier_semaphore(), 10)


def remote(src, dst, send, recv, peer):
    return pltpu.make_async_remote_copy(
        src_ref=src, dst_ref=dst, send_sem=send, recv_sem=recv, device_id=device(peer), device_id_type=MESH
    )


def chips(at, full):
    every = slice(None)
    y, z, x = at["y"], at["z"], at["x"]
    return (
        every if "y" in full else y // 2,
        every if "z" in full else z,
        every if "y" in full else y % 2,
        every if "x" in full else x,
    )


def rolled_down(x, step):
    zeros = jnp.zeros((8, x.shape[1]), x.dtype)
    return pltpu.roll(jnp.concatenate([zeros, x], axis=0), step, axis=0)[8:]


def rolled_up(x, step):
    rows = x.shape[0]
    zeros = jnp.zeros((8, x.shape[1]), x.dtype)
    return pltpu.roll(jnp.concatenate([x, zeros], axis=0), rows + 8 - step, axis=0)[:rows]


def tile(j, base=0, size=128):
    return pl.ds(pl.multiple_of(base + j * size, 128), size)


def dot_nt(a, b):
    return lax.dot_general(a, b, (((1,), (1,)), ((), ())), preferred_element_type=jnp.float32)


def dot(a, b, **more):
    return jnp.dot(a, b, preferred_element_type=jnp.float32, **more)


def row_sum(x):
    return jnp.sum(x, axis=1, keepdims=True)


def col_sum(x):
    return jnp.sum(x, axis=0, keepdims=True)


def block_kernel(
    lengths,
    ids,
    in_shard_hbm,
    wo_hbm,
    tokens_hbm,
    cotangent_hbm,
    params_hbm,
    block_out_hbm,
    input_grad,
    gi_hbm,
    go_hbm,
    small_hbm,
    norm_hbm,
    full_in,
    in_shard,
    wo,
    tokens,
    cotangent,
    params,
    block_out,
    gi_out,
    go_out,
    small_out,
    norm_out,
    wi,
    other,
    blk,
    skip,
    full_out,
    work,
    proj,
    act,
    dsilu,
    y_ref,
    dinner,
    dproj,
    inner_t,
    normed,
    normed_t,
    mix,
    mix_t,
    cum_parts,
    key_parts,
    cum_t,
    key_t,
    step_ref,
    q_ref,
    m_ref,
    dcum_ref,
    dstep_ref,
    back_ref,
    taps,
    gain,
    norm_gain,
    part0,
    recv1,
    part1,
    recv2,
    part2,
    recv3,
    swap_from,
    swap_to,
    small_now,
    small_other,
    small_half,
    small_got,
    small_last,
    norm_now,
    norm_got,
    swap_sem,
    local_sem,
    edge_sem,
    ag_send,
    ag_recv,
    ag_pass,
    ag_got,
    rs_send,
    rs_recv,
    rs_pass,
    rs_got,
    small_send,
    small_recv,
    norm_send,
    norm_recv,
):
    low, full = jnp.bfloat16, jnp.float32
    at = place()
    core = at["c"]
    first = core == 0
    sibling = moved(at, "c", 1)
    here = chips(at, ())
    inputs = [
        pltpu.make_async_copy(source, target, edge_sem.at[i])
        for i, (source, target) in enumerate(
            (
                (in_shard_hbm, in_shard),
                (params_hbm, params),
                (tokens_hbm, tokens),
                (wo_hbm, wo),
                (cotangent_hbm, cotangent),
            )
        )
    ]
    for copy in inputs:
        copy.start()
    greet(at)

    lane = lax.broadcasted_iota(jnp.int32, (TOK, 128), 1)
    left = lane < HEAD
    row = lax.broadcasted_iota(jnp.int32, (TOK, TOK), 0)
    column = lax.broadcasted_iota(jnp.int32, (TOK, TOK), 1)
    for copy in inputs[:2]:
        copy.wait()
    wi[:, COLS - 256 :] = jnp.zeros((8, 256), full)
    wi[:, :PROJ] = in_shard[...].astype(full)
    wi[:, COLS - 128 :] = params[0:8, :]
    meet()

    swap = remote(wi, other, swap_sem.at[0], swap_sem.at[1], sibling)
    swap.start()
    for copy in inputs[2:]:
        copy.wait()
    full_out[here + (core,)] = wo[...]

    def held(batch, part, reach):
        start, width = GET_PARTS[batch][part]
        if batch == OUT:
            return full_out.at[chips(at, reach) + (core, slice(None), pl.ds(start, width))]
        spot = pl.multiple_of(core * GET_WIDTH[batch] + start + GET_BASE[batch], 128)
        return full_in.at[chips(at, reach) + (slice(None), pl.ds(spot, width))]

    def wait_bytes(blocks, width, sem):
        size = 512 if width % 512 == 0 else 128
        count = blocks * width // size
        if count > 2 * CHIPS:
            size, count = 512, blocks * width // 512
        shape = work.at[pl.ds(0, count), :, pl.ds(0, size)]
        pltpu.make_async_copy(shape, shape, sem).wait()

    drained = []

    def hop(batch, phase):
        slot = batch * 3 + phase
        for part in range(3):
            target = held(batch, part, ORDERS[part][:phase])
            source = target
            if phase == 0 and batch != OUT:
                start, width = GET_PARTS[batch][part]
                source = blk.at[:, pl.ds(GET_BASE[batch] // 2 + start, width)]
            for step in (1, 2, 3):
                peer = moved(at, ORDERS[part][phase], step)
                remote(source, target, ag_send.at[slot], ag_recv.at[slot], peer).start()
        drained.append((3 * 4**phase, GET_WIDTH[batch], ag_send.at[slot]))

    def landed(batch, phase):
        wait_bytes(3 * 4**phase, GET_WIDTH[batch], ag_recv.at[batch * 3 + phase])

    def give(batch):
        landed(batch, 2)
        for part in range(3):
            region = held(batch, part, "xyz")
            remote(region, region, ag_pass.at[batch], ag_got.at[batch], sibling).start()
        drained.append((CHIPS, GET_WIDTH[batch], ag_pass.at[batch]))

    def taken(batch):
        wait_bytes(CHIPS, GET_WIDTH[batch], ag_got.at[batch])

    swap.wait()
    stores = []

    def begin(batch):
        base, width = GET_BASE[batch], GET_WIDTH[batch]
        lanes = pl.ds(pl.multiple_of(base + core * width, 128), width)
        mine, theirs = wi[:, lanes], other[:, lanes]
        blk[:, base // 2 : base // 2 + width] = jnp.concatenate(
            [jnp.where(first, mine, theirs), jnp.where(first, theirs, mine)], axis=0
        ).astype(low)
        launch(batch, 0)
        copy = pltpu.make_async_copy(
            blk.at[:, pl.ds(base // 2, width)], full_in.at[here + (slice(None), lanes)], local_sem.at[len(stores)]
        )
        copy.start()
        stores.append(copy)

    def launch(batch, phase):
        if phase:
            landed(batch, phase - 1)
        if phase == 1 and batch != OUT:
            stores.pop(0).wait()
        hop(batch, phase)

    begin(LATE)
    begin(EARLY)
    begin(GATE)
    launch(OUT, 0)
    length = lengths[ids[0]]

    def live(width):
        return (lax.broadcasted_iota(jnp.int32, (TOK, width), 0) < length).astype(full)

    m_ref[...] = jnp.zeros_like(m_ref)
    for j in range(D // 128):
        x = tokens[:, j * 128 : j * 128 + 128].astype(full)
        m_ref[...] += x * x
    token_scale = lax.rsqrt(row_sum(m_ref[...]) / D + eps)
    owner = lax.broadcasted_iota(jnp.int32, (128, INNER), 1) >> 6
    repeats = (lax.broadcasted_iota(jnp.int32, (128, INNER), 0) == owner).astype(full)
    skip[...] = dot(params[8:16, :], repeats, precision=highest)[2:3]
    heads = params[8:16, :]
    launch(LATE, 1)
    launch(EARLY, 1)
    launch(LATE, 2)
    launch(GATE, 1)
    launch(EARLY, 2)
    launch(OUT, 1)

    def slot_of(slot):
        if slot < 2:
            return work.reshape(4, 4, 2, 4, 16, 512).at[pl.ds(2 * slot, 2)]
        return inner_t.reshape(2, 4, 2, 4, 2, 16, 512).at[:, :, :, :, slot - 2]

    def fetched(slot, start, width):
        source = full_in.at[:, :, :, :, :, pl.ds(start, width)]
        return pltpu.make_async_copy(source, slot_of(slot).at[:, :, :, :, :, pl.ds(0, width)], local_sem.at[3 + slot])

    def fetch(i):
        fetched(i % 4, *TILES[i]).start()

    def weight(i):
        slot, width = i % 4, TILES[i][1]
        fetched(slot, *TILES[i]).wait()
        if slot < 2:
            return work[pl.ds(CHIPS * slot, CHIPS), :, :width].reshape(D, width)
        return inner_t[:, slot - 2, :, :width].reshape(D, width)

    give(LATE)
    launch(GATE, 2)
    taken(LATE)
    fetch(1)
    fetch(0)
    late = weight(1)
    packed = late[:, 128:]

    def spread(r, base, count, each):
        pick = (
            lax.broadcasted_iota(jnp.int32, (128, D), 0) * 8 + r == lax.broadcasted_iota(jnp.int32, (128, D), 1)
        ).astype(low)
        shared = dot(pick, packed).astype(low)
        line = lax.broadcasted_iota(jnp.int32, (128, count), 0).astype(full)
        spot = lax.broadcasted_iota(jnp.int32, (128, count), 1).astype(full) + base
        owner = jnp.floor((spot + 0.5) * (1.0 / each))
        found = dot(shared, (line == spot - owner * each).astype(low))
        return col_sum(jnp.where(line == owner, found, 0.0))

    norm_gain[...] = spread(0, 0, D, 8)
    for j in range(D // 128):
        cols = slice(j * 128, j * 128 + 128)
        value = (tokens[:, cols].astype(full) * token_scale * norm_gain[:, cols]).astype(low)
        normed[:, cols] = value
        normed_t[j * 8 : j * 8 + 8] = value.T.reshape(8, 16, TOK)

    def project(i, weights):
        start, width = TILES[i][0], weights.shape[1]
        proj[:, start : start + width] = dot(normed[...], weights)

    def convolve(begin, end):
        @pl.loop(begin, end)
        def _(j):
            cols = tile(j)
            x = proj[:, tile(j, INNER)]
            pre = taps[4:5, cols] + taps[3:4, cols] * x
            for step in (1, 2, 3):
                pre = pre + taps[3 - step : 4 - step, cols] * rolled_down(x, step)
            sig = jax.nn.sigmoid(pre)
            act[:, cols] = (pre * sig).astype(low)
            dsilu[:, cols] = (sig * (1.0 + pre * (1.0 - sig))).astype(low)

    project(1, late[:, :128])
    project(0, weight(0))
    taps[...] = jnp.zeros_like(taps)
    for base in (0, XBC // 2):
        for k in range(CONV + 1):
            taps[k : k + 1, base : base + XBC // 2] = spread((3, 4, 5, 6, 2)[k], base, XBC // 2, 18)
    give(EARLY)
    convolve(SPLIT, XBC // 128)

    raw = proj[:, INNER + XBC : INNER + XBC + 128] + heads[0:1, :]
    grown = jnp.exp(-jnp.abs(raw))
    more = 1.0 + grown
    logged = jnp.where(more == 1.0, grown, jnp.log(more) * grown / jnp.where(more == 1.0, 1.0, more - 1.0))
    steps = jnp.where(lane < HEADS, jnp.maximum(raw, 0.0) + logged, 0.0)
    rate = -jnp.exp(heads[1:2, :])

    def split(x):
        top = x.astype(low)
        middle = (x - top.astype(full)).astype(low)
        return top, middle, (x - top.astype(full) - middle.astype(full)).astype(low)

    def summed(mask, x):
        found = dot(jnp.where(mask, 1.0, 0.0).astype(low), jnp.concatenate(split(x), axis=1))
        return found[:, :128] + found[:, 128:256] + found[:, 256:]

    cum = summed(row >= column, steps * rate) * LOG2E
    step_ref[...] = steps
    key = cum - jnp.log2(jnp.maximum(steps, 1e-37))
    turned, key_turned = cum.T, key.T
    for head in range(HEADS):
        cum_t[head] = turned[head : head + 1]
        key_t[head] = key_turned[head : head + 1]

    def thirds(x):
        top, middle, rest = [part.astype(full) for part in split(jnp.where(lane < HEADS, x, 0.0))]
        return (top + pltpu.roll(middle, HEADS, axis=1) + pltpu.roll(rest, 2 * HEADS, axis=1)).astype(low)

    cum_parts[...] = thirds(cum)
    key_parts[...] = thirds(key)
    mixed = jnp.where(row >= column, dot_nt(act[:, INNER + STATE :], act[:, INNER : INNER + STATE]), 0.0)
    mix[...] = mixed
    mix_t[...] = mixed.T

    taken(EARLY)
    for i in (2, 3, 4):
        fetch(i)
    gain[...] = spread(1, 0, INNER, 16)
    fetch(5)
    launch(OUT, 2)
    for i in (2, 3):
        project(i, weight(i))
    give(GATE)
    for i in (4, 5):
        project(i, weight(i))
    convolve(0, 10)
    taken(GATE)
    for i in (6, 7, 8, 9):
        fetch(i)
    convolve(10, SPLIT)
    for i in (6, 7, 8, 9):
        project(i, weight(i))
    give(OUT)
    q_ref[...] = jnp.zeros_like(q_ref)
    dcum_ref[...] = jnp.zeros_like(dcum_ref)
    dstep_ref[...] = jnp.zeros_like(dstep_ref)

    causal = lax.broadcasted_iota(jnp.int32, (128, 128), 0) >= lax.broadcasted_iota(jnp.int32, (128, 128), 1)


    def spread_heads(parts, j):
        line = lax.broadcasted_iota(jnp.int32, (128, 256), 0)
        head = 2 * j + (lax.broadcasted_iota(jnp.int32, (128, 256), 1) >> 7)
        return dot(parts[...], jnp.where(((line & 31) == head) & (line < 96), 1.0, 0.0).astype(low))

    @pl.loop(0, HEADS // 2)
    def _(j):
        cols = tile(j)
        cums = spread_heads(cum_parts, j)
        values = act[:, cols]
        for block in range(TOK // 128):
            start, last = block * 128, block * 128 + 128
            halves = []
            for e in (0, 1):
                pieces = []
                for past in range(block + 1):
                    span = slice(past * 128, past * 128 + 128)
                    gap = cums[start:last, e * 128 : e * 128 + 128] - key_t[2 * j + e, :, span]
                    if past == block:
                        gap = jnp.where(causal, gap, -1e30)
                    pieces.append((mix[start:last, span] * jnp.exp2(gap)).astype(low))
                halves.append(jnp.concatenate(pieces, axis=1))
            found = dot(jnp.concatenate(halves, axis=0), values[:last])
            y = jnp.where(left[:128], found[:128], found[128:]) + skip[:, cols] * values[start:last].astype(full)
            y_ref[start:last, cols] = y
            gate = proj[start:last, cols]
            gated = y * gate * jax.nn.sigmoid(gate)
            q_ref[start:last] += gated * gated

    q_ref[...] = jnp.broadcast_to(lax.rsqrt(row_sum(q_ref[...]) / INNER + eps), (TOK, 128))
    mix[...] = jnp.zeros_like(mix)

    @pl.loop(0, INNER // 128)
    def _(j):
        cols = tile(j)
        gate = proj[:, cols]
        gated = y_ref[:, cols] * gate * jax.nn.sigmoid(gate)
        value = (gated * q_ref[...] * gain[:, cols]).astype(low)
        dproj[:, cols] = value
        inner_t[pl.ds(4 * j, 4)] = value.T.reshape(4, 2, 16, TOK)

    for j in range(D // 128):
        cols = slice(j * 128, j * 128 + 128)
        normed[:, cols] = (live(128) * cotangent[:, cols].astype(full)).astype(low)

    def grads(batch, group, side, half):
        start = PARTS[batch][group[0]][0]
        width = sum(PARTS[batch][part][1] for part in group)
        if batch == OUT:
            lhs = inner_t[pl.ds(32 * half, 32), side].reshape(TOK, TOK)
            rhs = normed[:, start : start + width]
        else:
            lhs = normed_t[pl.ds(32 * half, 32)].reshape(TOK, TOK)
            rhs = dproj[:, pl.ds(pl.multiple_of(BASE[batch] + start + side * WIDTH[batch], 128), width)]
        value = dot(lhs, rhs)
        return [(part, PARTS[batch][part][0] - start, PARTS[batch][part][1], value) for part in group]

    def spot_of(part, half, m):
        spot = {"y": 2 * half + (m // 4) % 2, "z": m // 8, "x": m % 4}
        axes = ORDERS[part]
        return spot[axes[2]] * 16 + spot[axes[1]] * 4 + spot[axes[0]]

    users = [[], []]

    def rs_free():
        for gone in users:
            while gone:
                rs_pass_copy(*gone.pop()).wait_send()

    def rs_give(batch):
        for group, slot in GROUPS[batch]:
            while users[slot]:
                rs_pass_copy(*users[slot].pop()).wait_send()
            origin = PARTS[batch][group[0]][0]
            for half in (0, 1):
                for part, offset, width, value in grads(batch, group, 1 - core, half):
                    value = value[:, offset : offset + width].astype(low)
                    for m in range(32):
                        work[CHIPS * slot + spot_of(part, half, m), :, offset : offset + width] = value[
                            16 * m : 16 * m + 16
                        ]
            for part in group:
                offset = PARTS[batch][part][0] - origin
                users[slot].append((batch, part, slot, offset))
                rs_pass_copy(batch, part, slot, offset).start()

    def rs_pass_copy(batch, part, slot=0, offset=0):
        width = PARTS[batch][part][1]
        sem = batch * 3 + part
        return remote(
            work.at[pl.ds(CHIPS * slot, CHIPS), :, pl.ds(offset, width)],
            part0.at[:, :, lanes_of(batch, part)],
            rs_pass.at[sem],
            rs_got.at[batch],
            sibling,
        )

    def lanes_of(batch, part):
        start, width = PARTS[batch][part]
        return pl.ds(LOCAL[batch] + start, width)

    def rs_copies(batch, part, stage):
        lanes = lanes_of(batch, part)
        axis = ORDERS[part][3 - stage]
        copies = []
        for step in (1, 2, 3):
            peer = moved(at, axis, step)
            there, slot = peer[axis], pl.ds(step - 1, 1)
            if stage == 1:
                source, target = part0.at[pl.ds(there * 16, 16), :, lanes], recv1.at[pl.ds(16 * step - 16, 16), :, lanes]
            elif stage == 2:
                source, target = part1.at[pl.ds(there * 4, 4), :, lanes], recv2.at[pl.ds(4 * step - 4, 4), :, lanes]
            else:
                source, target = part2.at[pl.ds(there, 1), :, lanes], recv3.at[slot, :, lanes]
            sem = batch * 3 + stage - 1
            copies.append(remote(source, target, rs_send.at[sem], rs_recv.at[sem], peer))
        return copies

    def rs_hop(batch, part, stage):
        for copy in rs_copies(batch, part, stage):
            copy.start()

    def rs_wait(batch, stage, sems):
        lanes = pl.ds(LOCAL[batch], WIDTH[batch])
        every = (recv1, recv2, recv3)[stage - 1].at[:, :, lanes]
        pltpu.make_async_copy(every, every, sems.at[batch * 3 + stage - 1]).wait()

    def rs_own(batch):
        lanes = pl.ds(LOCAL[batch], WIDTH[batch])
        every = part0.at[:, :, lanes]
        pltpu.make_async_copy(every, every, rs_got.at[batch]).wait()
        for group, _ in GROUPS[batch]:
            for half in (0, 1):
                for part, offset, width, value in grads(batch, group, core, half):
                    lanes = lanes_of(batch, part)
                    for m in range(32):
                        now = pl.ds(spot_of(part, half, m), 1)
                        piece = value[16 * m : 16 * m + 16, offset : offset + width][None]
                        part0[now, :, lanes] = (piece + part0[now, :, lanes].astype(full)).astype(low)
            for part in group:
                rs_hop(batch, part, 1)

    def part_one(batch, part):
        lanes = lanes_of(batch, part)
        mine = at[ORDERS[part][2]] * 16
        for i in range(16):
            now = pl.ds(i, 1)
            value = part0[pl.ds(mine + i, 1), :, lanes].astype(full)
            for k in range(3):
                value = value + recv1[pl.ds(16 * k + i, 1), :, lanes].astype(full)
            part1[now, :, lanes] = value.astype(low)
        rs_hop(batch, part, 2)

    def part_two(batch, part):
        lanes = lanes_of(batch, part)
        mine = at[ORDERS[part][1]] * 4
        for i in range(4):
            now = pl.ds(i, 1)
            value = part1[pl.ds(mine + i, 1), :, lanes].astype(full)
            for k in range(3):
                value = value + recv2[pl.ds(4 * k + i, 1), :, lanes].astype(full)
            part2[now, :, lanes] = value.astype(low)
        rs_hop(batch, part, 3)

    def part_three(batch, part):
        lanes = lanes_of(batch, part)
        value = part2[pl.ds(at[ORDERS[part][0]], 1), :, lanes].astype(full)
        for k in range(3):
            value = value + recv3[pl.ds(k, 1), :, lanes].astype(full)
        value = value[0]
        start, width = PARTS[batch][part]
        if batch == OUT:
            go_out[:, start : start + width] = value
            return
        base = BASE[batch]
        at_column = pl.multiple_of(base + core * WIDTH[batch] + start, 128)
        gi_out[:, pl.ds(at_column, width)] = jnp.where(first, value[:8], value[8:])
        swap_from[:, pl.ds(base // 2 + start, width)] = jnp.where(first, value[8:], value[:8])

    rs_give(OUT)
    taken(OUT)
    while drained:
        wait_bytes(*drained.pop())
    wout = full_out.reshape(INNER, D)

    m_ref[...] = jnp.zeros_like(m_ref)

    @pl.loop(0, D // 256)
    def _(j):
        cols = tile(j, 0, 256)
        branch = dot(dproj[:, :INNER], wout[:, cols])
        block_out[:, cols] = (tokens[:, cols].astype(full) + live(256) * branch).astype(low)
        shares = normed[:, cols].astype(full) * branch
        m_ref[...] += shares[:, :128] + shares[:, 128:]

    outputs = [pltpu.make_async_copy(block_out, block_out_hbm, edge_sem.at[5])]
    outputs[0].start()

    m_ref[...] = jnp.broadcast_to(row_sum(m_ref[...]) / INNER, (TOK, 128))

    @pl.loop(0, INNER // 256)
    def _(j):
        wide = tile(j, 0, 256)
        sums = [jnp.zeros((1, 128), full)] * 2
        for rows in (slice(0, 256), slice(256, 512)):
            value = dot_nt(normed[rows, :], wout[wide, :])
            for half in (0, 1):
                cols = tile(2 * j + half)
                inside = value[:, half * 128 : half * 128 + 128]
                y, gate, q = y_ref[rows, cols], proj[rows, cols], q_ref[rows, :]
                sig = jax.nn.sigmoid(gate)
                silu = gate * sig
                u = y * silu * q
                sums[half] = sums[half] + col_sum(inside * u)
                dgated = q * (inside * gain[:, cols] - u * m_ref[rows, :])
                dproj[rows, cols] = (dgated * y * (sig + silu * (1.0 - sig))).astype(low)
                dinner[rows, cols] = dgated * silu
        for half in (0, 1):
            small_now[5:6, tile(2 * j + half)] = sums[half]

    rs_own(OUT)

    rs_give(GATE)

    dnormed = proj.at[:, pl.ds(0, D)]

    def back_load(i):
        fetched(2 + i % 2, *BACK_TILES[i]).start()

    def back_tile(i):
        start, width = BACK_TILES[i]
        fetched(2 + i % 2, start, width).wait()
        value = dot_nt(dproj[:, start : start + width], inner_t[:, i % 2, :, :width].reshape(D, width))
        dnormed[...] = value if i == 0 else dnormed[...] + value
        if i + 2 < len(BACK_TILES):
            back_load(i + 2)

    back_load(0)
    back_load(1)

    def conv_back(dact, j):
        cols = tile(j)
        x = proj[:, tile(j, INNER)]
        dpre = dact * dsilu[:, cols].astype(full)
        small_now[4:5, cols] = col_sum(dpre)
        small_now[3:4, cols] = col_sum(dpre * x)
        dx = taps[3:4, cols] * dpre
        for step in (1, 2, 3):
            moved_up = rolled_up(dpre, step)
            small_now[3 - step : 4 - step, cols] = col_sum(moved_up * x)
            dx = dx + taps[3 - step : 4 - step, cols] * moved_up
        dproj[:, tile(j, INNER)] = dx.astype(low)

    def rs_one(batch):
        rs_wait(batch, 1, rs_recv)
        for part in range(3):
            part_one(batch, part)

    def rs_two(batch):
        rs_wait(batch, 2, rs_recv)
        for part in range(3):
            part_two(batch, part)

    def rs_three(batch):
        rs_wait(batch, 3, rs_recv)
        for part in range(3):
            part_three(batch, part)

    back_ref[...] = jnp.zeros_like(back_ref)

    def settle(j):
        cols = tile(j)
        lane = lax.broadcasted_iota(jnp.int32, (TOK, 128), 1)
        left = lane < HEAD
        values, dy, back = act[:, cols].astype(full), dinner[:, cols], back_ref[...]
        direct = values * back
        crossing = dy.astype(low).astype(full) * (y_ref[:, cols] - skip[:, cols] * values) - direct
        small_now[7:8, cols] = col_sum(dy * values)
        for e in (0, 1):
            mine = left if e == 0 else jnp.logical_not(left)
            spot = lane == 2 * j + e
            dcum_ref[...] = jnp.where(spot, row_sum(jnp.where(mine, crossing, 0.0)), dcum_ref[...])
            dstep_ref[...] = jnp.where(spot, row_sum(jnp.where(mine, direct, 0.0)), dstep_ref[...])
        conv_back(back + skip[:, cols] * dy, j)

    @pl.loop(0, HEADS // 4 + 1)
    def _(run):
        for turn, events in PLAN:

            @pl.when(run == turn)
            def _(events=events):
                for action, what in events:
                    if action == "dn":
                        back_tile(what)
                    else:
                        {"give": rs_give, "own": rs_own, "one": rs_one, "two": rs_two}[action](what)

        @pl.loop(jnp.maximum(2 * run - 1, 0), jnp.minimum(2 * run + 1, HEADS // 2))
        def _(j):
            settle(jnp.maximum(j - 1, 0))
            cols = tile(j)
            keys = spread_heads(key_parts, j)
            left = lax.broadcasted_iota(jnp.int32, (TOK, 128), 1) < HEAD
            anti = lax.broadcasted_iota(jnp.int32, (128, 128), 0) <= lax.broadcasted_iota(
                jnp.int32, (128, 128), 1
            )
            v_low = act[:, cols]
            dy_low = dinner[:, cols].astype(low)
            own = (jnp.where(left, v_low, jnp.zeros_like(v_low)), jnp.where(left, jnp.zeros_like(v_low), v_low))
            found = []
            for block in range(TOK // 128):
                start, last = block * 128, block * 128 + 128
                both = dot_nt(jnp.concatenate([own[0][start:last], own[1][start:last]], axis=0), dy_low[start:])
                halves = []
                total = None
                for e in (0, 1):
                    pieces, shares = [], []
                    for later in range(block, TOK // 128):
                        span = slice(later * 128, later * 128 + 128)
                        gap = cum_t[2 * j + e, :, span] - keys[start:last, e * 128 : e * 128 + 128]
                        if later == block:
                            gap = jnp.where(anti, gap, -1e30)
                        decay = jnp.exp2(gap)
                        pieces.append((mix_t[start:last, span] * decay).astype(low))
                        inside = slice((later - block) * 128, (later - block + 1) * 128)
                        shares.append(both[e * 128 : e * 128 + 128, inside] * decay)
                    halves.append(jnp.concatenate(pieces, axis=1))
                    share = jnp.concatenate(shares, axis=1)
                    total = share if total is None else total + share
                mix[start:last, start:] += total
                given_back = dot(jnp.concatenate(halves, axis=0), dy_low[start:])
                found.append(jnp.where(left[:128], given_back[:128], given_back[128:]))
            for block, value in enumerate(found):
                back_ref[block * 128 : block * 128 + 128] = value

    settle(HEADS // 2 - 1)
    rs_own(MID)
    masked = jnp.where(row <= column, mix[...], 0.0)
    conv_back(dot(masked.astype(low), act[:, INNER + STATE :]), INNER // 128)
    conv_back(dot(masked.T.astype(low), act[:, INNER : INNER + STATE]), INNER // 128 + 1)
    dacc = summed(row <= column, dcum_ref[...])
    sig = jax.nn.sigmoid(proj[:, INNER + XBC : INNER + XBC + 128] + heads[0:1, :])
    steps = step_ref[...]
    ratio = jnp.where(steps > 1e-30, sig / jnp.maximum(steps, 1e-30), 1.0)
    draw = jnp.where(lane < HEADS, dstep_ref[...] * ratio + dacc * rate * sig, 0.0)
    dproj[:, INNER + XBC : INNER + XBC + 128] = draw.astype(low)
    dproj[:, INNER + XBC + 128 :] = jnp.zeros((TOK, 128), low)
    small_now[6:7, :] = jnp.zeros((1, XBC), full)
    small_now[6:7, :128] = col_sum(draw)
    small_now[6:7, 128:256] = rate * col_sum(dacc * steps)
    small_now[5:6, INNER:] = jnp.zeros((1, XBC - INNER), full)
    small_now[7:8, INNER:] = jnp.zeros((1, XBC - INNER), full)


    def small_swap():
        away = pl.ds(pl.multiple_of((1 - core) * HALF, 128), HALF)
        return remote(small_now.at[:, away], small_other, small_send.at[0], small_recv.at[0], sibling)

    def small_copies(stage):
        made = []
        for part in range(3):
            lanes = pl.ds(part * THIRD, THIRD)
            axis = ORDERS[part][stage - 1]
            for step in (1, 2, 3):
                slot = (stage - 1) * 3 + step - 1
                made.append(
                    remote(
                        small_half.at[stage - 1, :, lanes],
                        small_got.at[slot, :, lanes],
                        small_send.at[stage],
                        small_recv.at[stage],
                        moved(at, axis, step),
                    )
                )
        return made

    def small_back():
        return remote(small_half.at[3], small_last, small_send.at[4], small_recv.at[4], sibling)

    def small_wait(stage, sems):
        if stage in (0, 4):
            sems_of = small_other if stage == 0 else small_last
            pltpu.make_async_copy(sems_of, sems_of, sems.at[stage]).wait()
        else:
            every = small_got.at[pl.ds((stage - 1) * 3, 3)]
            pltpu.make_async_copy(every, every, sems.at[stage]).wait()

    def small_add(stage):
        small_wait(stage, small_recv)
        if stage == 0:
            mine = pl.ds(pl.multiple_of(core * HALF, 128), HALF)
            small_half[0] = small_now[:, mine] + small_other[...]
        else:
            value = small_half[stage - 1]
            for k in range(3):
                value = value + small_got[(stage - 1) * 3 + k]
            small_half[stage] = value
        for copy in small_copies(stage + 1) if stage < 3 else [small_back()]:
            copy.start()

    def norm_start(stage):
        for step in (1,) if stage == 0 else (1, 2, 3):
            slot = 0 if stage == 0 else stage * 3 - 3 + step
            peer = moved(at, "cxyz"[stage], step)
            remote(norm_now.at[stage], norm_got.at[slot], norm_send.at[stage], norm_recv.at[stage], peer).start()

    def norm_wait(stage, sems):
        every = norm_got.at[pl.ds(0, 1)] if stage == 0 else norm_got.at[pl.ds(stage * 3 - 2, 3)]
        pltpu.make_async_copy(every, every, sems.at[stage]).wait()

    def norm_add(stage):
        norm_wait(stage, norm_recv)
        value = norm_now[stage]
        for k in range(1 if stage == 0 else 3):
            value = value + norm_got[0 if stage == 0 else stage * 3 - 2 + k]
        if stage == 3:
            norm_out[...] = value
        else:
            norm_now[stage + 1] = value
            norm_start(stage + 1)

    small_swap().start()
    rs_give(LATE)
    back_tile(7)
    small_add(0)
    back_tile(8)
    back_tile(9)
    rs_own(LATE)
    rs_two(GATE)
    m_ref[...] = jnp.zeros_like(m_ref)
    for j in range(D // 128):
        cols = slice(j * 128, j * 128 + 128)
        u = tokens[:, cols].astype(full) * token_scale
        du = dnormed[:, cols] * u
        norm_now[0, j : j + 1, :] = col_sum(du)
        m_ref[...] += du * norm_gain[:, cols]
    mean = row_sum(m_ref[...]) / D
    norm_start(0)
    small_add(1)
    rs_one(EARLY)
    rs_one(MID)
    for j in range(D // 128):
        cols = slice(j * 128, j * 128 + 128)
        u = tokens[:, cols].astype(full) * token_scale
        du = dnormed[:, cols] * norm_gain[:, cols]
        normed[:, cols] = (cotangent[:, cols].astype(full) + token_scale * (du - u * mean)).astype(low)
    final = pltpu.make_async_copy(normed, input_grad, local_sem.at[0])
    final.start()
    norm_add(0)
    rs_three(OUT)
    rs_one(LATE)
    small_add(2)
    norm_add(1)
    rs_three(GATE)
    rs_two(EARLY)
    rs_two(MID)
    for batch in (OUT, GATE):
        for stage in (1, 2, 3):
            rs_wait(batch, stage, rs_send)
    rs_two(LATE)
    small_add(3)
    norm_add(2)
    rs_three(EARLY)
    rs_three(MID)
    small_wait(4, small_recv)
    mine = pl.ds(pl.multiple_of(core * HALF, 128), HALF)
    small_out[:, mine] = small_half[3]
    small_out[:, pl.ds(pl.multiple_of((1 - core) * HALF, 128), HALF)] = small_last[...]
    outputs.append(pltpu.make_async_copy(small_out, small_hbm, edge_sem.at[6]))
    outputs.append(pltpu.make_async_copy(go_out, go_hbm, edge_sem.at[7]))
    for copy in outputs[1:]:
        copy.start()
    rs_free()
    for stage in range(5):
        small_wait(stage, small_send)
    for batch in (EARLY, MID):
        for stage in (1, 2, 3):
            rs_wait(batch, stage, rs_send)
    rs_three(LATE)
    last = remote(swap_from, swap_to, swap_sem.at[2], swap_sem.at[3], sibling)
    last.start()
    norm_add(3)
    outputs.append(pltpu.make_async_copy(norm_out, norm_hbm, edge_sem.at[8]))
    outputs[3].start()
    for stage in range(4):
        norm_wait(stage, norm_send)
    for stage in (1, 2, 3):
        rs_wait(LATE, stage, rs_send)
    final.wait()
    last.wait()
    for batch in (GATE, EARLY, MID, LATE):
        base, width = BASE[batch], WIDTH[batch]
        lanes = pl.ds(pl.multiple_of(base + (1 - core) * width, 128), width)
        gi_out[:, lanes] = swap_to[:, base // 2 : base // 2 + width]
    outputs.append(pltpu.make_async_copy(gi_out, gi_hbm, edge_sem.at[9]))
    outputs[4].start()
    for copy in outputs:
        copy.wait()


def block(lengths, ids, in_shard, wo, tokens, cotangent, params):
    full, low = jnp.float32, jnp.bfloat16
    anywhere = pl.BlockSpec(memory_space=pl.ANY)
    sems = pltpu.SemaphoreType.DMA
    return pl.pallas_call(
        block_kernel,
        out_shape=(
            jax.ShapeDtypeStruct((TOK, D), low),
            jax.ShapeDtypeStruct((TOK, D), low),
            jax.ShapeDtypeStruct((8, COLS), full),
            jax.ShapeDtypeStruct((16, D), full),
            jax.ShapeDtypeStruct((8, XBC), full),
            jax.ShapeDtypeStruct((8, 128), full),
            jax.ShapeDtypeStruct((2, 4, 2, 4, 16, COLS), low),
        ),
        in_specs=[pl.BlockSpec(memory_space=pltpu.SMEM)] * 2 + [anywhere] * 5,
        out_specs=[anywhere] * 7,
        scratch_shapes=[
            pltpu.VMEM((8, PROJ), low),
            pltpu.VMEM((16, D), low),
            pltpu.VMEM((TOK, D), low),
            pltpu.VMEM((TOK, D), low),
            pltpu.VMEM((16, 128), full),
            pltpu.VMEM((TOK, D), low),
            pltpu.VMEM((8, COLS), full),
            pltpu.VMEM((16, D), full),
            pltpu.VMEM((8, XBC), full),
            pltpu.VMEM((8, 128), full),
            pltpu.VMEM((8, COLS), full),
            pltpu.VMEM((8, COLS), full),
            pltpu.VMEM((16, XBC), low),
            pltpu.VMEM((1, INNER), full),
            pltpu.VMEM((2, 4, 2, 4, 2, 16, D), low),
            pltpu.VMEM((2 * CHIPS, 16, 512), low),
            pltpu.VMEM((TOK, COLS - 128), full),
            pltpu.VMEM((TOK, XBC), low),
            pltpu.VMEM((TOK, XBC), low),
            pltpu.VMEM((TOK, INNER), full),
            pltpu.VMEM((TOK, INNER), full),
            pltpu.VMEM((TOK, COLS), low),
            pltpu.VMEM((CHIPS, 2, 16, TOK), low),
            pltpu.VMEM((TOK, D), low),
            pltpu.VMEM((CHIPS, 16, TOK), low),
            pltpu.VMEM((TOK, TOK), full),
            pltpu.VMEM((TOK, TOK), full),
            pltpu.VMEM((TOK, 128), low),
            pltpu.VMEM((TOK, 128), low),
            pltpu.VMEM((HEADS, 1, TOK), full),
            pltpu.VMEM((HEADS, 1, TOK), full),
            pltpu.VMEM((TOK, 128), full),
            pltpu.VMEM((TOK, 128), full),
            pltpu.VMEM((TOK, 128), full),
            pltpu.VMEM((TOK, 128), full),
            pltpu.VMEM((TOK, 128), full),
            pltpu.VMEM((TOK, 128), full),
            pltpu.VMEM((8, XBC), full),
            pltpu.VMEM((1, INNER), full),
            pltpu.VMEM((1, D), full),
            pltpu.VMEM((CHIPS, 16, SIDE), low),
            pltpu.VMEM((48, 16, SIDE), low),
            pltpu.VMEM((16, 16, SIDE), low),
            pltpu.VMEM((12, 16, SIDE), low),
            pltpu.VMEM((4, 16, SIDE), low),
            pltpu.VMEM((3, 16, SIDE), low),
            pltpu.VMEM((8, XBC), full),
            pltpu.VMEM((8, XBC), full),
            pltpu.VMEM((8, XBC), full),
            pltpu.VMEM((8, HALF), full),
            pltpu.VMEM((4, 8, HALF), full),
            pltpu.VMEM((9, 8, HALF), full),
            pltpu.VMEM((8, HALF), full),
            pltpu.VMEM((4, 8, 128), full),
            pltpu.VMEM((10, 8, 128), full),
            sems((4,)),
            sems((7,)),
            sems((10,)),
            sems((15,)),
            sems((15,)),
            sems((5,)),
            sems((5,)),
            sems((15,)),
            sems((15,)),
            sems((15,)),
            sems((5,)),
            sems((5,)),
            sems((5,)),
            sems((4,)),
            sems((4,)),
        ],
        compiler_params=pltpu.CompilerParams(collective_id=0, has_side_effects=True, vmem_limit_bytes=63 << 20),
    )(lengths, ids, in_shard, wo, tokens, cotangent, params)


def finish_kernel(
    out_in,
    grad_in,
    gi_in,
    go_in,
    small_in,
    norm_in,
    out_hbm,
    grad_hbm,
    gain_hbm,
    gi_hbm,
    conv_hbm,
    bias_hbm,
    dt_hbm,
    log_hbm,
    skip_hbm,
    inner_hbm,
    go_hbm,
    small,
    norm,
    gi,
    go,
    out,
    grad,
    gain_out,
    gi_out,
    conv_out,
    bias_out,
    dt_out,
    log_out,
    skip_out,
    inner_out,
    sem,
):
    pairs = [(small_in, small), (norm_in, norm), (gi_in, gi), (go_in, go)]
    halves = [pl.ds(0, TOK // 2), pl.ds(TOK // 2, TOK // 2)]
    for source, target in ((out_in, out), (grad_in, grad)):
        pairs += [(source.at[half, :], target.at[half, :]) for half in halves]
    copies = [pltpu.make_async_copy(source, target, sem.at[i]) for i, (source, target) in enumerate(pairs)]
    for copy in copies[:1] + copies[4:] + copies[1:4]:
        copy.start()
    writes = []

    def write(source, target):
        writes.append(pltpu.make_async_copy(source, target, sem.at[len(copies) + len(writes)]))
        writes[-1].start()

    me = lax.axis_index("dp") * 16 + lax.axis_index("fsdp")
    copies[0].wait()

    def from_lane(count):
        return pltpu.roll(small[...], lax.rem(XBC - count * me, XBC), axis=1)

    conv = from_lane(18)
    conv_out[...] = conv[:CONV, :18]
    write(conv_out, conv_hbm)
    bias_out[...] = conv[CONV : CONV + 1, :18]
    write(bias_out, bias_hbm)
    inner_out[...] = from_lane(16)[5:6, :16]
    write(inner_out, inner_hbm)
    dt_out[...] = small[6:7, :HEADS]
    write(dt_out, dt_hbm)
    log_out[...] = small[6:7, 128 : 128 + HEADS]
    write(log_out, log_hbm)
    for i, (source, target) in enumerate(((out, out_hbm), (grad, grad_hbm))):
        for k, half in enumerate(halves):
            copies[4 + 2 * i + k].wait()
            write(source.at[half, :], target.at[half, :])
    copies[2].wait()
    gi_out[...] = gi[:, :PROJ]
    write(gi_out, gi_hbm)
    copies[3].wait()
    write(go, go_hbm)
    owner = lax.broadcasted_iota(jnp.int32, (INNER, 128), 0) >> 6
    sums = (owner == lax.broadcasted_iota(jnp.int32, (INNER, 128), 1)).astype(jnp.float32)
    skip_out[...] = dot(small[:, :INNER], sums, precision=highest)[7:8, :HEADS]
    write(skip_out, skip_hbm)
    copies[1].wait()
    line = lax.broadcasted_iota(jnp.int32, (8, 128), 0)
    row = jnp.sum(jnp.where(line == me // 16, norm[...], 0.0), axis=0, keepdims=True)
    gain_out[...] = pltpu.roll(row, lax.rem(128 - 8 * lax.rem(me, 16), 128), axis=1)[:, :8]
    write(gain_out, gain_hbm)
    for copy in writes:
        copy.wait()


def finish(out, grad, gi, go, small, norm):
    full = jnp.float32
    anywhere = pl.BlockSpec(memory_space=pl.ANY)
    rest = [(CONV, 18), (1, 18), (1, HEADS), (1, HEADS), (1, HEADS), (1, 16)]
    shapes = [(1, 8), (8, PROJ)] + rest
    return pl.pallas_call(
        finish_kernel,
        out_shape=[jax.ShapeDtypeStruct(out.shape, out.dtype)] * 2
        + [jax.ShapeDtypeStruct(shape, full) for shape in shapes + [(16, D)]],
        in_specs=[anywhere] * 6,
        out_specs=[anywhere] * 11,
        scratch_shapes=[
            pltpu.VMEM(small.shape, full),
            pltpu.VMEM(norm.shape, full),
            pltpu.VMEM(gi.shape, full),
            pltpu.VMEM(go.shape, full),
            pltpu.VMEM(out.shape, out.dtype),
            pltpu.VMEM(out.shape, out.dtype),
        ]
        + [pltpu.VMEM(shape, full) for shape in shapes]
        + [pltpu.SemaphoreType.DMA((21,))],
        compiler_params=pltpu.CompilerParams(vmem_limit_bytes=62 << 20),
    )(out, grad, gi, go, small, norm)


def body(
    tokens,
    lengths,
    placement_ids,
    norm_gain,
    in_weight,
    conv_weight,
    conv_bias,
    dt_bias,
    a_log,
    d_skip,
    inner_gain,
    out_weight,
    cotangent,
):
    full = jnp.float32

    def line(values, first):
        values = values.astype(full).reshape(-1, values.shape[-1])
        rows, lanes = values.shape
        return jnp.pad(values, ((first, 16 - first - rows), (0, 128 - lanes)))

    params = (
        line(norm_gain, 0)
        + line(inner_gain, 1)
        + line(conv_bias, 2)
        + line(conv_weight, 3)
        + line(dt_bias, 8)
        + line(a_log, 9)
        + line(d_skip, 10)
    )
    block_out, input_grad, shard_in, shard_out, small, norm, _ = block(
        lengths, placement_ids, in_weight, out_weight, tokens, cotangent, params
    )
    found = finish(block_out, input_grad, shard_in, shard_out, small, norm)
    flat = [0, 0, 1, 0, 0, 1, 1, 1, 1, 1, 0]
    return tuple(value[0] if one else value for value, one in zip(found, flat))


def solution(mesh):
    placed = (
        P(("dp", "fsdp"), None),
        P(),
        P(("dp", "fsdp")),
        P(("dp", "fsdp")),
        P(("dp", "fsdp"), None),
        P(None, ("dp", "fsdp")),
        P(("dp", "fsdp")),
        P(),
        P(),
        P(),
        P(("dp", "fsdp")),
        P(("dp", "fsdp"), None),
        P(("dp", "fsdp"), None),
    )
    return jax.shard_map(
        body,
        mesh=mesh,
        in_specs=placed,
        out_specs=(
            P(("dp", "fsdp"), None),
            P(("dp", "fsdp"), None),
            P(("dp", "fsdp")),
            P(("dp", "fsdp"), None),
            P(None, ("dp", "fsdp")),
            P(("dp", "fsdp")),
            P(),
            P(),
            P(),
            P(("dp", "fsdp")),
            P(("dp", "fsdp"), None),
        ),
        check_vma=False,
    )
```

```python
import jax
import jax.numpy as jnp
import numpy as np
from jax import lax
from jax.experimental import pallas as pl
from jax.experimental.pallas import tpu as pltpu
from jax.sharding import PartitionSpec as P

D = 1024
INNER = 2048
STATE = 128
HEAD = 64
CONV = 4
HEADS = 32
XBC = 2304
PROJ = 4384
TOK = 512
CHIPS = 64
COLS = 4608
SIDE = 3328
HALF = 1152
THIRD = 384
MESH = pl.DeviceIdType.MESH
ORDERS = (("x", "y", "z"), ("y", "z", "x"), ("z", "x", "y"))
OUT, GATE, EARLY, MID, LATE = 0, 1, 2, 3, 4
GET_PARTS = {
    OUT: ((0, 384), (384, 384), (768, 256)),
    GATE: ((0, 384), (384, 384), (768, 384)),
    EARLY: ((0, 256), (256, 256), (512, 256)),
    LATE: ((0, 128), (128, 128), (256, 128)),
}
GET_BASE = {GATE: 0, EARLY: 2304, LATE: 3840}
GET_WIDTH = {OUT: 1024, GATE: 1152, EARLY: 768, LATE: 384}
SPLIT = 14
TILES = (
    (3840, 512),
    (4352, 256),
    (2304, 512),
    (2816, 512),
    (3328, 512),
    (2048, 256),
    (0, 512),
    (512, 512),
    (1024, 512),
    (1536, 512),
)
PARTS = {
    OUT: ((0, 512), (512, 256), (768, 256)),
    GATE: ((0, 256), (512, 512), (256, 256)),
    EARLY: ((0, 128), (128, 128), (256, 256)),
    MID: ((0, 128), (128, 128), (256, 128)),
    LATE: ((0, 128), (128, 128), (256, 128)),
}
GROUPS = {
    OUT: (((0,), 0), ((1, 2), 1)),
    GATE: (((0, 2), 0), ((1,), 1)),
    EARLY: (((0, 1, 2), 0),),
    MID: (((0, 1, 2), 1),),
    LATE: (((0, 1, 2), 0),),
}
LOCAL = {OUT: 0, GATE: 1024, EARLY: 2048, MID: 2560, LATE: 2944}
BASE = {GATE: 0, EARLY: 2048, MID: 3072, LATE: 3840}
WIDTH = {OUT: 1024, GATE: 1024, EARLY: 512, MID: 384, LATE: 384}
BACK_TILES = (
    (0, 512),
    (512, 512),
    (1024, 512),
    (1536, 512),
    (2048, 512),
    (2560, 512),
    (3072, 512),
    (3584, 256),
    (3840, 512),
    (4352, 256),
)

eps = 1e-05
LOG2E = 1.4426950408889634
highest = lax.Precision.HIGHEST

PLAN = (
    (1, (("dn", 0),)),
    (2, (("own", GATE), ("dn", 1))),
    (4, (("dn", 2), ("dn", 3), ("one", OUT))),
    (5, (("give", EARLY),)),
    (6, (("own", EARLY), ("dn", 4), ("one", GATE))),
    (7, (("dn", 5), ("two", OUT))),
    (8, (("give", MID), ("dn", 6))),
)


def place():
    dp, fsdp = lax.axis_index("dp"), lax.axis_index("fsdp")
    return {"x": (fsdp // 2) % 4, "y": (dp // 4) * 2 + fsdp // 8, "z": dp % 4, "c": fsdp % 2}


def device(at):
    y = at["y"]
    return ((y // 2) * 4 + at["z"], (y % 2) * 8 + at["x"] * 2 + at["c"])


def moved(at, axis, step):
    size = 2 if axis == "c" else 4
    return dict(at, **{axis: lax.rem(at[axis] + step, size)})


def greet(at):
    peers = [moved(at, axis, step) for axis in "xyz" for step in (1, 2, 3)] + [moved(at, "c", 1)]
    for peer in peers:
        pl.semaphore_signal(pltpu.get_barrier_semaphore(), inc=1, device_id=device(peer), device_id_type=MESH)


def meet():
    pl.semaphore_wait(pltpu.get_barrier_semaphore(), 10)


def remote(src, dst, send, recv, peer):
    return pltpu.make_async_remote_copy(
        src_ref=src, dst_ref=dst, send_sem=send, recv_sem=recv, device_id=device(peer), device_id_type=MESH
    )


def chips(at, full):
    every = slice(None)
    y, z, x = at["y"], at["z"], at["x"]
    return (
        every if "y" in full else y // 2,
        every if "z" in full else z,
        every if "y" in full else y % 2,
        every if "x" in full else x,
    )


def rolled_down(x, step):
    zeros = jnp.zeros((8, x.shape[1]), x.dtype)
    return pltpu.roll(jnp.concatenate([zeros, x], axis=0), step, axis=0)[8:]


def rolled_up(x, step):
    rows = x.shape[0]
    zeros = jnp.zeros((8, x.shape[1]), x.dtype)
    return pltpu.roll(jnp.concatenate([x, zeros], axis=0), rows + 8 - step, axis=0)[:rows]


def tile(j, base=0, size=128):
    return pl.ds(pl.multiple_of(base + j * size, 128), size)


def dot_nt(a, b):
    return lax.dot_general(a, b, (((1,), (1,)), ((), ())), preferred_element_type=jnp.float32)


def dot(a, b, **more):
    return jnp.dot(a, b, preferred_element_type=jnp.float32, **more)


def row_sum(x):
    return jnp.sum(x, axis=1, keepdims=True)


def col_sum(x):
    return jnp.sum(x, axis=0, keepdims=True)


def block_kernel(
    lengths,
    ids,
    in_shard_hbm,
    wo_hbm,
    tokens_hbm,
    cotangent_hbm,
    params_hbm,
    block_out_hbm,
    input_grad,
    gi_hbm,
    go_hbm,
    small_hbm,
    norm_hbm,
    full_in,
    in_shard,
    wo,
    tokens,
    cotangent,
    params,
    block_out,
    gi_out,
    go_out,
    small_out,
    norm_out,
    wi,
    other,
    blk,
    skip,
    full_out,
    work,
    proj,
    act,
    dsilu,
    y_ref,
    dinner,
    dproj,
    inner_t,
    normed,
    normed_t,
    mix,
    mix_t,
    cum_parts,
    key_parts,
    cum_t,
    key_t,
    step_ref,
    q_ref,
    m_ref,
    dcum_ref,
    dstep_ref,
    back_ref,
    taps,
    gain,
    norm_gain,
    part0,
    recv1,
    part1,
    recv2,
    part2,
    recv3,
    swap_from,
    swap_to,
    small_now,
    small_other,
    small_half,
    small_got,
    small_last,
    norm_now,
    norm_got,
    swap_sem,
    local_sem,
    edge_sem,
    ag_send,
    ag_recv,
    ag_pass,
    ag_got,
    rs_send,
    rs_recv,
    rs_pass,
    rs_got,
    small_send,
    small_recv,
    norm_send,
    norm_recv,
):
    low, full = jnp.bfloat16, jnp.float32
    at = place()
    core = at["c"]
    first = core == 0
    sibling = moved(at, "c", 1)
    here = chips(at, ())
    inputs = [
        pltpu.make_async_copy(source, target, edge_sem.at[i])
        for i, (source, target) in enumerate(
            (
                (in_shard_hbm, in_shard),
                (params_hbm, params),
                (tokens_hbm, tokens),
                (wo_hbm, wo),
                (cotangent_hbm, cotangent),
            )
        )
    ]
    for copy in inputs:
        copy.start()
    greet(at)

    lane = lax.broadcasted_iota(jnp.int32, (TOK, 128), 1)
    left = lane < HEAD
    row = lax.broadcasted_iota(jnp.int32, (TOK, TOK), 0)
    column = lax.broadcasted_iota(jnp.int32, (TOK, TOK), 1)
    for copy in inputs[:2]:
        copy.wait()
    wi[:, COLS - 256 :] = jnp.zeros((8, 256), full)
    wi[:, :PROJ] = in_shard[...].astype(full)
    wi[:, COLS - 128 :] = params[0:8, :]
    meet()

    swap = remote(wi, other, swap_sem.at[0], swap_sem.at[1], sibling)
    swap.start()
    for copy in inputs[2:]:
        copy.wait()
    full_out[here + (core,)] = wo[...]

    def held(batch, part, reach):
        start, width = GET_PARTS[batch][part]
        if batch == OUT:
            return full_out.at[chips(at, reach) + (core, slice(None), pl.ds(start, width))]
        spot = pl.multiple_of(core * GET_WIDTH[batch] + start + GET_BASE[batch], 128)
        return full_in.at[chips(at, reach) + (slice(None), pl.ds(spot, width))]

    def wait_bytes(blocks, width, sem):
        size = 512 if width % 512 == 0 else 128
        count = blocks * width // size
        if count > 2 * CHIPS:
            size, count = 512, blocks * width // 512
        if blocks == CHIPS:
            shape = full_in.at[:, :, :, :, :, pl.ds(0, width)]
        else:
            shape = work.at[pl.ds(0, count), :, pl.ds(0, size)]
        pltpu.make_async_copy(shape, shape, sem).wait()

    drained = []

    def hop(batch, phase):
        slot = batch * 3 + phase
        for part in range(3):
            target = held(batch, part, ORDERS[part][:phase])
            source = target
            if phase == 0 and batch != OUT:
                start, width = GET_PARTS[batch][part]
                source = blk.at[:, pl.ds(GET_BASE[batch] // 2 + start, width)]
            for step in (1, 2, 3):
                peer = moved(at, ORDERS[part][phase], step)
                remote(source, target, ag_send.at[slot], ag_recv.at[slot], peer).start()
        drained.append((3 * 4**phase, GET_WIDTH[batch], ag_send.at[slot]))

    def landed(batch, phase):
        wait_bytes(3 * 4**phase, GET_WIDTH[batch], ag_recv.at[batch * 3 + phase])

    def give(batch):
        landed(batch, 2)
        for part in range(3):
            region = held(batch, part, "xyz")
            remote(region, region, ag_pass.at[batch], ag_got.at[batch], sibling).start()
        drained.append((CHIPS, GET_WIDTH[batch], ag_pass.at[batch]))

    def taken(batch):
        wait_bytes(CHIPS, GET_WIDTH[batch], ag_got.at[batch])

    swap.wait()
    stores = []

    def begin(batch):
        base, width = GET_BASE[batch], GET_WIDTH[batch]
        lanes = pl.ds(pl.multiple_of(base + core * width, 128), width)
        mine, theirs = wi[:, lanes], other[:, lanes]
        blk[:, base // 2 : base // 2 + width] = jnp.concatenate(
            [jnp.where(first, mine, theirs), jnp.where(first, theirs, mine)], axis=0
        ).astype(low)
        launch(batch, 0)
        copy = pltpu.make_async_copy(
            blk.at[:, pl.ds(base // 2, width)], full_in.at[here + (slice(None), lanes)], local_sem.at[len(stores)]
        )
        copy.start()
        stores.append(copy)

    def launch(batch, phase):
        if phase:
            landed(batch, phase - 1)
        if phase == 1 and batch != OUT:
            stores.pop(0).wait()
        hop(batch, phase)

    begin(LATE)
    begin(EARLY)
    begin(GATE)
    launch(OUT, 0)
    length = lengths[ids[0]]

    def live(width):
        return (lax.broadcasted_iota(jnp.int32, (TOK, width), 0) < length).astype(full)

    m_ref[...] = jnp.zeros_like(m_ref)
    for j in range(D // 128):
        x = tokens[:, j * 128 : j * 128 + 128].astype(full)
        m_ref[...] += x * x
    token_scale = lax.rsqrt(row_sum(m_ref[...]) / D + eps)
    owner = lax.broadcasted_iota(jnp.int32, (128, INNER), 1) >> 6
    repeats = (lax.broadcasted_iota(jnp.int32, (128, INNER), 0) == owner).astype(full)
    skip[...] = dot(params[8:16, :], repeats, precision=highest)[2:3]
    heads = params[8:16, :]
    launch(LATE, 1)
    launch(EARLY, 1)
    launch(LATE, 2)
    launch(GATE, 1)
    launch(EARLY, 2)
    launch(OUT, 1)

    def slot_of(slot):
        if slot < 2:
            return work.reshape(4, 4, 2, 4, 16, 512).at[pl.ds(2 * slot, 2)]
        return inner_t.reshape(2, 4, 2, 4, 2, 16, 512).at[:, :, :, :, slot - 2]

    def fetched(slot, start, width):
        source = full_in.at[:, :, :, :, :, pl.ds(start, width)]
        return pltpu.make_async_copy(source, slot_of(slot).at[:, :, :, :, :, pl.ds(0, width)], local_sem.at[3 + slot])

    def fetch(i):
        fetched(i % 4, *TILES[i]).start()

    def weight(i):
        slot, width = i % 4, TILES[i][1]
        fetched(slot, *TILES[i]).wait()
        if slot < 2:
            return work[pl.ds(CHIPS * slot, CHIPS), :, :width].reshape(D, width)
        return inner_t[:, slot - 2, :, :width].reshape(D, width)

    give(LATE)
    launch(GATE, 2)
    taken(LATE)
    fetch(1)
    fetch(0)
    late = weight(1)
    packed = late[:, 128:]

    def spread(r, base, count, each):
        pick = (
            lax.broadcasted_iota(jnp.int32, (128, D), 0) * 8 + r == lax.broadcasted_iota(jnp.int32, (128, D), 1)
        ).astype(low)
        shared = dot(pick, packed).astype(low)
        line = lax.broadcasted_iota(jnp.int32, (128, count), 0).astype(full)
        spot = lax.broadcasted_iota(jnp.int32, (128, count), 1).astype(full) + base
        owner = jnp.floor((spot + 0.5) * (1.0 / each))
        found = dot(shared, (line == spot - owner * each).astype(low))
        return col_sum(jnp.where(line == owner, found, 0.0))

    norm_gain[...] = spread(0, 0, D, 8)
    for j in range(D // 128):
        cols = slice(j * 128, j * 128 + 128)
        value = (tokens[:, cols].astype(full) * token_scale * norm_gain[:, cols]).astype(low)
        normed[:, cols] = value
        normed_t[j * 8 : j * 8 + 8] = value.T.reshape(8, 16, TOK)

    def project(i, weights):
        start, width = TILES[i][0], weights.shape[1]
        proj[:, start : start + width] = dot(normed[...], weights)

    def convolve(begin, end):
        @pl.loop(begin, end)
        def _(j):
            cols = tile(j)
            x = proj[:, tile(j, INNER)]
            pre = taps[4:5, cols] + taps[3:4, cols] * x
            for step in (1, 2, 3):
                pre = pre + taps[3 - step : 4 - step, cols] * rolled_down(x, step)
            sig = jax.nn.sigmoid(pre)
            act[:, cols] = (pre * sig).astype(low)
            dsilu[:, cols] = (sig * (1.0 + pre * (1.0 - sig))).astype(low)

    project(1, late[:, :128])
    project(0, weight(0))
    taps[...] = jnp.zeros_like(taps)
    for base in (0, XBC // 2):
        for k in range(CONV + 1):
            taps[k : k + 1, base : base + XBC // 2] = spread((3, 4, 5, 6, 2)[k], base, XBC // 2, 18)
    give(EARLY)
    convolve(SPLIT, XBC // 128)

    raw = proj[:, INNER + XBC : INNER + XBC + 128] + heads[0:1, :]
    grown = jnp.exp(-jnp.abs(raw))
    more = 1.0 + grown
    logged = jnp.where(more == 1.0, grown, jnp.log(more) * grown / jnp.where(more == 1.0, 1.0, more - 1.0))
    steps = jnp.where(lane < HEADS, jnp.maximum(raw, 0.0) + logged, 0.0)
    rate = -jnp.exp(heads[1:2, :])

    def split(x):
        top = x.astype(low)
        middle = (x - top.astype(full)).astype(low)
        return top, middle, (x - top.astype(full) - middle.astype(full)).astype(low)

    def summed(mask, x):
        found = dot(jnp.where(mask, 1.0, 0.0).astype(low), jnp.concatenate(split(x), axis=1))
        return found[:, :128] + found[:, 128:256] + found[:, 256:]

    cum = summed(row >= column, steps * rate) * LOG2E
    step_ref[...] = steps
    key = cum - jnp.log2(jnp.maximum(steps, 1e-37))
    turned, key_turned = cum.T, key.T
    for head in range(HEADS):
        cum_t[head] = turned[head : head + 1]
        key_t[head] = key_turned[head : head + 1]

    def thirds(x):
        top, middle, rest = [part.astype(full) for part in split(jnp.where(lane < HEADS, x, 0.0))]
        return (top + pltpu.roll(middle, HEADS, axis=1) + pltpu.roll(rest, 2 * HEADS, axis=1)).astype(low)

    cum_parts[...] = thirds(cum)
    key_parts[...] = thirds(key)
    mixed = jnp.where(row >= column, dot_nt(act[:, INNER + STATE :], act[:, INNER : INNER + STATE]), 0.0)
    mix[...] = mixed
    mix_t[...] = mixed.T

    taken(EARLY)
    for i in (2, 3, 4):
        fetch(i)
    gain[...] = spread(1, 0, INNER, 16)
    launch(OUT, 2)
    for i in (2, 3):
        project(i, weight(i))
    give(GATE)
    project(4, weight(4))
    convolve(2, 10)
    taken(GATE)
    for i in (5, 6, 7, 8):
        fetch(i)
    convolve(10, SPLIT)
    project(5, weight(5))
    fetch(9)
    convolve(0, 2)
    for i in (6, 7, 8, 9):
        project(i, weight(i))
    give(OUT)
    q_ref[...] = jnp.zeros_like(q_ref)
    dcum_ref[...] = jnp.zeros_like(dcum_ref)
    dstep_ref[...] = jnp.zeros_like(dstep_ref)

    causal = lax.broadcasted_iota(jnp.int32, (128, 128), 0) >= lax.broadcasted_iota(jnp.int32, (128, 128), 1)


    def spread_heads(parts, j):
        line = lax.broadcasted_iota(jnp.int32, (128, 256), 0)
        head = 2 * j + (lax.broadcasted_iota(jnp.int32, (128, 256), 1) >> 7)
        return dot(parts[...], jnp.where(((line & 31) == head) & (line < 96), 1.0, 0.0).astype(low))

    @pl.loop(0, HEADS // 2)
    def _(j):
        cols = tile(j)
        cums = spread_heads(cum_parts, j)
        values = act[:, cols]
        for block in range(TOK // 128):
            start, last = block * 128, block * 128 + 128
            halves = []
            for e in (0, 1):
                pieces = []
                for past in range(block + 1):
                    span = slice(past * 128, past * 128 + 128)
                    gap = cums[start:last, e * 128 : e * 128 + 128] - key_t[2 * j + e, :, span]
                    if past == block:
                        gap = jnp.where(causal, gap, -1e30)
                    pieces.append((mix[start:last, span] * jnp.exp2(gap)).astype(low))
                halves.append(jnp.concatenate(pieces, axis=1))
            found = dot(jnp.concatenate(halves, axis=0), values[:last])
            y = jnp.where(left[:128], found[:128], found[128:]) + skip[:, cols] * values[start:last].astype(full)
            y_ref[start:last, cols] = y
            gate = proj[start:last, cols]
            gated = y * gate * jax.nn.sigmoid(gate)
            q_ref[start:last] += gated * gated

    q_ref[...] = jnp.broadcast_to(lax.rsqrt(row_sum(q_ref[...]) / INNER + eps), (TOK, 128))
    mix[...] = jnp.zeros_like(mix)

    @pl.loop(0, INNER // 128)
    def _(j):
        cols = tile(j)
        gate = proj[:, cols]
        gated = y_ref[:, cols] * gate * jax.nn.sigmoid(gate)
        value = (gated * q_ref[...] * gain[:, cols]).astype(low)
        dproj[:, cols] = value
        inner_t[pl.ds(4 * j, 4)] = value.T.reshape(4, 2, 16, TOK)

    for j in range(D // 128):
        cols = slice(j * 128, j * 128 + 128)
        normed[:, cols] = (live(128) * cotangent[:, cols].astype(full)).astype(low)

    def grads(batch, group, side, half):
        start = PARTS[batch][group[0]][0]
        width = sum(PARTS[batch][part][1] for part in group)
        if batch == OUT:
            lhs = inner_t[pl.ds(32 * half, 32), side].reshape(TOK, TOK)
            rhs = normed[:, start : start + width]
        else:
            lhs = normed_t[pl.ds(32 * half, 32)].reshape(TOK, TOK)
            rhs = dproj[:, pl.ds(pl.multiple_of(BASE[batch] + start + side * WIDTH[batch], 128), width)]
        value = dot(lhs, rhs)
        return [(part, PARTS[batch][part][0] - start, PARTS[batch][part][1], value) for part in group]

    def spot_of(part, half, m):
        spot = {"y": 2 * half + (m // 4) % 2, "z": m // 8, "x": m % 4}
        axes = ORDERS[part]
        return spot[axes[2]] * 16 + spot[axes[1]] * 4 + spot[axes[0]]

    users = [[], []]

    def rs_free():
        for gone in users:
            while gone:
                rs_pass_copy(*gone.pop()).wait_send()

    def rs_give(batch):
        for group, slot in GROUPS[batch]:
            while users[slot]:
                rs_pass_copy(*users[slot].pop()).wait_send()
            origin = PARTS[batch][group[0]][0]
            for half in (0, 1):
                for part, offset, width, value in grads(batch, group, 1 - core, half):
                    value = value[:, offset : offset + width].astype(low)
                    for m in range(32):
                        work[CHIPS * slot + spot_of(part, half, m), :, offset : offset + width] = value[
                            16 * m : 16 * m + 16
                        ]
            for part in group:
                offset = PARTS[batch][part][0] - origin
                users[slot].append((batch, part, slot, offset))
                rs_pass_copy(batch, part, slot, offset).start()

    def rs_pass_copy(batch, part, slot=0, offset=0):
        width = PARTS[batch][part][1]
        sem = batch * 3 + part
        return remote(
            work.at[pl.ds(CHIPS * slot, CHIPS), :, pl.ds(offset, width)],
            part0.at[:, :, lanes_of(batch, part)],
            rs_pass.at[sem],
            rs_got.at[batch],
            sibling,
        )

    def lanes_of(batch, part):
        start, width = PARTS[batch][part]
        return pl.ds(LOCAL[batch] + start, width)

    def rs_copies(batch, part, stage):
        lanes = lanes_of(batch, part)
        axis = ORDERS[part][3 - stage]
        copies = []
        for step in (1, 2, 3):
            peer = moved(at, axis, step)
            there, slot = peer[axis], pl.ds(step - 1, 1)
            if stage == 1:
                source, target = part0.at[pl.ds(there * 16, 16), :, lanes], recv1.at[pl.ds(16 * step - 16, 16), :, lanes]
            elif stage == 2:
                source, target = part1.at[pl.ds(there * 4, 4), :, lanes], recv2.at[pl.ds(4 * step - 4, 4), :, lanes]
            else:
                source, target = part2.at[pl.ds(there, 1), :, lanes], recv3.at[slot, :, lanes]
            sem = batch * 3 + stage - 1
            copies.append(remote(source, target, rs_send.at[sem], rs_recv.at[sem], peer))
        return copies

    def rs_hop(batch, part, stage):
        for copy in rs_copies(batch, part, stage):
            copy.start()

    def rs_wait(batch, stage, sems):
        lanes = pl.ds(LOCAL[batch], WIDTH[batch])
        every = (recv1, recv2, recv3)[stage - 1].at[:, :, lanes]
        pltpu.make_async_copy(every, every, sems.at[batch * 3 + stage - 1]).wait()

    def rs_own(batch):
        lanes = pl.ds(LOCAL[batch], WIDTH[batch])
        every = part0.at[:, :, lanes]
        pltpu.make_async_copy(every, every, rs_got.at[batch]).wait()
        for group, _ in GROUPS[batch]:
            for half in (0, 1):
                for part, offset, width, value in grads(batch, group, core, half):
                    lanes = lanes_of(batch, part)
                    for m in range(32):
                        now = pl.ds(spot_of(part, half, m), 1)
                        piece = value[16 * m : 16 * m + 16, offset : offset + width][None]
                        part0[now, :, lanes] = (piece + part0[now, :, lanes].astype(full)).astype(low)
            for part in group:
                rs_hop(batch, part, 1)

    def part_one(batch, part):
        lanes = lanes_of(batch, part)
        mine = at[ORDERS[part][2]] * 16
        for i in range(16):
            now = pl.ds(i, 1)
            value = part0[pl.ds(mine + i, 1), :, lanes].astype(full)
            for k in range(3):
                value = value + recv1[pl.ds(16 * k + i, 1), :, lanes].astype(full)
            part1[now, :, lanes] = value.astype(low)
        rs_hop(batch, part, 2)

    def part_two(batch, part):
        lanes = lanes_of(batch, part)
        mine = at[ORDERS[part][1]] * 4
        for i in range(4):
            now = pl.ds(i, 1)
            value = part1[pl.ds(mine + i, 1), :, lanes].astype(full)
            for k in range(3):
                value = value + recv2[pl.ds(4 * k + i, 1), :, lanes].astype(full)
            part2[now, :, lanes] = value.astype(low)
        rs_hop(batch, part, 3)

    def part_three(batch, part):
        lanes = lanes_of(batch, part)
        value = part2[pl.ds(at[ORDERS[part][0]], 1), :, lanes].astype(full)
        for k in range(3):
            value = value + recv3[pl.ds(k, 1), :, lanes].astype(full)
        value = value[0]
        start, width = PARTS[batch][part]
        if batch == OUT:
            go_out[:, start : start + width] = value
            return
        base = BASE[batch]
        at_column = pl.multiple_of(base + core * WIDTH[batch] + start, 128)
        gi_out[:, pl.ds(at_column, width)] = jnp.where(first, value[:8], value[8:])
        swap_from[:, pl.ds(base // 2 + start, width)] = jnp.where(first, value[8:], value[:8])

    rs_give(OUT)
    taken(OUT)
    while drained:
        wait_bytes(*drained.pop())
    wout = full_out.reshape(INNER, D)

    m_ref[...] = jnp.zeros_like(m_ref)

    @pl.loop(0, D // 256)
    def _(j):
        cols = tile(j, 0, 256)
        branch = dot(dproj[:, :INNER], wout[:, cols])
        block_out[:, cols] = (tokens[:, cols].astype(full) + live(256) * branch).astype(low)
        shares = normed[:, cols].astype(full) * branch
        m_ref[...] += shares[:, :128] + shares[:, 128:]

    outputs = [pltpu.make_async_copy(block_out, block_out_hbm, edge_sem.at[5])]
    outputs[0].start()

    m_ref[...] = jnp.broadcast_to(row_sum(m_ref[...]) / INNER, (TOK, 128))

    @pl.loop(0, INNER // 256)
    def _(j):
        wide = tile(j, 0, 256)
        sums = [jnp.zeros((1, 128), full)] * 2
        for rows in (slice(0, 256), slice(256, 512)):
            value = dot_nt(normed[rows, :], wout[wide, :])
            for half in (0, 1):
                cols = tile(2 * j + half)
                inside = value[:, half * 128 : half * 128 + 128]
                y, gate, q = y_ref[rows, cols], proj[rows, cols], q_ref[rows, :]
                sig = jax.nn.sigmoid(gate)
                silu = gate * sig
                u = y * silu * q
                sums[half] = sums[half] + col_sum(inside * u)
                dgated = q * (inside * gain[:, cols] - u * m_ref[rows, :])
                dproj[rows, cols] = (dgated * y * (sig + silu * (1.0 - sig))).astype(low)
                dinner[rows, cols] = dgated * silu
        for half in (0, 1):
            small_now[5:6, tile(2 * j + half)] = sums[half]

    rs_own(OUT)

    rs_give(GATE)

    dnormed = proj.at[:, pl.ds(0, D)]

    def back_load(i):
        fetched(2 + i % 2, *BACK_TILES[i]).start()

    def back_tile(i):
        start, width = BACK_TILES[i]
        fetched(2 + i % 2, start, width).wait()
        value = dot_nt(dproj[:, start : start + width], inner_t[:, i % 2, :, :width].reshape(D, width))
        dnormed[...] = value if i == 0 else dnormed[...] + value
        if i + 2 < len(BACK_TILES):
            back_load(i + 2)

    back_load(0)
    back_load(1)

    def conv_back(dact, j):
        cols = tile(j)
        x = proj[:, tile(j, INNER)]
        dpre = dact * dsilu[:, cols].astype(full)
        small_now[4:5, cols] = col_sum(dpre)
        small_now[3:4, cols] = col_sum(dpre * x)
        dx = taps[3:4, cols] * dpre
        for step in (1, 2, 3):
            moved_up = rolled_up(dpre, step)
            small_now[3 - step : 4 - step, cols] = col_sum(moved_up * x)
            dx = dx + taps[3 - step : 4 - step, cols] * moved_up
        dproj[:, tile(j, INNER)] = dx.astype(low)

    def rs_one(batch):
        rs_wait(batch, 1, rs_recv)
        for part in range(3):
            part_one(batch, part)

    def rs_two(batch):
        rs_wait(batch, 2, rs_recv)
        for part in range(3):
            part_two(batch, part)

    def rs_three(batch):
        rs_wait(batch, 3, rs_recv)
        for part in range(3):
            part_three(batch, part)

    back_ref[...] = jnp.zeros_like(back_ref)

    def settle(j):
        cols = tile(j)
        lane = lax.broadcasted_iota(jnp.int32, (TOK, 128), 1)
        left = lane < HEAD
        values, dy, back = act[:, cols].astype(full), dinner[:, cols], back_ref[...]
        direct = values * back
        crossing = dy.astype(low).astype(full) * (y_ref[:, cols] - skip[:, cols] * values) - direct
        small_now[7:8, cols] = col_sum(dy * values)
        for e in (0, 1):
            mine = left if e == 0 else jnp.logical_not(left)
            spot = lane == 2 * j + e
            dcum_ref[...] = jnp.where(spot, row_sum(jnp.where(mine, crossing, 0.0)), dcum_ref[...])
            dstep_ref[...] = jnp.where(spot, row_sum(jnp.where(mine, direct, 0.0)), dstep_ref[...])
        conv_back(back + skip[:, cols] * dy, j)

    @pl.loop(0, HEADS // 4 + 1)
    def _(run):
        for turn, events in PLAN:

            @pl.when(run == turn)
            def _(events=events):
                for action, what in events:
                    if action == "dn":
                        back_tile(what)
                    else:
                        {"give": rs_give, "own": rs_own, "one": rs_one, "two": rs_two}[action](what)

        @pl.loop(jnp.maximum(2 * run - 1, 0), jnp.minimum(2 * run + 1, HEADS // 2))
        def _(j):
            settle(jnp.maximum(j - 1, 0))
            cols = tile(j)
            keys = spread_heads(key_parts, j)
            left = lax.broadcasted_iota(jnp.int32, (TOK, 128), 1) < HEAD
            anti = lax.broadcasted_iota(jnp.int32, (128, 128), 0) <= lax.broadcasted_iota(
                jnp.int32, (128, 128), 1
            )
            v_low = act[:, cols]
            dy_low = dinner[:, cols].astype(low)
            own = (jnp.where(left, v_low, jnp.zeros_like(v_low)), jnp.where(left, jnp.zeros_like(v_low), v_low))
            found = []
            for block in range(TOK // 128):
                start, last = block * 128, block * 128 + 128
                both = dot_nt(jnp.concatenate([own[0][start:last], own[1][start:last]], axis=0), dy_low[start:])
                halves = []
                total = None
                for e in (0, 1):
                    pieces, shares = [], []
                    for later in range(block, TOK // 128):
                        span = slice(later * 128, later * 128 + 128)
                        gap = cum_t[2 * j + e, :, span] - keys[start:last, e * 128 : e * 128 + 128]
                        if later == block:
                            gap = jnp.where(anti, gap, -1e30)
                        decay = jnp.exp2(gap)
                        pieces.append((mix_t[start:last, span] * decay).astype(low))
                        inside = slice((later - block) * 128, (later - block + 1) * 128)
                        shares.append(both[e * 128 : e * 128 + 128, inside] * decay)
                    halves.append(jnp.concatenate(pieces, axis=1))
                    share = jnp.concatenate(shares, axis=1)
                    total = share if total is None else total + share
                mix[start:last, start:] += total
                given_back = dot(jnp.concatenate(halves, axis=0), dy_low[start:])
                found.append(jnp.where(left[:128], given_back[:128], given_back[128:]))
            for block, value in enumerate(found):
                back_ref[block * 128 : block * 128 + 128] = value

    settle(HEADS // 2 - 1)
    rs_own(MID)
    rs_one(EARLY)
    masked = jnp.where(row <= column, mix[...], 0.0)
    conv_back(dot(masked.astype(low), act[:, INNER + STATE :]), INNER // 128)
    conv_back(dot(masked.T.astype(low), act[:, INNER : INNER + STATE]), INNER // 128 + 1)
    dacc = summed(row <= column, dcum_ref[...])
    sig = jax.nn.sigmoid(proj[:, INNER + XBC : INNER + XBC + 128] + heads[0:1, :])
    steps = step_ref[...]
    ratio = jnp.where(steps > 1e-30, sig / jnp.maximum(steps, 1e-30), 1.0)
    draw = jnp.where(lane < HEADS, dstep_ref[...] * ratio + dacc * rate * sig, 0.0)
    dproj[:, INNER + XBC : INNER + XBC + 128] = draw.astype(low)
    dproj[:, INNER + XBC + 128 :] = jnp.zeros((TOK, 128), low)
    small_now[6:7, :] = jnp.zeros((1, XBC), full)
    small_now[6:7, :128] = col_sum(draw)
    small_now[6:7, 128:256] = rate * col_sum(dacc * steps)
    small_now[5:6, INNER:] = jnp.zeros((1, XBC - INNER), full)
    small_now[7:8, INNER:] = jnp.zeros((1, XBC - INNER), full)


    def small_swap():
        away = pl.ds(pl.multiple_of((1 - core) * HALF, 128), HALF)
        return remote(small_now.at[:, away], small_other, small_send.at[0], small_recv.at[0], sibling)

    def small_copies(stage):
        made = []
        for part in range(3):
            lanes = pl.ds(part * THIRD, THIRD)
            axis = ORDERS[part][stage - 1]
            for step in (1, 2, 3):
                slot = (stage - 1) * 3 + step - 1
                made.append(
                    remote(
                        small_half.at[stage - 1, :, lanes],
                        small_got.at[slot, :, lanes],
                        small_send.at[stage],
                        small_recv.at[stage],
                        moved(at, axis, step),
                    )
                )
        return made

    def small_back():
        return remote(small_half.at[3], small_last, small_send.at[4], small_recv.at[4], sibling)

    def small_wait(stage, sems):
        if stage in (0, 4):
            sems_of = small_other if stage == 0 else small_last
            pltpu.make_async_copy(sems_of, sems_of, sems.at[stage]).wait()
        else:
            every = small_got.at[pl.ds((stage - 1) * 3, 3)]
            pltpu.make_async_copy(every, every, sems.at[stage]).wait()

    def small_add(stage):
        small_wait(stage, small_recv)
        if stage == 0:
            mine = pl.ds(pl.multiple_of(core * HALF, 128), HALF)
            small_half[0] = small_now[:, mine] + small_other[...]
        else:
            value = small_half[stage - 1]
            for k in range(3):
                value = value + small_got[(stage - 1) * 3 + k]
            small_half[stage] = value
        for copy in small_copies(stage + 1) if stage < 3 else [small_back()]:
            copy.start()

    def norm_start(stage):
        for step in (1,) if stage == 0 else (1, 2, 3):
            slot = 0 if stage == 0 else stage * 3 - 3 + step
            peer = moved(at, "cxyz"[stage], step)
            remote(norm_now.at[stage], norm_got.at[slot], norm_send.at[stage], norm_recv.at[stage], peer).start()

    def norm_wait(stage, sems):
        every = norm_got.at[pl.ds(0, 1)] if stage == 0 else norm_got.at[pl.ds(stage * 3 - 2, 3)]
        pltpu.make_async_copy(every, every, sems.at[stage]).wait()

    def norm_add(stage):
        norm_wait(stage, norm_recv)
        value = norm_now[stage]
        for k in range(1 if stage == 0 else 3):
            value = value + norm_got[0 if stage == 0 else stage * 3 - 2 + k]
        if stage == 3:
            norm_out[...] = value
        else:
            norm_now[stage + 1] = value
            norm_start(stage + 1)

    small_swap().start()
    rs_give(LATE)
    back_tile(7)
    small_add(0)
    back_tile(8)
    back_tile(9)
    rs_own(LATE)
    rs_two(GATE)
    m_ref[...] = jnp.zeros_like(m_ref)
    for j in range(D // 128):
        cols = slice(j * 128, j * 128 + 128)
        u = tokens[:, cols].astype(full) * token_scale
        du = dnormed[:, cols] * u
        norm_now[0, j : j + 1, :] = col_sum(du)
        m_ref[...] += du * norm_gain[:, cols]
    mean = row_sum(m_ref[...]) / D
    norm_start(0)
    small_add(1)
    rs_two(EARLY)
    rs_one(MID)
    for j in range(D // 128):
        cols = slice(j * 128, j * 128 + 128)
        u = tokens[:, cols].astype(full) * token_scale
        du = dnormed[:, cols] * norm_gain[:, cols]
        normed[:, cols] = (cotangent[:, cols].astype(full) + token_scale * (du - u * mean)).astype(low)
    final = pltpu.make_async_copy(normed, input_grad, local_sem.at[0])
    final.start()
    norm_add(0)
    rs_three(OUT)
    rs_one(LATE)
    small_add(2)
    norm_add(1)
    rs_three(GATE)
    rs_two(MID)
    for batch in (OUT, GATE):
        for stage in (1, 2, 3):
            rs_wait(batch, stage, rs_send)
    rs_two(LATE)
    small_add(3)
    norm_add(2)
    rs_three(EARLY)
    rs_three(MID)
    small_wait(4, small_recv)
    mine = pl.ds(pl.multiple_of(core * HALF, 128), HALF)
    small_out[:, mine] = small_half[3]
    small_out[:, pl.ds(pl.multiple_of((1 - core) * HALF, 128), HALF)] = small_last[...]
    outputs.append(pltpu.make_async_copy(small_out, small_hbm, edge_sem.at[6]))
    outputs.append(pltpu.make_async_copy(go_out, go_hbm, edge_sem.at[7]))
    for copy in outputs[1:]:
        copy.start()
    rs_free()
    for stage in range(5):
        small_wait(stage, small_send)
    for batch in (EARLY, MID):
        for stage in (1, 2, 3):
            rs_wait(batch, stage, rs_send)
    rs_three(LATE)
    last = remote(swap_from, swap_to, swap_sem.at[2], swap_sem.at[3], sibling)
    last.start()
    norm_add(3)
    outputs.append(pltpu.make_async_copy(norm_out, norm_hbm, edge_sem.at[8]))
    outputs[3].start()
    for stage in range(4):
        norm_wait(stage, norm_send)
    for stage in (1, 2, 3):
        rs_wait(LATE, stage, rs_send)
    final.wait()
    last.wait()
    for batch in (GATE, EARLY, MID, LATE):
        base, width = BASE[batch], WIDTH[batch]
        lanes = pl.ds(pl.multiple_of(base + (1 - core) * width, 128), width)
        gi_out[:, lanes] = swap_to[:, base // 2 : base // 2 + width]
    outputs.append(pltpu.make_async_copy(gi_out, gi_hbm, edge_sem.at[9]))
    outputs[4].start()
    for copy in outputs:
        copy.wait()


def block(lengths, ids, in_shard, wo, tokens, cotangent, params):
    full, low = jnp.float32, jnp.bfloat16
    anywhere = pl.BlockSpec(memory_space=pl.ANY)
    sems = pltpu.SemaphoreType.DMA
    return pl.pallas_call(
        block_kernel,
        out_shape=(
            jax.ShapeDtypeStruct((TOK, D), low),
            jax.ShapeDtypeStruct((TOK, D), low),
            jax.ShapeDtypeStruct((8, COLS), full),
            jax.ShapeDtypeStruct((16, D), full),
            jax.ShapeDtypeStruct((8, XBC), full),
            jax.ShapeDtypeStruct((8, 128), full),
            jax.ShapeDtypeStruct((2, 4, 2, 4, 16, COLS), low),
        ),
        in_specs=[pl.BlockSpec(memory_space=pltpu.SMEM)] * 2 + [anywhere] * 5,
        out_specs=[anywhere] * 7,
        scratch_shapes=[
            pltpu.VMEM((8, PROJ), low),
            pltpu.VMEM((16, D), low),
            pltpu.VMEM((TOK, D), low),
            pltpu.VMEM((TOK, D), low),
            pltpu.VMEM((16, 128), full),
            pltpu.VMEM((TOK, D), low),
            pltpu.VMEM((8, COLS), full),
            pltpu.VMEM((16, D), full),
            pltpu.VMEM((8, XBC), full),
            pltpu.VMEM((8, 128), full),
            pltpu.VMEM((8, COLS), full),
            pltpu.VMEM((8, COLS), full),
            pltpu.VMEM((16, XBC), low),
            pltpu.VMEM((1, INNER), full),
            pltpu.VMEM((2, 4, 2, 4, 2, 16, D), low),
            pltpu.VMEM((2 * CHIPS, 16, 512), low),
            pltpu.VMEM((TOK, COLS - 128), full),
            pltpu.VMEM((TOK, XBC), low),
            pltpu.VMEM((TOK, XBC), low),
            pltpu.VMEM((TOK, INNER), full),
            pltpu.VMEM((TOK, INNER), full),
            pltpu.VMEM((TOK, COLS), low),
            pltpu.VMEM((CHIPS, 2, 16, TOK), low),
            pltpu.VMEM((TOK, D), low),
            pltpu.VMEM((CHIPS, 16, TOK), low),
            pltpu.VMEM((TOK, TOK), full),
            pltpu.VMEM((TOK, TOK), full),
            pltpu.VMEM((TOK, 128), low),
            pltpu.VMEM((TOK, 128), low),
            pltpu.VMEM((HEADS, 1, TOK), full),
            pltpu.VMEM((HEADS, 1, TOK), full),
            pltpu.VMEM((TOK, 128), full),
            pltpu.VMEM((TOK, 128), full),
            pltpu.VMEM((TOK, 128), full),
            pltpu.VMEM((TOK, 128), full),
            pltpu.VMEM((TOK, 128), full),
            pltpu.VMEM((TOK, 128), full),
            pltpu.VMEM((8, XBC), full),
            pltpu.VMEM((1, INNER), full),
            pltpu.VMEM((1, D), full),
            pltpu.VMEM((CHIPS, 16, SIDE), low),
            pltpu.VMEM((48, 16, SIDE), low),
            pltpu.VMEM((16, 16, SIDE), low),
            pltpu.VMEM((12, 16, SIDE), low),
            pltpu.VMEM((4, 16, SIDE), low),
            pltpu.VMEM((3, 16, SIDE), low),
            pltpu.VMEM((8, XBC), full),
            pltpu.VMEM((8, XBC), full),
            pltpu.VMEM((8, XBC), full),
            pltpu.VMEM((8, HALF), full),
            pltpu.VMEM((4, 8, HALF), full),
            pltpu.VMEM((9, 8, HALF), full),
            pltpu.VMEM((8, HALF), full),
            pltpu.VMEM((4, 8, 128), full),
            pltpu.VMEM((10, 8, 128), full),
            sems((4,)),
            sems((7,)),
            sems((10,)),
            sems((15,)),
            sems((15,)),
            sems((5,)),
            sems((5,)),
            sems((15,)),
            sems((15,)),
            sems((15,)),
            sems((5,)),
            sems((5,)),
            sems((5,)),
            sems((4,)),
            sems((4,)),
        ],
        compiler_params=pltpu.CompilerParams(collective_id=0, has_side_effects=True, vmem_limit_bytes=63 << 20),
    )(lengths, ids, in_shard, wo, tokens, cotangent, params)


def finish_kernel(
    out_in,
    grad_in,
    gi_in,
    go_in,
    small_in,
    norm_in,
    out_hbm,
    grad_hbm,
    gain_hbm,
    gi_hbm,
    conv_hbm,
    bias_hbm,
    dt_hbm,
    log_hbm,
    skip_hbm,
    inner_hbm,
    go_hbm,
    small,
    norm,
    gi,
    go,
    out,
    grad,
    gain_out,
    gi_out,
    conv_out,
    bias_out,
    dt_out,
    log_out,
    skip_out,
    inner_out,
    sem,
):
    pairs = [(small_in, small), (norm_in, norm), (gi_in, gi), (go_in, go)]
    halves = [pl.ds(0, TOK // 2), pl.ds(TOK // 2, TOK // 2)]
    for source, target in ((out_in, out), (grad_in, grad)):
        pairs += [(source.at[half, :], target.at[half, :]) for half in halves]
    copies = [pltpu.make_async_copy(source, target, sem.at[i]) for i, (source, target) in enumerate(pairs)]
    for copy in copies[:1] + copies[4:] + copies[1:4]:
        copy.start()
    writes = []

    def write(source, target):
        writes.append(pltpu.make_async_copy(source, target, sem.at[len(copies) + len(writes)]))
        writes[-1].start()

    me = lax.axis_index("dp") * 16 + lax.axis_index("fsdp")
    copies[0].wait()

    def from_lane(count):
        return pltpu.roll(small[...], lax.rem(XBC - count * me, XBC), axis=1)

    conv = from_lane(18)
    conv_out[...] = conv[:CONV, :18]
    write(conv_out, conv_hbm)
    bias_out[...] = conv[CONV : CONV + 1, :18]
    write(bias_out, bias_hbm)
    inner_out[...] = from_lane(16)[5:6, :16]
    write(inner_out, inner_hbm)
    dt_out[...] = small[6:7, :HEADS]
    write(dt_out, dt_hbm)
    log_out[...] = small[6:7, 128 : 128 + HEADS]
    write(log_out, log_hbm)
    owner = lax.broadcasted_iota(jnp.int32, (INNER, 128), 0) >> 6
    sums = (owner == lax.broadcasted_iota(jnp.int32, (INNER, 128), 1)).astype(jnp.float32)
    skip_out[...] = dot(small[:, :INNER], sums, precision=highest)[7:8, :HEADS]
    write(skip_out, skip_hbm)
    copies[1].wait()
    line = lax.broadcasted_iota(jnp.int32, (8, 128), 0)
    row = jnp.sum(jnp.where(line == me // 16, norm[...], 0.0), axis=0, keepdims=True)
    gain_out[...] = pltpu.roll(row, lax.rem(128 - 8 * lax.rem(me, 16), 128), axis=1)[:, :8]
    write(gain_out, gain_hbm)
    for i, (source, target) in enumerate(((out, out_hbm), (grad, grad_hbm))):
        for k, half in enumerate(halves):
            copies[4 + 2 * i + k].wait()
            write(source.at[half, :], target.at[half, :])
    copies[2].wait()
    gi_out[...] = gi[:, :PROJ]
    write(gi_out, gi_hbm)
    copies[3].wait()
    write(go, go_hbm)
    for copy in writes:
        copy.wait()


def finish(out, grad, gi, go, small, norm):
    full = jnp.float32
    anywhere = pl.BlockSpec(memory_space=pl.ANY)
    rest = [(CONV, 18), (1, 18), (1, HEADS), (1, HEADS), (1, HEADS), (1, 16)]
    shapes = [(1, 8), (8, PROJ)] + rest
    return pl.pallas_call(
        finish_kernel,
        out_shape=[jax.ShapeDtypeStruct(out.shape, out.dtype)] * 2
        + [jax.ShapeDtypeStruct(shape, full) for shape in shapes + [(16, D)]],
        in_specs=[anywhere] * 6,
        out_specs=[anywhere] * 11,
        scratch_shapes=[
            pltpu.VMEM(small.shape, full),
            pltpu.VMEM(norm.shape, full),
            pltpu.VMEM(gi.shape, full),
            pltpu.VMEM(go.shape, full),
            pltpu.VMEM(out.shape, out.dtype),
            pltpu.VMEM(out.shape, out.dtype),
        ]
        + [pltpu.VMEM(shape, full) for shape in shapes]
        + [pltpu.SemaphoreType.DMA((21,))],
        compiler_params=pltpu.CompilerParams(vmem_limit_bytes=62 << 20),
    )(out, grad, gi, go, small, norm)


def body(
    tokens,
    lengths,
    placement_ids,
    norm_gain,
    in_weight,
    conv_weight,
    conv_bias,
    dt_bias,
    a_log,
    d_skip,
    inner_gain,
    out_weight,
    cotangent,
):
    full = jnp.float32

    def line(values, first):
        values = values.astype(full).reshape(-1, values.shape[-1])
        rows, lanes = values.shape
        return jnp.pad(values, ((first, 16 - first - rows), (0, 128 - lanes)))

    params = (
        line(norm_gain, 0)
        + line(inner_gain, 1)
        + line(conv_bias, 2)
        + line(conv_weight, 3)
        + line(dt_bias, 8)
        + line(a_log, 9)
        + line(d_skip, 10)
    )
    block_out, input_grad, shard_in, shard_out, small, norm, _ = block(
        lengths, placement_ids, in_weight, out_weight, tokens, cotangent, params
    )
    found = finish(block_out, input_grad, shard_in, shard_out, small, norm)
    flat = [0, 0, 1, 0, 0, 1, 1, 1, 1, 1, 0]
    return tuple(value[0] if one else value for value, one in zip(found, flat))


def solution(mesh):
    placed = (
        P(("dp", "fsdp"), None),
        P(),
        P(("dp", "fsdp")),
        P(("dp", "fsdp")),
        P(("dp", "fsdp"), None),
        P(None, ("dp", "fsdp")),
        P(("dp", "fsdp")),
        P(),
        P(),
        P(),
        P(("dp", "fsdp")),
        P(("dp", "fsdp"), None),
        P(("dp", "fsdp"), None),
    )
    return jax.shard_map(
        body,
        mesh=mesh,
        in_specs=placed,
        out_specs=(
            P(("dp", "fsdp"), None),
            P(("dp", "fsdp"), None),
            P(("dp", "fsdp")),
            P(("dp", "fsdp"), None),
            P(None, ("dp", "fsdp")),
            P(("dp", "fsdp")),
            P(),
            P(),
            P(),
            P(("dp", "fsdp")),
            P(("dp", "fsdp"), None),
        ),
        check_vma=False,
    )
```
